128 devices in a mesh: grp: 4 (over z), aux: 32 (over y, x, core).
Axes of the slice: x: 4, y: 4, z: 4, core: 2. Of those that a mesh axis runs over, the one named last changes fastest.
Arguments:
- three_index: bfloat16 [64, 768, 16384], P(None, None, ('grp', 'aux')), may hold values from -0.25 to 0.25
- block_owner: int32 [64], replicated, may hold values from 0 to 31, as said below
- pair_screen: int32 [64, 64], replicated, may hold values from 0 to 1, as said below
- orbital_counts: int32 [64], replicated, may hold values from 1 to 16, as said below
- occupied_energy: float32 [64, 16], replicated, may hold values from -1.5 to -0.3
- virtual_energy: float32 [64, 48], replicated, may hold values from 0.3 to 2.5
Outputs:
- virtual_density: float32 [64, 48, 48], P('aux', 'grp')
The draws below stay inside these ranges and needn't reach their ends.
Inputs may be any that keep to these rules, and one draw needn't show every extreme that they name: `block_owner`: every owner index holds 1 to 3 blocks, and some hold exactly 3. `pair_screen`: symmetric, with ones on the diagonal. `orbital_counts`: some block uses all 16 slots.
All inputs are finite; a program needn't handle non-finite values.
Results may differ from the reference program's by a relative error of at most 0.0019.
Values may be sent and summed in bfloat16 or wider, within the bound.
A program may use at most 128 MiB of HBM per device.

```python
import jax
import jax.numpy as jnp
import numpy as np
from jax import lax

OB = 16
NV = 48
NAUX = 16384
BLK_DEV = 2
CAP = 3
NBLK = 64
N_AUX = 32


def draw_block_owner(key, part):
    key = jax.random.fold_in(key, 11)
    first_key, second_key = jax.random.split(key)
    pattern = jnp.array([CAP, 1, 1, 4 * BLK_DEV - CAP - 2], dtype=jnp.int32)
    block_loads = jnp.tile(pattern, N_AUX // 4)[jax.random.permutation(first_key, N_AUX)]
    owner_slots = jnp.repeat(jnp.arange(N_AUX, dtype=jnp.int32), block_loads, total_repeat_length=NBLK)
    return owner_slots[jax.random.permutation(second_key, NBLK)].astype(jnp.int32)


def draw_pair_screen(key, part):
    key = jax.random.fold_in(key, 12)
    random_bits = jax.random.randint(key, (NBLK, NBLK), 0, 4)
    kept_pairs = (random_bits != 0).astype(jnp.int32)
    upper_half = jnp.triu(kept_pairs, 1)
    return (upper_half + upper_half.T + jnp.eye(NBLK, dtype=jnp.int32)).astype(jnp.int32)


def draw_orbital_counts(key, part):
    key = jax.random.fold_in(key, 13)
    first_key, second_key = jax.random.split(key)
    orbital_counts = jax.random.randint(first_key, (NBLK,), 1, OB + 1)
    full_block = jax.random.randint(second_key, (), 0, NBLK)
    return orbital_counts.at[full_block].set(OB).astype(jnp.int32)


def steps_of(key, shape, pieces, smallest, largest):
    level = 1.0
    for position, blocks in pieces:
        draws = jax.random.uniform(jax.random.fold_in(jax.random.fold_in(key, 6), position), (blocks,), jnp.float32, smallest / len(pieces), largest / len(pieces))
        level = level * jnp.repeat(jnp.exp(draws), shape[position] // blocks).reshape((-1,) + (1,) * (len(shape) - 1 - position))
    return level


def noise(stream_key, shape, spread, most, shards=(), held_as=jnp.bfloat16):
    values = spread * jax.random.normal(stream_key, shape, jnp.float32)
    if shards:
        values = values * steps_of(stream_key, shape, shards, -0.22, 0.18)
    return jnp.clip(values, -most, most).astype(held_as)


def setup_inputs(seed: int = 0) -> dict:
    keys = jax.random.split(jax.random.key(seed), 7)
    return {
        "three_index": noise(keys[0], (NBLK, OB * NV, NAUX), 0.04, 0.25, ((2, 128),)),
        "block_owner": draw_block_owner(jax.random.fold_in(keys[6], 71), 0),
        "pair_screen": draw_pair_screen(jax.random.fold_in(keys[6], 71), 0),
        "orbital_counts": draw_orbital_counts(jax.random.fold_in(keys[6], 71), 0),
        "occupied_energy": jnp.clip(jax.random.uniform(keys[4], (NBLK, OB), jnp.float32, -1.5, -0.3), -1.5, -0.3),
        "virtual_energy": jnp.clip(jax.random.uniform(keys[5], (NBLK, NV), jnp.float32, 0.3, 2.5), 0.3, 2.5),
    }


def reference(three_index, block_owner, pair_screen, orbital_counts, occupied_energy, virtual_energy):
    block_count = three_index.shape[0]
    row_count = three_index.shape[1]
    occupied_width = occupied_energy.shape[1]
    virtual_width = virtual_energy.shape[1]
    energy = (virtual_energy[:, None, :] - occupied_energy[:, :, None]).reshape(block_count, row_count)
    occupied_flags = (jnp.arange(occupied_width, dtype=jnp.int32)[None, :] < orbital_counts[:, None]).astype(jnp.float32)
    occupancy = jnp.repeat(occupied_flags, virtual_width, axis=1)
    first_index, second_index = np.triu_indices(block_count)
    pair_list = jnp.stack([jnp.asarray(first_index, dtype=jnp.int32), jnp.asarray(second_index, dtype=jnp.int32)], axis=1)

    def add_pair(density, pair):
        row_block = pair[0]
        col_block = pair[1]
        is_live = jnp.logical_and(block_owner[row_block] == block_owner[col_block], pair_screen[row_block, col_block] == 1)

        def compute(current):
            integral = lax.dot_general(three_index[row_block], three_index[col_block], (((1,), (1,)), ((), ())), preferred_element_type=jnp.float32)
            divisor = energy[row_block][:, None] + energy[col_block][None, :]
            rounded = (occupancy[row_block][:, None] * occupancy[col_block][None, :] * integral / divisor).astype(jnp.bfloat16)
            amplitude = lax.optimization_barrier(rounded).astype(jnp.float32)
            row_form = amplitude.reshape(occupied_width, virtual_width, row_count)
            own_part = jnp.einsum("iax,ibx->ab", row_form, row_form)
            col_form = amplitude.reshape(row_count, occupied_width, virtual_width)
            other_part = jnp.einsum("xjc,xjd->cd", col_form, col_form)
            other_part = jnp.where(row_block != col_block, other_part, jnp.zeros_like(other_part))
            current = current.at[row_block].add(own_part)
            return current.at[col_block].add(other_part)

        return lax.cond(is_live, compute, lambda current: current, density), None

    start = jnp.zeros((block_count, virtual_width, virtual_width), jnp.float32)
    density, ignored = lax.scan(add_pair, start, pair_list)
    return density
```

```python
import functools

import jax
import jax.numpy as jnp
import numpy as np
from jax import lax
from jax.experimental import pallas as pl
from jax.experimental.pallas import tpu as pltpu
from jax.sharding import PartitionSpec as P

NV = 48
OB = 16
BINS = 16
GROUP = 8
ROWS = GROUP * NV
SIDE = 4
PART_A = 6
ALL = (0, BINS)
ROOMY = (((ALL,) * 6), ((ALL,) * 4))
TIGHT = ((ALL, ALL, ALL, (0, 15), (0, 9), (0, 4)), (ALL, (2, BINS)))
MESH = pl.DeviceIdType.MESH
VMEM = pl.BlockSpec(memory_space=pltpu.VMEM)
SMEM = pl.BlockSpec(memory_space=pltpu.SMEM)
ANY = pl.BlockSpec(memory_space=pl.ANY)


def has(limits, index):
    first, end = limits
    return (index >= first) & (index < end)


def plan(block_owner, orbital_counts):
    ids = jnp.arange(block_owner.shape[0], dtype=jnp.int32)
    same = block_owner[:, None] == block_owner[None, :]
    earlier = same & (ids[None, :] < ids[:, None])
    load = jnp.sum(jnp.where(same, orbital_counts[None, :], 0), axis=1)
    base = jnp.sum(jnp.where(earlier, orbital_counts[None, :], 0), axis=1)
    first = jnp.sum(earlier.astype(jnp.int32), axis=1) == 0
    ahead = (load[None, :] > load[:, None]) | (
        (load[None, :] == load[:, None]) & (block_owner[None, :] < block_owner[:, None])
    )
    rank = jnp.sum((ahead & first[None, :]).astype(jnp.int32), axis=1)
    second = rank >= BINS
    bin_of = jnp.where(second, 2 * BINS - 1 - rank, rank)
    local = base + jnp.where(second, PART_A * GROUP, 0)
    room = jnp.zeros_like(load)
    for part, limits in enumerate(TIGHT):
        for limit in limits:
            room = room + jnp.where(second == (part == 1), has(limit, bin_of) * GROUP, 0)
    return bin_of, local, jnp.all(load <= room)


def pack_kernel(slots, start_ref, count_ref, source, packed, sem):
    def copies(block, act):
        count = count_ref[block]
        start = start_ref[block]
        for size in (16, 8, 4, 2, 1):
            offset = (count // (2 * size)) * (2 * size)

            @pl.when((count // size) % 2 == 1)
            def _(size=size, offset=offset):
                act(
                    pltpu.make_async_copy(
                        source.at[pl.ds(block * OB + offset, size)],
                        packed.at[pl.ds(start + offset, size)],
                        sem,
                    )
                )

    @pl.loop(0, source.shape[0] // OB)
    def _(block):
        copies(block, lambda copy: copy.start())

    @pl.loop(0, source.shape[0] // OB)
    def _(block):
        copies(block, lambda copy: copy.wait())


def position():
    z = lax.axis_index("grp")
    aux = lax.axis_index("aux")
    core = lax.rem(aux, 2)
    x = lax.rem(aux // 2, SIDE)
    y = aux // (2 * SIDE)
    return x, y, z, core


def device(x, y, z, core):
    return (z, (y * SIDE + x) * 2 + core)


def bin_index(x, y, z, core):
    kind = lax.rem(x, 2) + 2 * lax.rem(y, 2) + 4 * lax.rem(z, 2)
    return kind + core * (BINS - 1 - 2 * kind)


def shifted(value, by):
    return lax.rem(value + by + SIDE, SIDE)


def gram_kernel(
    limits,
    packed,
    out,
    held,
    tiles,
    parts,
    send_sem,
    recv_sem,
    local_sem,
    tile_send,
    tile_recv,
    out_buf,
    out_sem,
    exact,
    exact_parts,
    exact_send,
    exact_recv,
):
    x, y, z, core = position()
    sign = 1 - 2 * core
    own_bin = bin_index(x, y, z, core)
    own_part = x // 2 + 2 * (y // 2) + 4 * (z // 2)
    counts = [len(limits[0]), len(limits[1])]
    limits = limits[0] + limits[1]
    groups = len(limits)
    bits = [(d % 2, (d // 2) % 2, d // 4) for d in range(8)]

    barrier = pltpu.get_barrier_semaphore()

    def greet(target):
        pl.semaphore_signal(barrier, inc=1, device_id=target, device_id_type=MESH)

    greet(device(x, y, z, 1 - core))
    for d in range(1, 8):
        dx, dy, dz = bits[d]
        greet(device(shifted(x, -dx), shifted(y, -dy), shifted(z, -dz), 0))
        greet(device(shifted(x, dx), shifted(y, dy), shifted(z, dz), 1))
        greet(device(shifted(x, 2 * dx), shifted(y, 2 * dy), shifted(z, 2 * dz), core))
    pl.semaphore_wait(barrier, 22)

    def gather(d, target_core, group, act):
        dx, dy, dz = bits[d]
        tx, ty, tz = shifted(x, sign * dx), shifted(y, sign * dy), shifted(z, sign * dz)
        target_bin = bin_index(tx, ty, tz, target_core)
        copy = pltpu.make_async_remote_copy(
            src_ref=packed.at[target_bin, group],
            dst_ref=held.at[2 * d + core, group],
            send_sem=send_sem.at[2 * d + target_core, group],
            recv_sem=recv_sem.at[2 * d + core, group],
            device_id=device(tx, ty, tz, target_core),
            device_id_type=MESH,
        )
        when(group, target_bin, lambda: act(copy))

    def when(group, index, act):
        if limits[group] == ALL:
            act()
        else:
            pl.when(has(limits[group], index))(act)

    def keep(group):
        return pltpu.make_async_copy(
            packed.at[own_bin, group], held.at[core, group], local_sem.at[group]
        )

    for group in range(groups):
        when(group, own_bin, lambda: keep(group).start())
        for d in range(1, 8):
            for target_core in range(2):
                gather(d, target_core, group, lambda copy: copy.start())
        gather(0, 1 - core, group, lambda copy: copy.start())

    def arrived(group):
        keep(group).wait()
        pltpu.make_async_copy(
            held.at[1 - core, group], held.at[1 - core, group], recv_sem.at[1 - core, group]
        ).wait()
        for source in range(2, BINS):
            pltpu.make_async_copy(
                held.at[source, group], held.at[source, group], recv_sem.at[source, group]
            ).wait()

    def rows_of(group):
        return jnp.concatenate([held[source, group] for source in range(BINS)], axis=1)

    def scatter(e, first, count, column):
        dx, dy, dz = bits[e]
        px, py, pz = shifted(x, 2 * dx), shifted(y, 2 * dy), shifted(z, 2 * dz)
        part = px // 2 + 2 * (py // 2) + 4 * (pz // 2)
        return pltpu.make_async_remote_copy(
            src_ref=tiles.at[part, pl.ds(first, count)],
            dst_ref=parts.at[e - 1, pl.ds(first, count)],
            send_sem=tile_send.at[e - 1, column],
            recv_sem=tile_recv.at[e - 1, column],
            device_id=device(px, py, pz, core),
            device_id_type=MESH,
        )

    columns = []
    first = 0
    for base, count in ((0, counts[0]), (counts[0], counts[1])):
        for v in range(count):
            columns.append((base, v, first))
            first += v + 1
    same_row = lax.broadcasted_iota(jnp.int32, (ROWS, ROWS), 0) == lax.broadcasted_iota(
        jnp.int32, (ROWS, ROWS), 1
    )

    def make_column(column, base, v, first):
        arrived(base + v)

        @pl.loop(0, v + 1)
        def _(u):
            tile = lax.dot_general(
                rows_of(base + u),
                rows_of(base + v),
                (((1,), (1,)), ((), ())),
                preferred_element_type=jnp.float32,
            )

            @pl.when(u == v)
            def _():
                exact[pl.ds(column, 1), :] = jnp.sum(
                    jnp.where(same_row, tile, 0.0), axis=0, keepdims=True
                )

            rounded = tile.astype(jnp.bfloat16)
            for part in range(8):
                tiles[part, first + u] = rounded[part * NV : (part + 1) * NV]

        for e in range(1, 8):
            scatter(e, first, v + 1, column).start()

    for column, (base, v, first) in enumerate(columns):
        when(column, own_bin, functools.partial(make_column, column, base, v, first))

    def scatter_exact(e):
        dx, dy, dz = bits[e]
        px, py, pz = shifted(x, 2 * dx), shifted(y, 2 * dy), shifted(z, 2 * dz)
        return pltpu.make_async_remote_copy(
            src_ref=exact,
            dst_ref=exact_parts.at[e - 1],
            send_sem=exact_send.at[e - 1],
            recv_sem=exact_recv.at[e - 1],
            device_id=device(px, py, pz, core),
            device_id_type=MESH,
        )

    for e in range(1, 8):
        scatter_exact(e).start()
    for e in range(1, 8):
        scatter_exact(e).wait()
    exact[...] = exact[...] + jnp.sum(exact_parts[...], axis=0)
    own_diagonal = (
        lax.broadcasted_iota(jnp.int32, (NV, ROWS), 0) + own_part * NV
        == lax.broadcasted_iota(jnp.int32, (NV, ROWS), 1)
    )

    def add_column(column, base, v, first):
        for e in range(1, 8):
            scatter(e, first, v + 1, column).wait_recv()

        @pl.loop(first, first + v + 1)
        def _(index):
            total = tiles[own_part, index].astype(jnp.float32)
            for e in range(7):
                total = total + parts[e, index].astype(jnp.float32)
            out_buf[index] = total

        out_buf[first + v] = jnp.where(own_diagonal, exact[pl.ds(column, 1), :], out_buf[first + v])

    for column, (base, v, first) in enumerate(columns):
        when(column, own_bin, functools.partial(add_column, column, base, v, first))

    done = pltpu.make_async_copy(out_buf, out, out_sem)
    done.start()

    def sent_column(column, base, v, first):
        for e in range(1, 8):
            scatter(e, first, v + 1, column).wait_send()

    for column, (base, v, first) in enumerate(columns):
        when(column, own_bin, functools.partial(sent_column, column, base, v, first))
    for group in range(groups):
        gather(0, 1 - core, group, lambda copy: copy.wait_send())
        for d in range(1, 8):
            for target_core in range(2):
                gather(d, target_core, group, lambda copy: copy.wait_send())
    done.wait()


def density_kernel(counts, block_ref, part_ref, strips, row_energy, column_energy, mask, density, fold):
    part = part_ref[0]
    density[...] = jnp.zeros_like(density)
    row_slot = lax.broadcasted_iota(jnp.int32, (ROWS, ROWS), 0) // NV
    column_slot = lax.broadcasted_iota(jnp.int32, (ROWS, ROWS), 1) // NV
    diagonal = row_slot == column_slot
    fold[...] = (
        lax.rem(lax.broadcasted_iota(jnp.int32, (ROWS, NV), 0), NV)
        == lax.broadcasted_iota(jnp.int32, (ROWS, NV), 1)
    ).astype(jnp.float32)
    first = 0
    for base, count in ((0, counts[0]), (counts[0], counts[1])):
        row_sums = [jnp.zeros((NV, NV), jnp.float32) for u in range(count)]
        for v in range(count):
            stack = []
            for u in range(v + 1):
                kind = mask[base + u, base + v]
                quotient = strips[first + u] / (row_energy[base + u] + column_energy[base + v])
                amplitude = jnp.where(kind > 0, quotient, 0.0).astype(jnp.bfloat16)
                row_sums[u] = row_sums[u] + lax.dot_general(
                    amplitude, amplitude, (((1,), (1,)), ((), ())), preferred_element_type=jnp.float32
                )
                if u == v:
                    amplitude = jnp.where(kind > 1, quotient, 0.0).astype(jnp.bfloat16)
                stack.append(amplitude)
            first += v + 1
            stacked = jnp.concatenate(stack, axis=0)
            product = lax.dot_general(
                stacked, stacked, (((0,), (0,)), ((), ())), preferred_element_type=jnp.float32
            )
            folded = jnp.dot(
                jnp.where(diagonal, product, 0.0),
                fold[...],
                precision=lax.Precision.HIGHEST,
                preferred_element_type=jnp.float32,
            )
            for j in range(GROUP):
                block = block_ref[(base + v) * GROUP + j]
                density[block] = density[block] + folded[j * NV : (j + 1) * NV]
        for u in range(count):
            block = block_ref[(base + u) * GROUP + part]
            density[block] = density[block] + row_sums[u]


def exchange_kernel(spread, out, held, total, summed, z_send, z_recv, send_sem, recv_sem):
    z = lax.axis_index("grp")
    aux = lax.axis_index("aux")
    groups = lax.axis_size("grp")
    owners = lax.axis_size("aux")
    rows = out.shape[0]
    barrier = pltpu.get_barrier_semaphore()
    for step in range(1, groups):
        pl.semaphore_signal(
            barrier, inc=1, device_id=(lax.rem(z + step, groups), aux), device_id_type=MESH
        )

    @pl.loop(1, owners)
    def _(step):
        pl.semaphore_signal(
            barrier, inc=1, device_id=(z, lax.rem(aux + step, owners)), device_id_type=MESH
        )

    pl.semaphore_wait(barrier, groups + owners - 2)

    def across(step):
        target = lax.rem(z + step, groups)
        return pltpu.make_async_remote_copy(
            src_ref=spread.at[target],
            dst_ref=held.at[step - 1],
            send_sem=z_send.at[step - 1],
            recv_sem=z_recv.at[step - 1],
            device_id=(target, aux),
            device_id_type=MESH,
        )

    for step in range(1, groups):
        across(step).start()
    for step in range(1, groups):
        across(step).wait_recv()
    total[...] = spread[z] + held[0] + held[1] + held[2]

    def along(step):
        target = lax.rem(aux + step, owners)
        return pltpu.make_async_remote_copy(
            src_ref=total.at[pl.ds(pl.multiple_of(target * rows, rows), rows)],
            dst_ref=summed.at[step],
            send_sem=send_sem.at[step],
            recv_sem=recv_sem.at[step],
            device_id=(z, target),
            device_id_type=MESH,
        )

    @pl.loop(1, owners)
    def _(step):
        along(step).start()

    summed[0] = total[pl.ds(pl.multiple_of(aux * rows, rows), rows), :]

    @pl.loop(1, owners)
    def _(step):
        along(step).wait_recv()

    out[...] = jnp.sum(summed[...], axis=0)

    @pl.loop(1, owners)
    def _(step):
        along(step).wait_send()

    for step in range(1, groups):
        across(step).wait_send()


def partial_density(
    limits,
    collective_id,
    bin_of,
    start,
    three_index,
    pair_screen,
    orbital_counts,
    occupied_energy,
    virtual_energy,
):
    blocks, row_count, aux_local = three_index.shape
    counts = [len(part) for part in limits]
    groups = sum(counts)
    slots = groups * GROUP
    tile_count = sum(count * (count + 1) // 2 for count in counts)

    packed = pl.pallas_call(
        functools.partial(pack_kernel, slots),
        out_shape=jax.ShapeDtypeStruct((BINS * slots, NV, aux_local), jnp.bfloat16),
        in_specs=[SMEM, SMEM, ANY],
        out_specs=ANY,
        scratch_shapes=[pltpu.SemaphoreType.DMA],
    )(bin_of * slots + start, orbital_counts, three_index.reshape(blocks * OB, NV, aux_local))

    strips = pl.pallas_call(
        functools.partial(gram_kernel, limits),
        out_shape=jax.ShapeDtypeStruct((tile_count, NV, ROWS), jnp.float32),
        in_specs=[ANY],
        out_specs=ANY,
        scratch_shapes=[
            pltpu.VMEM((BINS, groups, ROWS, aux_local), jnp.bfloat16),
            pltpu.VMEM((8, tile_count, NV, ROWS), jnp.bfloat16),
            pltpu.VMEM((7, tile_count, NV, ROWS), jnp.bfloat16),
            pltpu.SemaphoreType.DMA((BINS, groups)),
            pltpu.SemaphoreType.DMA((BINS, groups)),
            pltpu.SemaphoreType.DMA((groups,)),
            pltpu.SemaphoreType.DMA((7, groups)),
            pltpu.SemaphoreType.DMA((7, groups)),
            pltpu.VMEM((tile_count, NV, ROWS), jnp.float32),
            pltpu.SemaphoreType.DMA,
            pltpu.VMEM((16, ROWS), jnp.float32),
            pltpu.VMEM((7, 16, ROWS), jnp.float32),
            pltpu.SemaphoreType.DMA((7,)),
            pltpu.SemaphoreType.DMA((7,)),
        ],
        compiler_params=pltpu.CompilerParams(
            collective_id=collective_id, has_side_effects=True, vmem_limit_bytes=58 * 2**20
        ),
    )(packed.reshape(BINS, groups, ROWS, aux_local))

    x, y, z, core = position()
    own_bin = bin_index(x, y, z, core)
    own_part = x // 2 + 2 * (y // 2) + 4 * (z // 2)
    slot_ids = jnp.arange(slots, dtype=jnp.int32)
    inside = (
        (bin_of[None, :] == own_bin)
        & (start[None, :] <= slot_ids[:, None])
        & (slot_ids[:, None] < (start + orbital_counts)[None, :])
    )
    pick = inside.astype(jnp.float32)
    slot_block = jnp.sum(jnp.where(inside, jnp.arange(blocks, dtype=jnp.int32)[None, :], 0), axis=1)
    orbital = slot_ids[:, None] - start[None, :]
    occupied = jnp.sum(
        jnp.where(
            inside[:, :, None] & (orbital[:, :, None] == jnp.arange(OB, dtype=jnp.int32)),
            occupied_energy[None],
            0.0,
        ),
        axis=(1, 2),
    )
    energy = (
        jnp.sum(jnp.where(inside[:, :, None], virtual_energy[None], 0.0), axis=1) - occupied[:, None]
    )
    row_pick = lax.dynamic_index_in_dim(pick.reshape(groups, GROUP, blocks), own_part, 1, False)
    row_energy = lax.dynamic_index_in_dim(energy.reshape(groups, GROUP, NV), own_part, 1, False)
    screen = (pair_screen == 1).astype(jnp.float32)
    live = jnp.dot(jnp.dot(row_pick, screen), pick.T)
    row_ids = jnp.arange(groups, dtype=jnp.int32) * GROUP + own_part
    kind = jnp.where(
        live > 0.5,
        jnp.where(row_ids[:, None] < slot_ids, 2.0, jnp.where(row_ids[:, None] == slot_ids, 1.0, 0.0)),
        0.0,
    )
    kind = jnp.broadcast_to(kind.reshape(groups, groups, 1, GROUP, 1), (groups, groups, 1, GROUP, NV))

    return pl.pallas_call(
        functools.partial(density_kernel, counts),
        out_shape=jax.ShapeDtypeStruct((blocks, NV, NV), jnp.float32),
        in_specs=[SMEM, SMEM, VMEM, VMEM, VMEM, VMEM],
        out_specs=VMEM,
        scratch_shapes=[pltpu.VMEM((ROWS, NV), jnp.float32)],
        compiler_params=pltpu.CompilerParams(vmem_limit_bytes=40 * 2**20),
    )(
        slot_block,
        own_part.reshape(1),
        strips,
        row_energy.reshape(groups, NV, 1),
        energy.reshape(groups, 1, ROWS),
        kind.reshape(groups, groups, 1, ROWS),
    )


def local(three_index, block_owner, pair_screen, orbital_counts, occupied_energy, virtual_energy):
    bin_of, start, fits = plan(block_owner, orbital_counts)
    density = lax.cond(
        fits,
        functools.partial(partial_density, TIGHT, 0),
        functools.partial(partial_density, ROOMY, 2),
        bin_of,
        start,
        three_index,
        pair_screen,
        orbital_counts,
        occupied_energy,
        virtual_energy,
    )

    groups_z = lax.axis_size("grp")
    owners = lax.axis_size("aux")
    width = NV // groups_z
    spread = density.reshape(owners, 2, groups_z, width, NV).transpose(2, 0, 3, 1, 4)
    spread = jnp.pad(spread, ((0, 0), (0, 0), (0, 16 - width), (0, 0), (0, 64 - NV)))
    spread = spread.reshape(groups_z, owners * 16, 128)
    home = pl.pallas_call(
        exchange_kernel,
        out_shape=jax.ShapeDtypeStruct((16, 128), jnp.float32),
        in_specs=[VMEM],
        out_specs=VMEM,
        scratch_shapes=[
            pltpu.VMEM((groups_z - 1, owners * 16, 128), jnp.float32),
            pltpu.VMEM((owners * 16, 128), jnp.float32),
            pltpu.VMEM((owners, 16, 128), jnp.float32),
            pltpu.SemaphoreType.DMA((groups_z - 1,)),
            pltpu.SemaphoreType.DMA((groups_z - 1,)),
            pltpu.SemaphoreType.DMA((owners,)),
            pltpu.SemaphoreType.DMA((owners,)),
        ],
        compiler_params=pltpu.CompilerParams(
            collective_id=1, has_side_effects=True, vmem_limit_bytes=32 * 2**20
        ),
    )(spread)
    return home.reshape(16, 2, 64)[:width, :, :NV].transpose(1, 0, 2)


def solution(mesh):
    in_specs = (P(None, None, ("grp", "aux")), P(), P(), P(), P(), P())
    out_specs = P("aux", "grp", None)
    return jax.shard_map(local, mesh=mesh, in_specs=in_specs, out_specs=out_specs, check_vma=False)
```

```python
import jax
import jax.numpy as jnp
from jax import lax
from jax.experimental import pallas as pl
from jax.experimental.pallas import tpu as pltpu
from jax.sharding import PartitionSpec as P

CAP = 3


def slot_tiles(source, slot_block, slot_valid, owners):
    picked = jnp.take(source, slot_block.reshape(-1), axis=0)
    picked = picked.reshape(owners, CAP, source.shape[1], source.shape[2])
    return jnp.where(slot_valid[:, :, None, None] > 0, picked, jnp.zeros_like(picked))


def pair_block(received, first, second):
    return lax.dot_general(
        received[:, first],
        received[:, second],
        (((0, 2), (0, 2)), ((), ())),
        preferred_element_type=jnp.float32,
    )


def general(three_index, block_owner, pair_screen, orbital_counts, occupied_energy, virtual_energy):
    block_count, row_count, aux_local = three_index.shape
    occupied_width = occupied_energy.shape[1]
    virtual_width = virtual_energy.shape[1]
    groups = lax.axis_size("grp")
    owners = lax.axis_size("aux")
    own_index = lax.axis_index("aux")
    group_index = lax.axis_index("grp")
    quarter = row_count // groups
    owner_ids = jnp.arange(owners, dtype=jnp.int32)
    owned = (block_owner[None, :] == owner_ids[:, None]).astype(jnp.int32)
    slot_rank = jnp.cumsum(owned, axis=1) - 1
    slot_ids = jnp.arange(CAP, dtype=jnp.int32)
    selection = owned[:, None, :] * (slot_rank[:, None, :] == slot_ids[None, :, None]).astype(
        jnp.int32
    )
    block_ids = jnp.arange(block_count, dtype=jnp.int32)
    slot_block = jnp.sum(selection * block_ids[None, None, :], axis=2)
    slot_valid = jnp.sum(selection, axis=2)
    mine = lax.dynamic_index_in_dim(selection, own_index, 0, keepdims=False)
    my_block = jnp.sum(mine * block_ids[None, :], axis=1)
    my_valid = jnp.sum(mine, axis=1)
    energy = (virtual_energy[:, None, :] - occupied_energy[:, :, None]).reshape(
        block_count, row_count
    )
    occupied_flags = (
        jnp.arange(occupied_width, dtype=jnp.int32)[None, :] < orbital_counts[:, None]
    ).astype(jnp.float32)
    occupancy = jnp.repeat(occupied_flags, virtual_width, axis=1)
    slot_energy = jnp.take(energy, my_block, axis=0)
    slot_occupancy = jnp.take(occupancy, my_block, axis=0)
    screened = jnp.take(jnp.take(pair_screen, my_block, axis=0), my_block, axis=1)
    is_live = screened * my_valid[:, None] * my_valid[None, :] > 0

    def slot_amplitude(integral, first, second):
        energy_rows = lax.dynamic_slice_in_dim(slot_energy[first], group_index * quarter, quarter)
        occupied_rows = lax.dynamic_slice_in_dim(
            slot_occupancy[first], group_index * quarter, quarter
        )
        divisor = energy_rows[:, None] + slot_energy[second][None, :]
        return (
            occupied_rows[:, None] * slot_occupancy[second][None, :] * integral / divisor
        ).astype(jnp.bfloat16)

    def own_density(amplitude):
        row_form = amplitude.reshape(quarter // virtual_width, virtual_width, row_count)
        return jnp.einsum("iax,ibx->ab", row_form, row_form, preferred_element_type=jnp.float32)

    outgoing = slot_tiles(three_index, slot_block, slot_valid, owners)
    received = lax.all_to_all(outgoing, "aux", split_axis=0, concat_axis=0, tiled=True)
    zero_block = jnp.zeros((row_count, row_count), jnp.float32)
    empty = jnp.zeros((virtual_width, virtual_width), jnp.float32)
    pair_keys = [(first, second) for first in range(CAP) for second in range(first, CAP)]
    uppers = []
    for first, second in pair_keys:
        uppers.append(
            lax.cond(
                is_live[first, second],
                lambda first=first, second=second: pair_block(received, first, second),
                lambda: zero_block,
            )
        )
    slot_parts = [empty for first in range(CAP)]
    blocks = [[zero_block for second in range(CAP)] for first in range(CAP)]
    for index, (first, second) in enumerate(pair_keys):
        blocks[first][second] = uppers[index]
        blocks[second][first] = uppers[index].T
    stacked = jnp.stack([jnp.stack(line) for line in blocks])
    summed = lax.psum_scatter(stacked, "grp", scatter_dimension=2, tiled=True)
    for first in range(CAP):
        for second in range(CAP):

            def one_part(first=first, second=second):
                return own_density(slot_amplitude(summed[first, second], first, second))

            slot_parts[first] = slot_parts[first] + lax.cond(
                is_live[first, second], one_part, lambda: empty
            )
    spread = jnp.stack(slot_parts).reshape(CAP, groups, virtual_width // groups, virtual_width)
    placed = jnp.einsum(
        "cb,cgxy->gbxy", mine.astype(jnp.float32), spread, precision=lax.Precision.HIGHEST
    )
    placed = placed.reshape(groups * block_count, virtual_width // groups, virtual_width)
    return lax.psum_scatter(placed, ("grp", "aux"), scatter_dimension=0, tiled=True)


NV = 48
OB = 16
BINS = 16
GROUP = 8
ROWS = GROUP * NV
SIDE = 4
PART_A = 6
PART_B = 2
GROUPS = PART_A + PART_B
SLOTS = GROUPS * GROUP
CHUNK = 16
ALL = (0, BINS)
LIMITS = (ALL, ALL, ALL, (0, 15), (0, 9), (0, 4), ALL, (2, BINS))
COLUMNS = tuple(
    [(0, v, v * (v + 1) // 2) for v in range(PART_A)]
    + [(PART_A, v, PART_A * (PART_A + 1) // 2 + v * (v + 1) // 2) for v in range(PART_B)]
)
TILES = PART_A * (PART_A + 1) // 2 + PART_B * (PART_B + 1) // 2
BITS = [(d % 2, (d // 2) % 2, d // 4) for d in range(8)]
MESH = pl.DeviceIdType.MESH
VMEM = pl.BlockSpec(memory_space=pltpu.VMEM)
SMEM = pl.BlockSpec(memory_space=pltpu.SMEM)
ANY = pl.BlockSpec(memory_space=pl.ANY)


def has(limits, index):
    first, end = limits
    return (index >= first) & (index < end)


def plan(block_owner, orbital_counts):
    ids = jnp.arange(block_owner.shape[0], dtype=jnp.int32)
    same = block_owner[:, None] == block_owner[None, :]
    earlier = same & (ids[None, :] < ids[:, None])
    load = jnp.sum(jnp.where(same, orbital_counts[None, :], 0), axis=1)
    base = jnp.sum(jnp.where(earlier, orbital_counts[None, :], 0), axis=1)
    place = jnp.sum(earlier.astype(jnp.int32), axis=1)
    ahead = (load[None, :] > load[:, None]) | (
        (load[None, :] == load[:, None]) & (block_owner[None, :] < block_owner[:, None])
    )
    rank = jnp.sum((ahead & (place == 0)[None, :]).astype(jnp.int32), axis=1)
    second = rank >= BINS
    bin_of = jnp.where(second, 2 * BINS - 1 - rank, rank)
    local = base + jnp.where(second, PART_A * GROUP, 0)
    room = jnp.zeros_like(load)
    for group, limits in enumerate(LIMITS):
        room = room + jnp.where(second == (group >= PART_A), has(limits, bin_of) * GROUP, 0)
    return bin_of, local, place, second, jnp.all(load <= room)


def position():
    z = lax.axis_index("grp")
    aux = lax.axis_index("aux")
    core = lax.rem(aux, 2)
    x = lax.rem(aux // 2, SIDE)
    y = aux // (2 * SIDE)
    return x, y, z, core


def device(x, y, z, core):
    return (z, (y * SIDE + x) * 2 + core)


def bin_index(x, y, z, core):
    kind = lax.rem(x, 2) + 2 * lax.rem(y, 2) + 4 * lax.rem(z, 2)
    return kind + core * (BINS - 1 - 2 * kind)


def part_index(x, y, z):
    return x // 2 + 2 * (y // 2) + 4 * (z // 2)


def shifted(value, by):
    return lax.rem(value + by + SIDE, SIDE)


def kernel(
    origin_ref,
    place_ref,
    block_ref,
    source,
    row_energy,
    column_energy,
    mask,
    out,
    whole,
    packed,
    held,
    tiles,
    parts,
    exact,
    exact_parts,
    stack,
    row_sums,
    slot_sums,
    fold,
    chunks,
    chunk_parts,
    dense,
    homes,
    load_sem,
    local_sem,
    send_sem,
    recv_sem,
    tile_send,
    tile_recv,
    exact_send,
    exact_recv,
    chunk_send,
    chunk_recv,
    home_send,
    home_recv,
):
    x, y, z, core = position()
    aux = lax.axis_index("aux")
    owners = lax.axis_size("aux")
    sign = 1 - 2 * core
    own_bin = bin_index(x, y, z, core)
    own_part = part_index(x, y, z)
    quarter = lax.rem(own_part, SIDE)
    half = own_part // SIDE

    pieces = load_sem.shape[0]
    size = source.shape[0] // pieces

    def load(piece):
        part = pl.ds(piece * size, size)
        return pltpu.make_async_copy(source.at[part], whole.at[part], load_sem.at[piece])

    for piece in range(pieces):
        load(piece).start()

    barrier = pltpu.get_barrier_semaphore()

    def greet(target):
        pl.semaphore_signal(barrier, inc=1, device_id=target, device_id_type=MESH)

    greet(device(x, y, z, 1 - core))
    for d in range(1, 8):
        dx, dy, dz = BITS[d]
        greet(device(shifted(x, -dx), shifted(y, -dy), shifted(z, -dz), 0))
        greet(device(shifted(x, dx), shifted(y, dy), shifted(z, dz), 1))
        greet(device(shifted(x, 2 * dx), shifted(y, 2 * dy), shifted(z, 2 * dz), core))

    def feeder(index):
        number = index // 2
        feed_core = number // 8
        kind = number + feed_core * (BINS - 1 - 2 * number)
        return (
            lax.rem(kind, 2) + 2 * lax.rem(z, 2),
            lax.rem(kind // 2, 2) + 2 * (z // 2),
            kind // 4 + 2 * lax.rem(index, 2),
            feed_core,
        )

    own_feed = own_bin * 2 + half

    @pl.loop(0, owners)
    def _(index):
        @pl.when((quarter != z) | (index != own_feed))
        def _():
            greet(device(*feeder(index)))

    fold[...] = (
        lax.rem(lax.broadcasted_iota(jnp.int32, (ROWS, NV), 0), NV)
        == lax.broadcasted_iota(jnp.int32, (ROWS, NV), 1)
    ).astype(jnp.float32)
    slot_sums[...] = jnp.zeros_like(slot_sums)
    row_sums[...] = jnp.zeros_like(row_sums)
    chunks[...] = jnp.zeros_like(chunks)

    for piece in range(pieces):
        load(piece).wait()
    pl.semaphore_wait(barrier, 22 + owners - (quarter == z).astype(jnp.int32))

    def when(group, index, act):
        if LIMITS[group] == ALL:
            act()
        else:
            pl.when(has(LIMITS[group], index))(act)

    def gather(d, target_core, group, act):
        dx, dy, dz = BITS[d]
        tx, ty, tz = shifted(x, sign * dx), shifted(y, sign * dy), shifted(z, sign * dz)
        target_bin = bin_index(tx, ty, tz, target_core)
        copy = pltpu.make_async_remote_copy(
            src_ref=packed.at[target_bin, group],
            dst_ref=held.at[2 * d + core, group],
            send_sem=send_sem.at[2 * d + target_core, group],
            recv_sem=recv_sem.at[2 * d + core, group],
            device_id=device(tx, ty, tz, target_core),
            device_id_type=MESH,
        )
        when(group, target_bin, lambda: act(copy))

    def keep(group):
        return pltpu.make_async_copy(
            packed.at[own_bin, group], held.at[core, group], local_sem.at[group]
        )

    for group in range(GROUPS):

        @pl.loop(0, BINS)
        def _(number):
            for slot in range(GROUP):
                origin = origin_ref[number * SLOTS + group * GROUP + slot]
                packed[number, group, slot * NV : (slot + 1) * NV, :] = whole[origin]

        for d in range(7, 0, -1):
            for target_core in range(2):
                gather(d, target_core, group, lambda copy: copy.start())
        gather(0, 1 - core, group, lambda copy: copy.start())
        when(group, own_bin, lambda: keep(group).start())

    def arrived(group):
        keep(group).wait()
        pltpu.make_async_copy(
            held.at[1 - core, group], held.at[1 - core, group], recv_sem.at[1 - core, group]
        ).wait()
        for sender in range(2, BINS):
            pltpu.make_async_copy(
                held.at[sender, group], held.at[sender, group], recv_sem.at[sender, group]
            ).wait()

    def rows_of(group):
        return jnp.concatenate([held[sender, group] for sender in range(BINS)], axis=1)

    def peer(e):
        dx, dy, dz = BITS[e]
        px, py, pz = shifted(x, 2 * dx), shifted(y, 2 * dy), shifted(z, 2 * dz)
        return part_index(px, py, pz), device(px, py, pz, core)

    def scatter(e, column):
        base, v, first = COLUMNS[column]
        part, target = peer(e)
        return pltpu.make_async_remote_copy(
            src_ref=tiles.at[part, pl.ds(first, v + 1)],
            dst_ref=parts.at[e - 1, pl.ds(first, v + 1)],
            send_sem=tile_send.at[e - 1, column],
            recv_sem=tile_recv.at[e - 1, column],
            device_id=target,
            device_id_type=MESH,
        )

    def scatter_exact(e, column):
        part, target = peer(e)
        return pltpu.make_async_remote_copy(
            src_ref=exact.at[column],
            dst_ref=exact_parts.at[e - 1, column],
            send_sem=exact_send.at[e - 1, column],
            recv_sem=exact_recv.at[e - 1, column],
            device_id=target,
            device_id_type=MESH,
        )

    row_number = lax.broadcasted_iota(jnp.int32, (ROWS, ROWS), 0)
    column_number = lax.broadcasted_iota(jnp.int32, (ROWS, ROWS), 1)

    def make_column(column):
        base, v, first = COLUMNS[column]
        arrived(base + v)

        @pl.loop(0, v + 1)
        def _(u):
            tile = lax.dot_general(
                rows_of(base + u),
                rows_of(base + v),
                (((1,), (1,)), ((), ())),
                preferred_element_type=jnp.float32,
            )

            @pl.when(u == v)
            def _():
                diagonal = jnp.where(row_number == column_number, tile, 0.0)
                exact[column] = jnp.broadcast_to(
                    jnp.sum(diagonal, axis=0, keepdims=True), exact.shape[1:]
                )

            rounded = tile.astype(jnp.bfloat16)
            for part in range(8):
                tiles[part, first + u] = rounded[part * NV : (part + 1) * NV]

        for e in range(7, 0, -1):
            scatter(e, column).start()
            scatter_exact(e, column).start()

    own_diagonal = (
        lax.broadcasted_iota(jnp.int32, (NV, ROWS), 0) + own_part * NV
        == lax.broadcasted_iota(jnp.int32, (NV, ROWS), 1)
    )

    def add_column(column):
        base, v, first = COLUMNS[column]
        for e in range(1, 8):
            scatter(e, column).wait_recv()
            scatter_exact(e, column).wait_recv()
        diagonal = exact[column]
        for e in range(7):
            diagonal = diagonal + exact_parts[e, column]

        @pl.loop(0, v + 1)
        def _(u):
            integral = tiles[own_part, first + u].astype(jnp.float32)
            for e in range(7):
                integral = integral + parts[e, first + u].astype(jnp.float32)
            integral = jnp.where(own_diagonal & (u == v), diagonal[:1], integral)
            kind = mask[base + u, base + v]
            quotient = integral / (row_energy[base + u] + column_energy[base + v])
            amplitude = jnp.where(kind > 0, quotient, 0.0).astype(jnp.bfloat16)
            row_sums[base + u] = row_sums[base + u] + lax.dot_general(
                amplitude, amplitude, (((1,), (1,)), ((), ())), preferred_element_type=jnp.float32
            )
            stack[pl.ds(pl.multiple_of(u * NV, NV), NV), :] = jnp.where(
                kind > 1, quotient, 0.0
            ).astype(jnp.bfloat16)

        stacked = stack[: (v + 1) * NV, :]
        product = lax.dot_general(
            stacked, stacked, (((0,), (0,)), ((), ())), preferred_element_type=jnp.float32
        )
        slot_sums[(base + v) * ROWS : (base + v + 1) * ROWS, :] = jnp.dot(
            jnp.where(row_number // NV == column_number // NV, product, 0.0),
            fold[...],
            precision=lax.Precision.HIGHEST,
            preferred_element_type=jnp.float32,
        )

    for column in range(GROUPS):
        when(column, own_bin, lambda: make_column(column))
        if column >= 2:
            when(column - 2, own_bin, lambda: add_column(column - 2))
    for column in range(GROUPS - 2, GROUPS):
        when(column, own_bin, lambda: add_column(column))
    for group in range(GROUPS):
        part = pl.ds(pl.multiple_of(group * ROWS + own_part * NV, NV), NV)
        slot_sums[part, :] = slot_sums[part, :] + row_sums[group]

    for side in range(2):
        first_slot = side * PART_A * GROUP

        def add_slot(step, sums):
            slot = first_slot + step
            value = slot_sums[pl.ds(pl.multiple_of(slot * NV, NV), NV), :]
            number = place_ref[slot]
            return tuple(
                sums[i] + jnp.where(number == i, value, jnp.zeros_like(value)) for i in range(3)
            )

        zero = jnp.zeros((NV, NV), jnp.float32)
        sums = lax.fori_loop(0, (PART_A, PART_B)[side] * GROUP, add_slot, (zero, zero, zero))
        width = NV // SIDE
        for i in range(3):
            for g in range(SIDE):
                chunks[side * SIDE + g, i * CHUNK : i * CHUNK + width, :NV] = sums[i][
                    g * width : (g + 1) * width
                ]

    def scatter_chunk(e):
        part, target = peer(e)
        return pltpu.make_async_remote_copy(
            src_ref=chunks.at[part],
            dst_ref=chunk_parts.at[e - 1],
            send_sem=chunk_send.at[e - 1],
            recv_sem=chunk_recv.at[e - 1],
            device_id=target,
            device_id_type=MESH,
        )

    for e in range(7, 0, -1):
        scatter_chunk(e).start()
    for e in range(1, 8):
        scatter_chunk(e).wait_recv()
    total = chunks[own_part]
    for e in range(7):
        total = total + chunk_parts[e]
    pieces = [total[i * CHUNK : (i + 1) * CHUNK] for i in range(3)]
    turned = [pltpu.roll(piece, 64, 1) for piece in pieces]

    def send_home(target):
        return pltpu.make_async_remote_copy(
            src_ref=dense.at[target],
            dst_ref=homes.at[own_feed],
            send_sem=home_send.at[target],
            recv_sem=home_recv.at[own_feed],
            device_id=(quarter, target),
            device_id_type=MESH,
        )

    def away(target):
        return (quarter != z) | (target != aux)

    @pl.loop(0, owners)
    def _(target):
        message = jnp.zeros((CHUNK, 128), jnp.float32)
        for i in range(3):
            block = block_ref[i]
            message = message + jnp.where(block == 2 * target, pieces[i], 0.0)
            message = message + jnp.where(block == 2 * target + 1, turned[i], 0.0)
        dense[target] = message

        @pl.when(away(target))
        def _():
            send_home(target).start()

    @pl.when(quarter == z)
    def _():
        homes[own_feed] = dense[aux]

    @pl.loop(0, owners)
    def _(index):
        @pl.when((quarter != z) | (index != own_feed))
        def _():
            pltpu.make_async_copy(homes.at[index], homes.at[index], home_recv.at[index]).wait()

    out[...] = jnp.sum(homes[...], axis=0)

    @pl.loop(0, owners)
    def _(target):
        @pl.when(away(target))
        def _():
            send_home(target).wait_send()

    for e in range(1, 8):
        scatter_chunk(e).wait_send()

    def sent_column(column):
        for e in range(1, 8):
            scatter(e, column).wait_send()
            scatter_exact(e, column).wait_send()

    for column in range(GROUPS):
        when(column, own_bin, lambda: sent_column(column))
    for group in range(GROUPS):
        gather(0, 1 - core, group, lambda copy: copy.wait_send())
        for d in range(1, 8):
            for target_core in range(2):
                gather(d, target_core, group, lambda copy: copy.wait_send())


def binned(
    bin_of,
    start,
    place,
    second,
    three_index,
    block_owner,
    pair_screen,
    orbital_counts,
    occupied_energy,
    virtual_energy,
):
    blocks, row_count, aux_local = three_index.shape
    block_ids = jnp.arange(blocks, dtype=jnp.int32)
    slot_ids = jnp.arange(SLOTS, dtype=jnp.int32)
    within = (start[None, :] <= slot_ids[:, None]) & (
        slot_ids[:, None] < (start + orbital_counts)[None, :]
    )
    orbital = slot_ids[:, None] - start[None, :]
    bins = jnp.arange(BINS, dtype=jnp.int32)
    origin = jnp.sum(
        jnp.where(
            (bin_of[None, None, :] == bins[:, None, None]) & within[None],
            (block_ids[None, :] * OB + orbital)[None],
            0,
        ),
        axis=2,
    )
    x, y, z, core = position()
    own_bin = bin_index(x, y, z, core)
    own_part = part_index(x, y, z)
    inside = (bin_of[None, :] == own_bin) & within
    pick = inside.astype(jnp.float32)
    slot_place = jnp.sum(jnp.where(inside, place[None, :] + 1, 0), axis=1) - 1
    here = (bin_of == own_bin) & (second == (own_part >= SIDE))
    chunk_block = (
        jnp.sum(
            jnp.where(
                here[None, :] & (place[None, :] == jnp.arange(3, dtype=jnp.int32)[:, None]),
                block_ids[None, :] + 1,
                0,
            ),
            axis=1,
        )
        - 1
    )
    occupied = jnp.sum(
        jnp.where(
            inside[:, :, None] & (orbital[:, :, None] == jnp.arange(OB, dtype=jnp.int32)),
            occupied_energy[None],
            0.0,
        ),
        axis=(1, 2),
    )
    energy = (
        jnp.sum(jnp.where(inside[:, :, None], virtual_energy[None], 0.0), axis=1) - occupied[:, None]
    )
    row_pick = lax.dynamic_index_in_dim(pick.reshape(GROUPS, GROUP, blocks), own_part, 1, False)
    row_energy = lax.dynamic_index_in_dim(energy.reshape(GROUPS, GROUP, NV), own_part, 1, False)
    screen = (pair_screen == 1).astype(jnp.float32)
    live = jnp.dot(jnp.dot(row_pick, screen), pick.T)
    row_ids = jnp.arange(GROUPS, dtype=jnp.int32) * GROUP + own_part
    kind = jnp.where(
        live > 0.5,
        jnp.where(row_ids[:, None] < slot_ids, 2.0, jnp.where(row_ids[:, None] == slot_ids, 1.0, 0.0)),
        0.0,
    )
    kind = jnp.broadcast_to(kind.reshape(GROUPS, GROUPS, 1, GROUP, 1), (GROUPS, GROUPS, 1, GROUP, NV))
    owners = lax.axis_size("aux")
    home = pl.pallas_call(
        kernel,
        out_shape=jax.ShapeDtypeStruct((CHUNK, 128), jnp.float32),
        in_specs=[SMEM, SMEM, SMEM, ANY, VMEM, VMEM, VMEM],
        out_specs=VMEM,
        scratch_shapes=[
            pltpu.VMEM((blocks * OB, NV, aux_local), jnp.bfloat16),
            pltpu.VMEM((BINS, GROUPS, ROWS, aux_local), jnp.bfloat16),
            pltpu.VMEM((BINS, GROUPS, ROWS, aux_local), jnp.bfloat16),
            pltpu.VMEM((8, TILES, NV, ROWS), jnp.bfloat16),
            pltpu.VMEM((7, TILES, NV, ROWS), jnp.bfloat16),
            pltpu.VMEM((GROUPS, 8, ROWS), jnp.float32),
            pltpu.VMEM((7, GROUPS, 8, ROWS), jnp.float32),
            pltpu.VMEM((PART_A * NV, ROWS), jnp.bfloat16),
            pltpu.VMEM((GROUPS, NV, NV), jnp.float32),
            pltpu.VMEM((SLOTS * NV, NV), jnp.float32),
            pltpu.VMEM((ROWS, NV), jnp.float32),
            pltpu.VMEM((8, 3 * CHUNK, 128), jnp.float32),
            pltpu.VMEM((7, 3 * CHUNK, 128), jnp.float32),
            pltpu.VMEM((owners, CHUNK, 128), jnp.float32),
            pltpu.VMEM((owners, CHUNK, 128), jnp.float32),
            pltpu.SemaphoreType.DMA((8,)),
            pltpu.SemaphoreType.DMA((GROUPS,)),
            pltpu.SemaphoreType.DMA((BINS, GROUPS)),
            pltpu.SemaphoreType.DMA((BINS, GROUPS)),
            pltpu.SemaphoreType.DMA((7, GROUPS)),
            pltpu.SemaphoreType.DMA((7, GROUPS)),
            pltpu.SemaphoreType.DMA((7, GROUPS)),
            pltpu.SemaphoreType.DMA((7, GROUPS)),
            pltpu.SemaphoreType.DMA((7,)),
            pltpu.SemaphoreType.DMA((7,)),
            pltpu.SemaphoreType.DMA((owners,)),
            pltpu.SemaphoreType.DMA((owners,)),
        ],
        compiler_params=pltpu.CompilerParams(
            collective_id=0, has_side_effects=True, vmem_limit_bytes=60 * 2**20
        ),
    )(
        origin.reshape(-1),
        slot_place,
        chunk_block,
        three_index.reshape(blocks * OB, NV, aux_local),
        row_energy.reshape(GROUPS, NV, 1),
        energy.reshape(GROUPS, 1, ROWS),
        kind.reshape(GROUPS, GROUPS, 1, ROWS),
    )
    return home.reshape(CHUNK, 2, 64)[: NV // SIDE, :, :NV].transpose(1, 0, 2)


def local(three_index, block_owner, pair_screen, orbital_counts, occupied_energy, virtual_energy):
    bin_of, start, place, second, fits = plan(block_owner, orbital_counts)
    arguments = (
        three_index,
        block_owner,
        pair_screen,
        orbital_counts,
        occupied_energy,
        virtual_energy,
    )
    return lax.cond(
        fits,
        lambda: binned(bin_of, start, place, second, *arguments),
        lambda: general(*arguments),
    )


def solution(mesh):
    in_specs = (P(None, None, ("grp", "aux")), P(), P(), P(), P(), P())
    out_specs = P("aux", "grp", None)
    return jax.shard_map(local, mesh=mesh, in_specs=in_specs, out_specs=out_specs, check_vma=False)
```

```python
import jax
import jax.numpy as jnp
from jax import lax
from jax.experimental import pallas as pl
from jax.experimental.pallas import tpu as pltpu
from jax.sharding import PartitionSpec as P

CAP = 3


def slot_tiles(source, slot_block, slot_valid, owners):
    picked = jnp.take(source, slot_block.reshape(-1), axis=0)
    picked = picked.reshape(owners, CAP, source.shape[1], source.shape[2])
    return jnp.where(slot_valid[:, :, None, None] > 0, picked, jnp.zeros_like(picked))


def pair_block(received, first, second):
    return lax.dot_general(
        received[:, first],
        received[:, second],
        (((0, 2), (0, 2)), ((), ())),
        preferred_element_type=jnp.float32,
    )


def general(three_index, block_owner, pair_screen, orbital_counts, occupied_energy, virtual_energy):
    block_count, row_count, aux_local = three_index.shape
    occupied_width = occupied_energy.shape[1]
    virtual_width = virtual_energy.shape[1]
    groups = lax.axis_size("grp")
    owners = lax.axis_size("aux")
    own_index = lax.axis_index("aux")
    group_index = lax.axis_index("grp")
    quarter = row_count // groups
    owner_ids = jnp.arange(owners, dtype=jnp.int32)
    owned = (block_owner[None, :] == owner_ids[:, None]).astype(jnp.int32)
    slot_rank = jnp.cumsum(owned, axis=1) - 1
    slot_ids = jnp.arange(CAP, dtype=jnp.int32)
    selection = owned[:, None, :] * (slot_rank[:, None, :] == slot_ids[None, :, None]).astype(
        jnp.int32
    )
    block_ids = jnp.arange(block_count, dtype=jnp.int32)
    slot_block = jnp.sum(selection * block_ids[None, None, :], axis=2)
    slot_valid = jnp.sum(selection, axis=2)
    mine = lax.dynamic_index_in_dim(selection, own_index, 0, keepdims=False)
    my_block = jnp.sum(mine * block_ids[None, :], axis=1)
    my_valid = jnp.sum(mine, axis=1)
    energy = (virtual_energy[:, None, :] - occupied_energy[:, :, None]).reshape(
        block_count, row_count
    )
    occupied_flags = (
        jnp.arange(occupied_width, dtype=jnp.int32)[None, :] < orbital_counts[:, None]
    ).astype(jnp.float32)
    occupancy = jnp.repeat(occupied_flags, virtual_width, axis=1)
    slot_energy = jnp.take(energy, my_block, axis=0)
    slot_occupancy = jnp.take(occupancy, my_block, axis=0)
    screened = jnp.take(jnp.take(pair_screen, my_block, axis=0), my_block, axis=1)
    is_live = screened * my_valid[:, None] * my_valid[None, :] > 0

    def slot_amplitude(integral, first, second):
        energy_rows = lax.dynamic_slice_in_dim(slot_energy[first], group_index * quarter, quarter)
        occupied_rows = lax.dynamic_slice_in_dim(
            slot_occupancy[first], group_index * quarter, quarter
        )
        divisor = energy_rows[:, None] + slot_energy[second][None, :]
        return (
            occupied_rows[:, None] * slot_occupancy[second][None, :] * integral / divisor
        ).astype(jnp.bfloat16)

    def own_density(amplitude):
        row_form = amplitude.reshape(quarter // virtual_width, virtual_width, row_count)
        return jnp.einsum("iax,ibx->ab", row_form, row_form, preferred_element_type=jnp.float32)

    outgoing = slot_tiles(three_index, slot_block, slot_valid, owners)
    received = lax.all_to_all(outgoing, "aux", split_axis=0, concat_axis=0, tiled=True)
    zero_block = jnp.zeros((row_count, row_count), jnp.float32)
    empty = jnp.zeros((virtual_width, virtual_width), jnp.float32)
    pair_keys = [(first, second) for first in range(CAP) for second in range(first, CAP)]
    uppers = []
    for first, second in pair_keys:
        uppers.append(
            lax.cond(
                is_live[first, second],
                lambda first=first, second=second: pair_block(received, first, second),
                lambda: zero_block,
            )
        )
    slot_parts = [empty for first in range(CAP)]
    blocks = [[zero_block for second in range(CAP)] for first in range(CAP)]
    for index, (first, second) in enumerate(pair_keys):
        blocks[first][second] = uppers[index]
        blocks[second][first] = uppers[index].T
    stacked = jnp.stack([jnp.stack(line) for line in blocks])
    summed = lax.psum_scatter(stacked, "grp", scatter_dimension=2, tiled=True)
    for first in range(CAP):
        for second in range(CAP):

            def one_part(first=first, second=second):
                return own_density(slot_amplitude(summed[first, second], first, second))

            slot_parts[first] = slot_parts[first] + lax.cond(
                is_live[first, second], one_part, lambda: empty
            )
    spread = jnp.stack(slot_parts).reshape(CAP, groups, virtual_width // groups, virtual_width)
    placed = jnp.einsum(
        "cb,cgxy->gbxy", mine.astype(jnp.float32), spread, precision=lax.Precision.HIGHEST
    )
    placed = placed.reshape(groups * block_count, virtual_width // groups, virtual_width)
    return lax.psum_scatter(placed, ("grp", "aux"), scatter_dimension=0, tiled=True)


NV = 48
OB = 16
BINS = 16
GROUP = 8
ROWS = GROUP * NV
SIDE = 4
PART_A = 6
PART_B = 2
GROUPS = PART_A + PART_B
SLOTS = GROUPS * GROUP
CHUNK = 16
ALL = (0, BINS)
LIMITS = (ALL, ALL, ALL, (0, 15), (0, 9), (0, 4), ALL, (2, BINS))
STREAMS = tuple((GROUP * k, GROUP, ALL) for k in range(5)) + (
    (40, 4, ALL),
    (44, 4, (0, 8)),
    (48, 4, (0, 4)),
)
SENT = 52
COLUMNS = tuple(
    [(0, v, v * (v + 1) // 2) for v in range(PART_A)]
    + [(PART_A, v, PART_A * (PART_A + 1) // 2 + v * (v + 1) // 2) for v in range(PART_B)]
)
TILES = PART_A * (PART_A + 1) // 2 + PART_B * (PART_B + 1) // 2
UNITS = []
for column, (base, v, first) in enumerate(COLUMNS):
    for skip in range(0, v + 1, 2):
        turn = len(UNITS) % 3
        UNITS.append(
            (column, first + skip, min(2, v + 1 - skip), (turn, (turn + 1) % 3, (turn + 2) % 3))
        )
BITS = [(d % 2, (d // 2) % 2, d // 4) for d in range(8)]
MESH = pl.DeviceIdType.MESH
VMEM = pl.BlockSpec(memory_space=pltpu.VMEM)
SMEM = pl.BlockSpec(memory_space=pltpu.SMEM)
ANY = pl.BlockSpec(memory_space=pl.ANY)


def has(limits, index):
    first, end = limits
    return (index >= first) & (index < end)


def plan(block_owner, orbital_counts):
    ids = jnp.arange(block_owner.shape[0], dtype=jnp.int32)
    same = block_owner[:, None] == block_owner[None, :]
    earlier = same & (ids[None, :] < ids[:, None])
    load = jnp.sum(jnp.where(same, orbital_counts[None, :], 0), axis=1)
    base = jnp.sum(jnp.where(earlier, orbital_counts[None, :], 0), axis=1)
    place = jnp.sum(earlier.astype(jnp.int32), axis=1)
    ahead = (load[None, :] > load[:, None]) | (
        (load[None, :] == load[:, None]) & (block_owner[None, :] < block_owner[:, None])
    )
    rank = jnp.sum((ahead & (place == 0)[None, :]).astype(jnp.int32), axis=1)
    second = rank >= BINS
    bin_of = jnp.where(second, 2 * BINS - 1 - rank, rank)
    ahead_load = jnp.sum(
        jnp.where(
            (place == 0)[None, :] & (rank[None, :] == 2 * BINS - 1 - rank[:, None]), load[None, :], 0
        ),
        axis=1,
    )
    room = jnp.zeros_like(load)
    for group, limits in enumerate(LIMITS):
        room = room + jnp.where(second == (group >= PART_A), has(limits, bin_of) * GROUP, 0)
    sent = sum(has(limits, bin_of) * number for first, number, limits in STREAMS)
    fits = jnp.all((load <= room) & (load + ahead_load <= sent))
    return bin_of, base, jnp.where(second, ahead_load, 0), load, place, second, fits


def position():
    z = lax.axis_index("grp")
    aux = lax.axis_index("aux")
    core = lax.rem(aux, 2)
    x = lax.rem(aux // 2, SIDE)
    y = aux // (2 * SIDE)
    return x, y, z, core


def device(x, y, z, core):
    return (z, (y * SIDE + x) * 2 + core)


def bin_index(x, y, z, core):
    kind = lax.rem(x, 2) + 2 * lax.rem(y, 2) + 4 * lax.rem(z, 2)
    return kind + core * (BINS - 1 - 2 * kind)


def part_index(x, y, z):
    return x // 2 + 2 * (y // 2) + 4 * (z // 2)


def shifted(value, by):
    return lax.rem(value + by + SIDE, SIDE)


def kernel(
    origin_ref,
    offset_ref,
    place_ref,
    block_ref,
    source,
    row_energy,
    column_energy,
    mask,
    out,
    whole,
    packed,
    held,
    tiles,
    parts_1,
    parts_2,
    parts_3,
    exact,
    exact_parts,
    stack,
    row_sums,
    slot_sums,
    fold,
    chunks,
    chunk_parts,
    dense,
    homes,
    load_sem,
    local_sem,
    send_sem,
    recv_sem,
    tile_send,
    tile_recv,
    exact_send,
    exact_recv,
    chunk_send,
    chunk_recv,
    home_send,
    home_recv,
):
    x, y, z, core = position()
    aux = lax.axis_index("aux")
    owners = lax.axis_size("aux")
    sign = 1 - 2 * core
    own_bin = bin_index(x, y, z, core)
    own_part = part_index(x, y, z)
    quarter = lax.rem(own_part, SIDE)
    half = own_part // SIDE

    pieces = load_sem.shape[0]
    size = source.shape[0] // pieces

    def load(piece):
        part = pl.ds(piece * size, size)
        return pltpu.make_async_copy(source.at[part], whole.at[part], load_sem.at[piece])

    for piece in range(pieces):
        load(piece).start()

    barrier = pltpu.get_barrier_semaphore()

    def greet(target):
        pl.semaphore_signal(barrier, inc=1, device_id=target, device_id_type=MESH)

    greet(device(x, y, z, 1 - core))
    for d in range(1, 8):
        dx, dy, dz = BITS[d]
        greet(device(shifted(x, -dx), shifted(y, -dy), shifted(z, -dz), 0))
        greet(device(shifted(x, dx), shifted(y, dy), shifted(z, dz), 1))
        greet(device(shifted(x, 2 * dx), shifted(y, 2 * dy), shifted(z, 2 * dz), core))

    def feeder(index):
        number = index // 2
        feed_core = number // 8
        kind = number + feed_core * (BINS - 1 - 2 * number)
        return (
            lax.rem(kind, 2) + 2 * lax.rem(z, 2),
            lax.rem(kind // 2, 2) + 2 * (z // 2),
            kind // 4 + 2 * lax.rem(index, 2),
            feed_core,
        )

    own_feed = own_bin * 2 + half

    @pl.loop(0, owners)
    def _(index):
        @pl.when((quarter != z) | (index != own_feed))
        def _():
            greet(device(*feeder(index)))

    fold[...] = (
        lax.rem(lax.broadcasted_iota(jnp.int32, (ROWS, NV), 0), NV)
        == lax.broadcasted_iota(jnp.int32, (ROWS, NV), 1)
    ).astype(jnp.float32)
    slot_sums[...] = jnp.zeros_like(slot_sums)
    row_sums[...] = jnp.zeros_like(row_sums)
    chunks[...] = jnp.zeros_like(chunks)

    for piece in range(pieces):
        load(piece).wait()
    pl.semaphore_wait(barrier, 22 + owners - (quarter == z).astype(jnp.int32))

    def when(limits, index, act):
        if limits == ALL:
            act()
        else:
            pl.when(has(limits, index))(act)

    def slots(stream):
        first, number, limits = STREAMS[stream]
        return pl.ds(first, number)

    def gather(d, target_core, stream, act):
        dx, dy, dz = BITS[d]
        tx, ty, tz = shifted(x, sign * dx), shifted(y, sign * dy), shifted(z, sign * dz)
        target_bin = bin_index(tx, ty, tz, target_core)
        copy = pltpu.make_async_remote_copy(
            src_ref=packed.at[target_bin, slots(stream)],
            dst_ref=held.at[2 * d + core, slots(stream)],
            send_sem=send_sem.at[2 * d + target_core, stream],
            recv_sem=recv_sem.at[2 * d + core, stream],
            device_id=device(tx, ty, tz, target_core),
            device_id_type=MESH,
        )
        when(STREAMS[stream][2], target_bin, lambda: act(copy))

    def keep(stream):
        return pltpu.make_async_copy(
            packed.at[own_bin, slots(stream)], held.at[core, slots(stream)], local_sem.at[stream]
        )

    for stream, (first_slot, number_of_slots, limits) in enumerate(STREAMS):

        @pl.loop(0, BINS)
        def _(number):
            for slot in range(first_slot, first_slot + number_of_slots):
                origin = origin_ref[number * SENT + slot]
                packed[number, slot] = whole[origin]

        for d in range(7, 0, -1):
            for target_core in range(2):
                gather(d, target_core, stream, lambda copy: copy.start())
        gather(0, 1 - core, stream, lambda copy: copy.start())
        when(limits, own_bin, lambda: keep(stream).start())

    def arrived(stream):
        def wait_all():
            keep(stream).wait()
            for sender in range(2, BINS):
                part = held.at[sender, slots(stream)]
                pltpu.make_async_copy(part, part, recv_sem.at[sender, stream]).wait()
            part = held.at[1 - core, slots(stream)]
            pltpu.make_async_copy(part, part, recv_sem.at[1 - core, stream]).wait()

        when(STREAMS[stream][2], own_bin, wait_all)

    def settle():
        offset = offset_ref[0]

        @pl.loop(0, BINS)
        def _(sender):
            for slot in range(PART_B * GROUP):
                held[sender, SENT + slot] = held[sender, offset + slot]

    def rows_of(base, group):
        first = group * GROUP + (SENT if base else 0)
        return jnp.concatenate(
            [
                held[sender, pl.ds(first, GROUP)].reshape(ROWS, held.shape[-1])
                for sender in range(BINS)
            ],
            axis=1,
        )

    def peer(e):
        dx, dy, dz = BITS[e]
        px, py, pz = shifted(x, 2 * dx), shifted(y, 2 * dy), shifted(z, 2 * dz)
        return part_index(px, py, pz), device(px, py, pz, core)

    bit = (x // 2, y // 2, z // 2)

    def view(fixed):
        return tuple(fixed.get(axis, slice(None)) for axis in (2, 1, 0))

    def step(unit, phase):
        column, first, number, order = UNITS[unit]
        fixed = {axis: bit[axis] for axis in order[:phase]}
        axis = order[phase]
        fixed[axis] = 1 - bit[axis]
        run = pl.ds(first, number)
        far = [shifted(c, 2 * (axis == k)) for k, c in enumerate((x, y, z))]
        landing = (parts_1.at[:, :, run], parts_2.at[:, run], parts_3.at[run])[phase]
        return pltpu.make_async_remote_copy(
            src_ref=tiles.at[view(fixed) + (run,)],
            dst_ref=landing,
            send_sem=tile_send.at[unit, phase],
            recv_sem=tile_recv.at[unit, phase],
            device_id=device(*far, core),
            device_id_type=MESH,
        )

    def units_of(column):
        return [unit for unit in range(len(UNITS)) if UNITS[unit][0] == column]

    def merge(column, phase):
        for unit in units_of(column):
            _, first, number, order = UNITS[unit]
            step(unit, phase).wait_recv()
            fixed = {axis: bit[axis] for axis in order[: phase + 1]}
            rest = [axis for axis in (2, 1, 0) if axis not in fixed]
            landed = (parts_1, parts_2)[phase]

            @pl.loop(first, first + number)
            def _(index):
                for choice in range(2 ** len(rest)):
                    at = tuple((choice // 2**k) % 2 for k in range(len(rest)))
                    place = view({**fixed, **dict(zip(rest, at))}) + (index,)
                    tiles[place] = (
                        tiles[place].astype(jnp.float32) + landed[at + (index,)].astype(jnp.float32)
                    ).astype(jnp.bfloat16)

            step(unit, phase + 1).start()

    def scatter_exact(e, column):
        part, target = peer(e)
        return pltpu.make_async_remote_copy(
            src_ref=exact.at[column],
            dst_ref=exact_parts.at[e - 1, column],
            send_sem=exact_send.at[e - 1, column],
            recv_sem=exact_recv.at[e - 1, column],
            device_id=target,
            device_id_type=MESH,
        )

    row_number = lax.broadcasted_iota(jnp.int32, (ROWS, ROWS), 0)
    column_number = lax.broadcasted_iota(jnp.int32, (ROWS, ROWS), 1)

    def make_column(column):
        base, v, first = COLUMNS[column]

        @pl.loop(0, v + 1)
        def _(u):
            tile = lax.dot_general(
                rows_of(base, u),
                rows_of(base, v),
                (((1,), (1,)), ((), ())),
                preferred_element_type=jnp.float32,
            )

            @pl.when(u == v)
            def _():
                diagonal = jnp.where(row_number == column_number, tile, 0.0)
                exact[column] = jnp.broadcast_to(
                    jnp.sum(diagonal, axis=0, keepdims=True), exact.shape[1:]
                )

            rounded = tile.astype(jnp.bfloat16)
            for part in range(8):
                tiles[part // 4, (part // 2) % 2, part % 2, first + u] = rounded[
                    part * NV : (part + 1) * NV
                ]

        for unit in units_of(column):
            step(unit, 0).start()
        for e in range(7, 0, -1):
            scatter_exact(e, column).start()

    own_diagonal = (
        lax.broadcasted_iota(jnp.int32, (NV, ROWS), 0) + own_part * NV
        == lax.broadcasted_iota(jnp.int32, (NV, ROWS), 1)
    )

    def add_column(column):
        base, v, first = COLUMNS[column]
        for unit in units_of(column):
            step(unit, 2).wait_recv()
        for e in range(1, 8):
            scatter_exact(e, column).wait_recv()
        diagonal = exact[column]
        for e in range(7):
            diagonal = diagonal + exact_parts[e, column]

        @pl.loop(0, v + 1)
        def _(u):
            integral = tiles[bit[2], bit[1], bit[0], first + u].astype(jnp.float32) + parts_3[
                first + u
            ].astype(jnp.float32)
            integral = jnp.where(own_diagonal & (u == v), diagonal[:1], integral)
            kind = mask[base + u, base + v]
            quotient = integral / (row_energy[base + u] + column_energy[base + v])
            amplitude = jnp.where(kind > 0, quotient, 0.0).astype(jnp.bfloat16)
            row_sums[base + u] = row_sums[base + u] + lax.dot_general(
                amplitude, amplitude, (((1,), (1,)), ((), ())), preferred_element_type=jnp.float32
            )
            stack[pl.ds(pl.multiple_of(u * NV, NV), NV), :] = jnp.where(
                kind > 1, quotient, 0.0
            ).astype(jnp.bfloat16)

        stacked = stack[: (v + 1) * NV, :]
        product = lax.dot_general(
            stacked, stacked, (((0,), (0,)), ((), ())), preferred_element_type=jnp.float32
        )
        slot_sums[(base + v) * ROWS : (base + v + 1) * ROWS, :] = jnp.dot(
            jnp.where(row_number // NV == column_number // NV, product, 0.0),
            fold[...],
            precision=lax.Precision.HIGHEST,
            preferred_element_type=jnp.float32,
        )

    def advance(column, phase):
        if column < 0 or column >= GROUPS:
            return
        act = (
            lambda: make_column(column),
            lambda: merge(column, 0),
            lambda: merge(column, 1),
            lambda: add_column(column),
        )[phase]
        when(LIMITS[column], own_bin, act)

    for column in range(GROUPS + 3):
        for stream in ((column,) if column < 5 else (5, 6) if column == 5 else (7,) if column == 6 else ()):
            arrived(stream)
        if column == PART_A:
            settle()
        for phase in range(4):
            advance(column - phase, phase)
    for group in range(GROUPS):
        part = pl.ds(pl.multiple_of(group * ROWS + own_part * NV, NV), NV)
        slot_sums[part, :] = slot_sums[part, :] + row_sums[group]

    for side in range(2):
        first_slot = side * PART_A * GROUP

        def add_slot(step, sums):
            slot = first_slot + step
            value = slot_sums[pl.ds(pl.multiple_of(slot * NV, NV), NV), :]
            number = place_ref[slot]
            return tuple(
                sums[i] + jnp.where(number == i, value, jnp.zeros_like(value)) for i in range(3)
            )

        zero = jnp.zeros((NV, NV), jnp.float32)
        sums = lax.fori_loop(0, (PART_A, PART_B)[side] * GROUP, add_slot, (zero, zero, zero))
        width = NV // SIDE
        for i in range(3):
            for g in range(SIDE):
                chunks[side * SIDE + g, i * CHUNK : i * CHUNK + width, :NV] = sums[i][
                    g * width : (g + 1) * width
                ]

    def scatter_chunk(e):
        part, target = peer(e)
        return pltpu.make_async_remote_copy(
            src_ref=chunks.at[part],
            dst_ref=chunk_parts.at[e - 1],
            send_sem=chunk_send.at[e - 1],
            recv_sem=chunk_recv.at[e - 1],
            device_id=target,
            device_id_type=MESH,
        )

    for e in range(7, 0, -1):
        scatter_chunk(e).start()
    for e in range(1, 8):
        scatter_chunk(e).wait_recv()
    total = chunks[own_part]
    for e in range(7):
        total = total + chunk_parts[e]
    pieces = [total[i * CHUNK : (i + 1) * CHUNK] for i in range(3)]
    turned = [pltpu.roll(piece, 64, 1) for piece in pieces]

    def send_home(target):
        return pltpu.make_async_remote_copy(
            src_ref=dense.at[target],
            dst_ref=homes.at[own_feed],
            send_sem=home_send.at[target],
            recv_sem=home_recv.at[own_feed],
            device_id=(quarter, target),
            device_id_type=MESH,
        )

    def away(target):
        return (quarter != z) | (target != aux)

    @pl.loop(0, owners)
    def _(target):
        message = jnp.zeros((CHUNK, 128), jnp.float32)
        for i in range(3):
            block = block_ref[i]
            message = message + jnp.where(block == 2 * target, pieces[i], 0.0)
            message = message + jnp.where(block == 2 * target + 1, turned[i], 0.0)
        dense[target] = message

        @pl.when(away(target))
        def _():
            send_home(target).start()

    @pl.when(quarter == z)
    def _():
        homes[own_feed] = dense[aux]

    @pl.loop(0, owners)
    def _(index):
        @pl.when((quarter != z) | (index != own_feed))
        def _():
            pltpu.make_async_copy(homes.at[index], homes.at[index], home_recv.at[index]).wait()

    out[...] = jnp.sum(homes[...], axis=0)

    @pl.loop(0, owners)
    def _(target):
        @pl.when(away(target))
        def _():
            send_home(target).wait_send()

    for e in range(1, 8):
        scatter_chunk(e).wait_send()

    def sent_column(column):
        for unit in units_of(column):
            for phase in range(3):
                step(unit, phase).wait_send()
        for e in range(1, 8):
            scatter_exact(e, column).wait_send()

    for column in range(GROUPS):
        when(LIMITS[column], own_bin, lambda: sent_column(column))
    for stream in range(len(STREAMS)):
        gather(0, 1 - core, stream, lambda copy: copy.wait_send())
        for d in range(1, 8):
            for target_core in range(2):
                gather(d, target_core, stream, lambda copy: copy.wait_send())


def binned(
    bin_of,
    base,
    offset,
    load,
    place,
    second,
    three_index,
    block_owner,
    pair_screen,
    orbital_counts,
    occupied_energy,
    virtual_energy,
):
    blocks, row_count, aux_local = three_index.shape
    block_ids = jnp.arange(blocks, dtype=jnp.int32)
    start = base + jnp.where(second, PART_A * GROUP, 0)
    sent_ids = jnp.arange(SENT, dtype=jnp.int32)[:, None] - (base + offset)[None, :]
    slot_ids = jnp.arange(SLOTS, dtype=jnp.int32)
    within = (start[None, :] <= slot_ids[:, None]) & (
        slot_ids[:, None] < (start + orbital_counts)[None, :]
    )
    orbital = slot_ids[:, None] - start[None, :]
    bins = jnp.arange(BINS, dtype=jnp.int32)
    origin = jnp.sum(
        jnp.where(
            (bin_of[None, None, :] == bins[:, None, None])
            & ((sent_ids >= 0) & (sent_ids < orbital_counts[None, :]))[None],
            (block_ids[None, :] * OB + sent_ids)[None],
            0,
        ),
        axis=2,
    )
    x, y, z, core = position()
    own_bin = bin_index(x, y, z, core)
    own_part = part_index(x, y, z)
    own_offset = jnp.sum(jnp.where((bin_of == own_bin) & (place == 0) & ~second, load, 0))
    inside = (bin_of[None, :] == own_bin) & within
    pick = inside.astype(jnp.float32)
    slot_place = jnp.sum(jnp.where(inside, place[None, :] + 1, 0), axis=1) - 1
    here = (bin_of == own_bin) & (second == (own_part >= SIDE))
    chunk_block = (
        jnp.sum(
            jnp.where(
                here[None, :] & (place[None, :] == jnp.arange(3, dtype=jnp.int32)[:, None]),
                block_ids[None, :] + 1,
                0,
            ),
            axis=1,
        )
        - 1
    )
    occupied = jnp.sum(
        jnp.where(
            inside[:, :, None] & (orbital[:, :, None] == jnp.arange(OB, dtype=jnp.int32)),
            occupied_energy[None],
            0.0,
        ),
        axis=(1, 2),
    )
    energy = (
        jnp.sum(jnp.where(inside[:, :, None], virtual_energy[None], 0.0), axis=1) - occupied[:, None]
    )
    row_pick = lax.dynamic_index_in_dim(pick.reshape(GROUPS, GROUP, blocks), own_part, 1, False)
    row_energy = lax.dynamic_index_in_dim(energy.reshape(GROUPS, GROUP, NV), own_part, 1, False)
    screen = (pair_screen == 1).astype(jnp.float32)
    live = jnp.dot(jnp.dot(row_pick, screen), pick.T)
    row_ids = jnp.arange(GROUPS, dtype=jnp.int32) * GROUP + own_part
    kind = jnp.where(
        live > 0.5,
        jnp.where(row_ids[:, None] < slot_ids, 2.0, jnp.where(row_ids[:, None] == slot_ids, 1.0, 0.0)),
        0.0,
    )
    kind = jnp.broadcast_to(kind.reshape(GROUPS, GROUPS, 1, GROUP, 1), (GROUPS, GROUPS, 1, GROUP, NV))
    owners = lax.axis_size("aux")
    home = pl.pallas_call(
        kernel,
        out_shape=jax.ShapeDtypeStruct((CHUNK, 128), jnp.float32),
        in_specs=[SMEM, SMEM, SMEM, SMEM, ANY, VMEM, VMEM, VMEM],
        out_specs=VMEM,
        scratch_shapes=[
            pltpu.VMEM((blocks * OB, NV, aux_local), jnp.bfloat16),
            pltpu.VMEM((BINS, SENT, NV, aux_local), jnp.bfloat16),
            pltpu.VMEM((BINS, SENT + PART_B * GROUP, NV, aux_local), jnp.bfloat16),
            pltpu.VMEM((2, 2, 2, TILES, NV, ROWS), jnp.bfloat16),
            pltpu.VMEM((2, 2, TILES, NV, ROWS), jnp.bfloat16),
            pltpu.VMEM((2, TILES, NV, ROWS), jnp.bfloat16),
            pltpu.VMEM((TILES, NV, ROWS), jnp.bfloat16),
            pltpu.VMEM((GROUPS, 8, ROWS), jnp.float32),
            pltpu.VMEM((7, GROUPS, 8, ROWS), jnp.float32),
            pltpu.VMEM((PART_A * NV, ROWS), jnp.bfloat16),
            pltpu.VMEM((GROUPS, NV, NV), jnp.float32),
            pltpu.VMEM((SLOTS * NV, NV), jnp.float32),
            pltpu.VMEM((ROWS, NV), jnp.float32),
            pltpu.VMEM((8, 3 * CHUNK, 128), jnp.float32),
            pltpu.VMEM((7, 3 * CHUNK, 128), jnp.float32),
            pltpu.VMEM((owners, CHUNK, 128), jnp.float32),
            pltpu.VMEM((owners, CHUNK, 128), jnp.float32),
            pltpu.SemaphoreType.DMA((8,)),
            pltpu.SemaphoreType.DMA((len(STREAMS),)),
            pltpu.SemaphoreType.DMA((BINS, len(STREAMS))),
            pltpu.SemaphoreType.DMA((BINS, len(STREAMS))),
            pltpu.SemaphoreType.DMA((len(UNITS), 3)),
            pltpu.SemaphoreType.DMA((len(UNITS), 3)),
            pltpu.SemaphoreType.DMA((7, GROUPS)),
            pltpu.SemaphoreType.DMA((7, GROUPS)),
            pltpu.SemaphoreType.DMA((7,)),
            pltpu.SemaphoreType.DMA((7,)),
            pltpu.SemaphoreType.DMA((owners,)),
            pltpu.SemaphoreType.DMA((owners,)),
        ],
        compiler_params=pltpu.CompilerParams(
            collective_id=0, has_side_effects=True, vmem_limit_bytes=60 * 2**20
        ),
    )(
        origin.reshape(-1),
        own_offset.reshape(1),
        slot_place,
        chunk_block,
        three_index.reshape(blocks * OB, NV, aux_local),
        row_energy.reshape(GROUPS, NV, 1),
        energy.reshape(GROUPS, 1, ROWS),
        kind.reshape(GROUPS, GROUPS, 1, ROWS),
    )
    return home.reshape(CHUNK, 2, 64)[: NV // SIDE, :, :NV].transpose(1, 0, 2)


def local(three_index, block_owner, pair_screen, orbital_counts, occupied_energy, virtual_energy):
    *spots, fits = plan(block_owner, orbital_counts)
    arguments = (
        three_index,
        block_owner,
        pair_screen,
        orbital_counts,
        occupied_energy,
        virtual_energy,
    )
    return lax.cond(
        fits,
        lambda: binned(*spots, *arguments),
        lambda: general(*arguments),
    )


def solution(mesh):
    in_specs = (P(None, None, ("grp", "aux")), P(), P(), P(), P(), P())
    out_specs = P("aux", "grp", None)
    return jax.shard_map(local, mesh=mesh, in_specs=in_specs, out_specs=out_specs, check_vma=False)
```

```python
import jax
import jax.numpy as jnp
from jax import lax
from jax.experimental import pallas as pl
from jax.experimental.pallas import tpu as pltpu
from jax.sharding import PartitionSpec as P

CAP = 3


def slot_tiles(source, slot_block, slot_valid, owners):
    picked = jnp.take(source, slot_block.reshape(-1), axis=0)
    picked = picked.reshape(owners, CAP, source.shape[1], source.shape[2])
    return jnp.where(slot_valid[:, :, None, None] > 0, picked, jnp.zeros_like(picked))


def pair_block(received, first, second):
    return lax.dot_general(
        received[:, first],
        received[:, second],
        (((0, 2), (0, 2)), ((), ())),
        preferred_element_type=jnp.float32,
    )


def general(three_index, block_owner, pair_screen, orbital_counts, occupied_energy, virtual_energy):
    block_count, row_count, aux_local = three_index.shape
    occupied_width = occupied_energy.shape[1]
    virtual_width = virtual_energy.shape[1]
    groups = lax.axis_size("grp")
    owners = lax.axis_size("aux")
    own_index = lax.axis_index("aux")
    group_index = lax.axis_index("grp")
    quarter = row_count // groups
    owner_ids = jnp.arange(owners, dtype=jnp.int32)
    owned = (block_owner[None, :] == owner_ids[:, None]).astype(jnp.int32)
    slot_rank = jnp.cumsum(owned, axis=1) - 1
    slot_ids = jnp.arange(CAP, dtype=jnp.int32)
    selection = owned[:, None, :] * (slot_rank[:, None, :] == slot_ids[None, :, None]).astype(
        jnp.int32
    )
    block_ids = jnp.arange(block_count, dtype=jnp.int32)
    slot_block = jnp.sum(selection * block_ids[None, None, :], axis=2)
    slot_valid = jnp.sum(selection, axis=2)
    mine = lax.dynamic_index_in_dim(selection, own_index, 0, keepdims=False)
    my_block = jnp.sum(mine * block_ids[None, :], axis=1)
    my_valid = jnp.sum(mine, axis=1)
    energy = (virtual_energy[:, None, :] - occupied_energy[:, :, None]).reshape(
        block_count, row_count
    )
    occupied_flags = (
        jnp.arange(occupied_width, dtype=jnp.int32)[None, :] < orbital_counts[:, None]
    ).astype(jnp.float32)
    occupancy = jnp.repeat(occupied_flags, virtual_width, axis=1)
    slot_energy = jnp.take(energy, my_block, axis=0)
    slot_occupancy = jnp.take(occupancy, my_block, axis=0)
    screened = jnp.take(jnp.take(pair_screen, my_block, axis=0), my_block, axis=1)
    is_live = screened * my_valid[:, None] * my_valid[None, :] > 0

    def slot_amplitude(integral, first, second):
        energy_rows = lax.dynamic_slice_in_dim(slot_energy[first], group_index * quarter, quarter)
        occupied_rows = lax.dynamic_slice_in_dim(
            slot_occupancy[first], group_index * quarter, quarter
        )
        divisor = energy_rows[:, None] + slot_energy[second][None, :]
        return (
            occupied_rows[:, None] * slot_occupancy[second][None, :] * integral / divisor
        ).astype(jnp.bfloat16)

    def own_density(amplitude):
        row_form = amplitude.reshape(quarter // virtual_width, virtual_width, row_count)
        return jnp.einsum("iax,ibx->ab", row_form, row_form, preferred_element_type=jnp.float32)

    outgoing = slot_tiles(three_index, slot_block, slot_valid, owners)
    received = lax.all_to_all(outgoing, "aux", split_axis=0, concat_axis=0, tiled=True)
    zero_block = jnp.zeros((row_count, row_count), jnp.float32)
    empty = jnp.zeros((virtual_width, virtual_width), jnp.float32)
    pair_keys = [(first, second) for first in range(CAP) for second in range(first, CAP)]
    uppers = []
    for first, second in pair_keys:
        uppers.append(
            lax.cond(
                is_live[first, second],
                lambda first=first, second=second: pair_block(received, first, second),
                lambda: zero_block,
            )
        )
    slot_parts = [empty for first in range(CAP)]
    blocks = [[zero_block for second in range(CAP)] for first in range(CAP)]
    for index, (first, second) in enumerate(pair_keys):
        blocks[first][second] = uppers[index]
        blocks[second][first] = uppers[index].T
    stacked = jnp.stack([jnp.stack(line) for line in blocks])
    sent = stacked.reshape(CAP, CAP, groups, quarter, row_count)
    summed = jnp.sum(lax.all_to_all(sent, "grp", 2, 2, tiled=True), axis=2)
    for first in range(CAP):
        for second in range(CAP):

            def one_part(first=first, second=second):
                return own_density(slot_amplitude(summed[first, second], first, second))

            slot_parts[first] = slot_parts[first] + lax.cond(
                is_live[first, second], one_part, lambda: empty
            )
    spread = jnp.stack(slot_parts).reshape(CAP, groups, virtual_width // groups, virtual_width)
    placed = jnp.einsum(
        "cb,cgxy->gbxy", mine.astype(jnp.float32), spread, precision=lax.Precision.HIGHEST
    )
    placed = placed.reshape(groups, owners, block_count // owners, virtual_width // groups, virtual_width)
    placed = jnp.sum(lax.all_to_all(placed, "grp", 0, 0, tiled=True), axis=0)
    return jnp.sum(lax.all_to_all(placed, "aux", 0, 0, tiled=True), axis=0)


NV = 48
OB = 16
BINS = 16
GROUP = 8
ROWS = GROUP * NV
SIDE = 4
PART_A = 6
PART_B = 2
GROUPS = PART_A + PART_B
SLOTS = GROUPS * GROUP
CHUNK = 16
ALL = (0, BINS)
LIMITS = (ALL, ALL, ALL, (0, 15), (0, 9), (0, 4), ALL, (2, BINS))
STREAMS = tuple((GROUP * k, GROUP, ALL) for k in range(5)) + (
    (40, 4, ALL),
    (44, 4, (0, 8)),
    (48, 4, (0, 4)),
)
SENT = 52
COLUMNS = tuple(
    [(0, v, v * (v + 1) // 2) for v in range(PART_A)]
    + [(PART_A, v, PART_A * (PART_A + 1) // 2 + v * (v + 1) // 2) for v in range(PART_B)]
)
TILES = PART_A * (PART_A + 1) // 2 + PART_B * (PART_B + 1) // 2
UNITS = []
for column, (base, v, first) in enumerate(COLUMNS):
    for skip in range(0, v + 1, 2):
        turn = len(UNITS) % 3
        UNITS.append(
            (column, first + skip, min(2, v + 1 - skip), (turn, (turn + 1) % 3, (turn + 2) % 3))
        )
BITS = [(d % 2, (d // 2) % 2, d // 4) for d in range(8)]
MESH = pl.DeviceIdType.MESH
VMEM = pl.BlockSpec(memory_space=pltpu.VMEM)
SMEM = pl.BlockSpec(memory_space=pltpu.SMEM)
ANY = pl.BlockSpec(memory_space=pl.ANY)


def has(limits, index):
    first, end = limits
    return (index >= first) & (index < end)


def plan(block_owner, orbital_counts):
    ids = jnp.arange(block_owner.shape[0], dtype=jnp.int32)
    same = block_owner[:, None] == block_owner[None, :]
    earlier = same & (ids[None, :] < ids[:, None])
    load = jnp.sum(jnp.where(same, orbital_counts[None, :], 0), axis=1)
    base = jnp.sum(jnp.where(earlier, orbital_counts[None, :], 0), axis=1)
    place = jnp.sum(earlier.astype(jnp.int32), axis=1)
    ahead = (load[None, :] > load[:, None]) | (
        (load[None, :] == load[:, None]) & (block_owner[None, :] < block_owner[:, None])
    )
    rank = jnp.sum((ahead & (place == 0)[None, :]).astype(jnp.int32), axis=1)
    second = rank >= BINS
    bin_of = jnp.where(second, 2 * BINS - 1 - rank, rank)
    ahead_load = jnp.sum(
        jnp.where(
            (place == 0)[None, :] & (rank[None, :] == 2 * BINS - 1 - rank[:, None]), load[None, :], 0
        ),
        axis=1,
    )
    room = jnp.zeros_like(load)
    for group, limits in enumerate(LIMITS):
        room = room + jnp.where(second == (group >= PART_A), has(limits, bin_of) * GROUP, 0)
    sent = sum(has(limits, bin_of) * number for first, number, limits in STREAMS)
    fits = jnp.all((load <= room) & (load + ahead_load <= sent))
    return bin_of, base, jnp.where(second, ahead_load, 0), load, place, second, fits


def position():
    z = lax.axis_index("grp")
    aux = lax.axis_index("aux")
    core = lax.rem(aux, 2)
    x = lax.rem(aux // 2, SIDE)
    y = aux // (2 * SIDE)
    return x, y, z, core


def device(x, y, z, core):
    return (z, (y * SIDE + x) * 2 + core)


def bin_index(x, y, z, core):
    kind = lax.rem(x, 2) + 2 * lax.rem(y, 2) + 4 * lax.rem(z, 2)
    return kind + core * (BINS - 1 - 2 * kind)


def part_index(x, y, z):
    return x // 2 + 2 * (y // 2) + 4 * (z // 2)


def shifted(value, by):
    return lax.rem(value + by + SIDE, SIDE)


def kernel(
    origin_ref,
    meta_ref,
    source,
    meta,
    screen,
    occupied_energy,
    virtual_energy,
    out,
    whole,
    packed,
    held,
    tiles,
    parts_1,
    parts_2,
    parts_3,
    exact,
    exact_parts,
    stack,
    row_sums,
    slot_sums,
    fold,
    chunks,
    chunk_parts,
    dense,
    homes,
    row_energy,
    column_energy,
    mask,
    load_sem,
    local_sem,
    send_sem,
    recv_sem,
    tile_send,
    tile_recv,
    exact_send,
    exact_recv,
    chunk_send,
    chunk_recv,
    home_send,
    home_recv,
):
    x, y, z, core = position()
    aux = lax.axis_index("aux")
    owners = lax.axis_size("aux")
    sign = 1 - 2 * core
    own_bin = bin_index(x, y, z, core)
    own_part = part_index(x, y, z)
    quarter = lax.rem(own_part, SIDE)
    half = own_part // SIDE

    pieces = load_sem.shape[0]
    size = source.shape[0] // pieces

    def load(piece):
        part = pl.ds(piece * size, size)
        return pltpu.make_async_copy(source.at[part], whole.at[part], load_sem.at[piece])

    for piece in range(pieces):
        load(piece).start()

    barrier = pltpu.get_barrier_semaphore()

    def greet(target):
        pl.semaphore_signal(barrier, inc=1, device_id=target, device_id_type=MESH)

    greet(device(x, y, z, 1 - core))
    for d in range(1, 8):
        dx, dy, dz = BITS[d]
        greet(device(shifted(x, -dx), shifted(y, -dy), shifted(z, -dz), 0))
        greet(device(shifted(x, dx), shifted(y, dy), shifted(z, dz), 1))
        greet(device(shifted(x, 2 * dx), shifted(y, 2 * dy), shifted(z, 2 * dz), core))

    def feeder(index):
        number = index // 2
        feed_core = number // 8
        kind = number + feed_core * (BINS - 1 - 2 * number)
        return (
            lax.rem(kind, 2) + 2 * lax.rem(z, 2),
            lax.rem(kind // 2, 2) + 2 * (z // 2),
            kind // 4 + 2 * lax.rem(index, 2),
            feed_core,
        )

    own_feed = own_bin * 2 + half

    @pl.loop(0, owners)
    def _(index):
        @pl.when((quarter != z) | (index != own_feed))
        def _():
            greet(device(*feeder(index)))

    fold[...] = (
        lax.rem(lax.broadcasted_iota(jnp.int32, (ROWS, NV), 0), NV)
        == lax.broadcasted_iota(jnp.int32, (ROWS, NV), 1)
    ).astype(jnp.float32)
    slot_sums[...] = jnp.zeros_like(slot_sums)
    row_sums[...] = jnp.zeros_like(row_sums)
    chunks[...] = jnp.zeros_like(chunks)

    for piece in range(pieces):
        load(piece).wait()
    pl.semaphore_wait(barrier, 22 + owners - (quarter == z).astype(jnp.int32))

    def when(limits, index, act):
        if limits == ALL:
            act()
        else:
            pl.when(has(limits, index))(act)

    def slots(stream):
        first, number, limits = STREAMS[stream]
        return pl.ds(first, number)

    def gather(d, target_core, stream, act):
        dx, dy, dz = d % 2, (d // 2) % 2, d // 4
        tx, ty, tz = shifted(x, sign * dx), shifted(y, sign * dy), shifted(z, sign * dz)
        target_bin = bin_index(tx, ty, tz, target_core)
        copy = pltpu.make_async_remote_copy(
            src_ref=packed.at[target_bin, slots(stream)],
            dst_ref=held.at[2 * d + core, slots(stream)],
            send_sem=send_sem.at[2 * d + target_core, stream],
            recv_sem=recv_sem.at[2 * d + core, stream],
            device_id=device(tx, ty, tz, target_core),
            device_id_type=MESH,
        )
        when(STREAMS[stream][2], target_bin, lambda: act(copy))

    def keep(stream):
        return pltpu.make_async_copy(
            packed.at[own_bin, slots(stream)], held.at[core, slots(stream)], local_sem.at[stream]
        )

    for stream, (first_slot, number_of_slots, limits) in enumerate(STREAMS):

        @pl.loop(0, BINS)
        def _(number):
            for slot in range(first_slot, first_slot + number_of_slots):
                origin = origin_ref[number * SENT + slot]
                packed[number, slot] = whole[origin]

        @pl.loop(0, 14)
        def _(index):
            gather(7 - index // 2, lax.rem(index, 2), stream, lambda copy: copy.start())

        gather(0, 1 - core, stream, lambda copy: copy.start())
        when(limits, own_bin, lambda: keep(stream).start())

    def arrived(stream):
        def wait_all():
            keep(stream).wait()

            @pl.loop(2, BINS)
            def _(sender):
                part = held.at[sender, slots(stream)]
                pltpu.make_async_copy(part, part, recv_sem.at[sender, stream]).wait()

            part = held.at[1 - core, slots(stream)]
            pltpu.make_async_copy(part, part, recv_sem.at[1 - core, stream]).wait()

        when(STREAMS[stream][2], own_bin, wait_all)

    row_number = lax.broadcasted_iota(jnp.int32, (ROWS, ROWS), 0)
    column_number = lax.broadcasted_iota(jnp.int32, (ROWS, ROWS), 1)
    own_diagonal = (
        lax.broadcasted_iota(jnp.int32, (NV, ROWS), 0) + own_part * NV
        == lax.broadcasted_iota(jnp.int32, (NV, ROWS), 1)
    )
    same_slot = (
        lax.broadcasted_iota(jnp.int32, (GROUP, ROWS), 1) // NV
        == lax.broadcasted_iota(jnp.int32, (GROUP, ROWS), 0)
    )

    def exact_dot(left, right, axis=0):
        return lax.dot_general(
            left,
            right,
            (((1,), (axis,)), ((), ())),
            precision=lax.Precision.HIGHEST,
            preferred_element_type=jnp.float32,
        )

    blocks = meta.shape[1]
    slot_number = lax.broadcasted_iota(jnp.int32, (SLOTS, blocks), 0)
    orbital = slot_number - meta[1:2, :]
    inside = (meta[0:1, :] == own_bin) & (orbital >= 0) & (orbital < meta[2:3, :])
    pick = jnp.where(inside, 1.0, 0.0)
    slot_orbital = jnp.sum(jnp.where(inside, orbital, 0), axis=1, keepdims=True)
    occupied = exact_dot(pick, occupied_energy[...])
    occupied = jnp.where(
        lax.broadcasted_iota(jnp.int32, (SLOTS, OB), 1) == slot_orbital, occupied, 0.0
    )
    energy = exact_dot(pick, virtual_energy[...]) - jnp.sum(occupied, axis=1, keepdims=True)
    row_slot = lax.broadcasted_iota(jnp.int32, (GROUPS, SLOTS), 0) * GROUP + own_part
    column_slot = lax.broadcasted_iota(jnp.int32, (GROUPS, SLOTS), 1)
    row_pick = exact_dot(jnp.where(row_slot == column_slot, 1.0, 0.0), pick)
    live = exact_dot(exact_dot(row_pick, jnp.where(screen[...] == 1, 1.0, 0.0)), pick, 1)
    order = jnp.where(row_slot < column_slot, 2.0, jnp.where(row_slot == column_slot, 1.0, 0.0))
    kind = jnp.where(live > 0.5, order, 0.0)
    for group in range(GROUPS):
        lanes = exact_dot(energy[group * GROUP : (group + 1) * GROUP], fold[...], 1)
        lanes = jnp.sum(jnp.where(same_slot, lanes, 0.0), axis=0, keepdims=True)
        column_energy[group] = lanes
        row_energy[group] = jnp.sum(jnp.where(own_diagonal, lanes, 0.0), axis=1, keepdims=True)
        wide = lax.broadcasted_iota(jnp.int32, (SLOTS, ROWS), 0) == (
            group * GROUP + lax.broadcasted_iota(jnp.int32, (SLOTS, ROWS), 1) // NV
        )
        mask[group] = exact_dot(kind, jnp.where(wide, 1.0, 0.0))

    def find(block, found):
        result = []
        for index in range(6):
            hit = (
                (meta_ref[0, block] == own_bin)
                & (meta_ref[3, block] == index % 3)
                & (meta_ref[4, block] == index // 3)
            )
            old = found[3 * index : 3 * index + 3]
            new = (meta_ref[1, block], meta_ref[2, block], block)
            result += [jnp.where(hit, n, o) for n, o in zip(new, old)]
        return tuple(result)

    nothing = jnp.int32(0)
    found = lax.fori_loop(0, blocks, find, (nothing, nothing, jnp.int32(-1)) * 6)
    block_start, block_slots, block_id = found[0::3], found[1::3], found[2::3]

    def settle():
        offset = block_slots[0] + block_slots[1] + block_slots[2]

        @pl.loop(0, BINS)
        def _(sender):
            for slot in range(PART_B * GROUP):
                held[sender, SENT + slot] = held[sender, offset + slot]

    def rows_of(base, group):
        first = group * GROUP + (SENT if base else 0)
        return jnp.concatenate(
            [
                held[sender, pl.ds(first, GROUP)].reshape(ROWS, held.shape[-1])
                for sender in range(BINS)
            ],
            axis=1,
        )

    def peer(e):
        dx, dy, dz = BITS[e]
        px, py, pz = shifted(x, 2 * dx), shifted(y, 2 * dy), shifted(z, 2 * dz)
        return part_index(px, py, pz), device(px, py, pz, core)

    bit = (x // 2, y // 2, z // 2)

    def view(fixed):
        return tuple(fixed.get(axis, slice(None)) for axis in (2, 1, 0))

    def step(unit, phase):
        column, first, number, order = UNITS[unit]
        fixed = {axis: bit[axis] for axis in order[:phase]}
        axis = order[phase]
        fixed[axis] = 1 - bit[axis]
        run = pl.ds(first, number)
        far = [shifted(c, 2 * (axis == k)) for k, c in enumerate((x, y, z))]
        landing = (parts_1.at[:, :, run], parts_2.at[:, run], parts_3.at[run])[phase]
        return pltpu.make_async_remote_copy(
            src_ref=tiles.at[view(fixed) + (run,)],
            dst_ref=landing,
            send_sem=tile_send.at[unit, phase],
            recv_sem=tile_recv.at[unit, phase],
            device_id=device(*far, core),
            device_id_type=MESH,
        )

    def units_of(column):
        return [unit for unit in range(len(UNITS)) if UNITS[unit][0] == column]

    def merge(column, phase):
        for unit in units_of(column):
            _, first, number, order = UNITS[unit]
            step(unit, phase).wait_recv()
            fixed = {axis: bit[axis] for axis in order[: phase + 1]}
            rest = [axis for axis in (2, 1, 0) if axis not in fixed]
            landed = (parts_1, parts_2)[phase]

            @pl.loop(first, first + number)
            def _(index):
                for choice in range(2 ** len(rest)):
                    at = tuple((choice // 2**k) % 2 for k in range(len(rest)))
                    place = view({**fixed, **dict(zip(rest, at))}) + (index,)
                    tiles[place] = (
                        tiles[place].astype(jnp.float32) + landed[at + (index,)].astype(jnp.float32)
                    ).astype(jnp.bfloat16)

            step(unit, phase + 1).start()

    def scatter_exact(e, batch):
        part, target = peer(e)
        return pltpu.make_async_remote_copy(
            src_ref=exact.at[batch, part],
            dst_ref=exact_parts.at[e - 1, batch],
            send_sem=exact_send.at[e - 1, batch],
            recv_sem=exact_recv.at[e - 1, batch],
            device_id=target,
            device_id_type=MESH,
        )

    def make_column(column):
        base, v, first = COLUMNS[column]

        @pl.loop(0, v + 1)
        def _(u):
            tile = lax.dot_general(
                rows_of(base, u),
                rows_of(base, v),
                (((1,), (1,)), ((), ())),
                preferred_element_type=jnp.float32,
            )

            @pl.when(u == v)
            def _():
                diagonal = jnp.where(row_number == column_number, tile, 0.0)
                diagonal = jnp.where(same_slot, jnp.sum(diagonal, axis=0, keepdims=True), 0.0)
                diagonal = exact_dot(diagonal, fold[...])
                for part in range(8):
                    exact[column // 4, part, column % 4 : column % 4 + 1, :NV] = diagonal[
                        part : part + 1
                    ]

            rounded = tile.astype(jnp.bfloat16)
            for part in range(8):
                tiles[part // 4, (part // 2) % 2, part % 2, first + u] = rounded[
                    part * NV : (part + 1) * NV
                ]

        for unit in units_of(column):
            step(unit, 0).start()

    def add_column(column):
        base, v, first = COLUMNS[column]
        for unit in units_of(column):
            step(unit, 2).wait_recv()
        diagonal = exact[column // 4, own_part]
        for e in range(7):
            diagonal = diagonal + exact_parts[e, column // 4]
        diagonal = exact_dot(diagonal[:, :NV], fold[...], 1)[column % 4 : column % 4 + 1]

        @pl.loop(0, v + 1)
        def _(u):
            integral = tiles[bit[2], bit[1], bit[0], first + u].astype(jnp.float32) + parts_3[
                first + u
            ].astype(jnp.float32)
            integral = jnp.where(own_diagonal & (u == v), diagonal, integral)
            kind = mask[base + v, pl.ds(base + u, 1), :]
            quotient = integral / (row_energy[base + u] + column_energy[base + v])
            amplitude = jnp.where(kind > 0, quotient, 0.0).astype(jnp.bfloat16)
            row_sums[base + u] = row_sums[base + u] + lax.dot_general(
                amplitude, amplitude, (((1,), (1,)), ((), ())), preferred_element_type=jnp.float32
            )
            stack[pl.ds(pl.multiple_of(u * NV, NV), NV), :] = jnp.where(
                kind > 1, quotient, 0.0
            ).astype(jnp.bfloat16)

        stacked = stack[: (v + 1) * NV, :]
        product = lax.dot_general(
            stacked, stacked, (((0,), (0,)), ((), ())), preferred_element_type=jnp.float32
        )
        slot_sums[(base + v) * ROWS : (base + v + 1) * ROWS, :] = jnp.dot(
            jnp.where(row_number // NV == column_number // NV, product, 0.0),
            fold[...],
            precision=lax.Precision.HIGHEST,
            preferred_element_type=jnp.float32,
        )

    def advance(column, phase):
        if column < 0 or column >= GROUPS:
            return
        act = (
            lambda: make_column(column),
            lambda: merge(column, 0),
            lambda: merge(column, 1),
            lambda: add_column(column),
        )[phase]
        when(LIMITS[column], own_bin, act)

    for column in range(GROUPS + 3):
        for stream in ((column,) if column < 5 else (5, 6) if column == 5 else (7,) if column == 6 else ()):
            arrived(stream)
        if column == PART_A:
            settle()
        for phase in range(4):
            advance(column - phase, phase)
            if phase == 0 and column % 4 == 3 and column < GROUPS:
                for e in range(7, 0, -1):
                    scatter_exact(e, column // 4).start()
            if phase == 2 and column % 4 == 3 and column < GROUPS:
                for e in range(1, 8):
                    scatter_exact(e, column // 4).wait_recv()
    for group in range(GROUPS):
        part = pl.ds(pl.multiple_of(group * ROWS + own_part * NV, NV), NV)
        slot_sums[part, :] = slot_sums[part, :] + row_sums[group]

    for side in range(2):
        first_slot = side * PART_A * GROUP

        def add_slot(step, sums):
            slot = first_slot + step
            value = slot_sums[pl.ds(pl.multiple_of(slot * NV, NV), NV), :]
            result = []
            for i in range(3 * side, 3 * side + 3):
                own = (slot >= block_start[i]) & (slot < block_start[i] + block_slots[i])
                result.append(sums[i % 3] + jnp.where(own, value, jnp.zeros_like(value)))
            return tuple(result)

        zero = jnp.zeros((NV, NV), jnp.float32)
        sums = lax.fori_loop(0, (PART_A, PART_B)[side] * GROUP, add_slot, (zero, zero, zero))
        width = NV // SIDE
        for i in range(3):
            for g in range(SIDE):
                chunks[side * SIDE + g, i * CHUNK : i * CHUNK + width, :NV] = sums[i][
                    g * width : (g + 1) * width
                ]

    def scatter_chunk(e):
        part, target = peer(e)
        return pltpu.make_async_remote_copy(
            src_ref=chunks.at[part],
            dst_ref=chunk_parts.at[e - 1],
            send_sem=chunk_send.at[e - 1],
            recv_sem=chunk_recv.at[e - 1],
            device_id=target,
            device_id_type=MESH,
        )

    for e in range(7, 0, -1):
        scatter_chunk(e).start()
    for e in range(1, 8):
        scatter_chunk(e).wait_recv()
    total = chunks[own_part]
    for e in range(7):
        total = total + chunk_parts[e]
    pieces = [total[i * CHUNK : (i + 1) * CHUNK] for i in range(3)]
    turned = [pltpu.roll(piece, 64, 1) for piece in pieces]

    def send_home(target):
        return pltpu.make_async_remote_copy(
            src_ref=dense.at[target],
            dst_ref=homes.at[own_feed],
            send_sem=home_send.at[target],
            recv_sem=home_recv.at[own_feed],
            device_id=(quarter, target),
            device_id_type=MESH,
        )

    def away(target):
        return (quarter != z) | (target != aux)

    @pl.loop(0, owners)
    def _(target):
        message = jnp.zeros((CHUNK, 128), jnp.float32)
        for i in range(3):
            block = jnp.where(half == 0, block_id[i], block_id[3 + i])
            message = message + jnp.where(block == 2 * target, pieces[i], 0.0)
            message = message + jnp.where(block == 2 * target + 1, turned[i], 0.0)
        dense[target] = message

        @pl.when(away(target))
        def _():
            send_home(target).start()

    @pl.when(quarter == z)
    def _():
        homes[own_feed] = dense[aux]

    @pl.loop(0, owners)
    def _(index):
        @pl.when((quarter != z) | (index != own_feed))
        def _():
            pltpu.make_async_copy(homes.at[index], homes.at[index], home_recv.at[index]).wait()

    out[...] = jnp.sum(homes[...], axis=0)

    @pl.loop(0, owners)
    def _(target):
        @pl.when(away(target))
        def _():
            send_home(target).wait_send()

    for e in range(1, 8):
        scatter_chunk(e).wait_send()

    def sent_column(column):
        for unit in units_of(column):
            for phase in range(3):
                step(unit, phase).wait_send()

    for column in range(GROUPS):
        when(LIMITS[column], own_bin, lambda: sent_column(column))
    for batch in range(2):
        for e in range(1, 8):
            scatter_exact(e, batch).wait_send()
    for stream in range(len(STREAMS)):
        gather(0, 1 - core, stream, lambda copy: copy.wait_send())

        @pl.loop(2, BINS)
        def _(index):
            gather(index // 2, lax.rem(index, 2), stream, lambda copy: copy.wait_send())


def binned(
    bin_of,
    base,
    offset,
    load,
    place,
    second,
    three_index,
    block_owner,
    pair_screen,
    orbital_counts,
    occupied_energy,
    virtual_energy,
):
    blocks, row_count, aux_local = three_index.shape
    block_ids = jnp.arange(blocks, dtype=jnp.int32)
    sent_ids = jnp.arange(SENT, dtype=jnp.int32)[:, None] - (base + offset)[None, :]
    bins = jnp.arange(BINS, dtype=jnp.int32)
    origin = jnp.sum(
        jnp.where(
            (bin_of[None, None, :] == bins[:, None, None])
            & ((sent_ids >= 0) & (sent_ids < orbital_counts[None, :]))[None],
            (block_ids[None, :] * OB + sent_ids)[None],
            0,
        ),
        axis=2,
    )
    start = base + jnp.where(second, PART_A * GROUP, 0)
    meta = jnp.stack([bin_of, start, orbital_counts, place, second.astype(jnp.int32)] + [base] * 3)
    owners = lax.axis_size("aux")
    home = pl.pallas_call(
        kernel,
        out_shape=jax.ShapeDtypeStruct((CHUNK, 128), jnp.float32),
        in_specs=[SMEM, SMEM, ANY, VMEM, VMEM, VMEM, VMEM],
        out_specs=VMEM,
        scratch_shapes=[
            pltpu.VMEM((blocks * OB, NV, aux_local), jnp.bfloat16),
            pltpu.VMEM((BINS, SENT, NV, aux_local), jnp.bfloat16),
            pltpu.VMEM((BINS, SENT + PART_B * GROUP, NV, aux_local), jnp.bfloat16),
            pltpu.VMEM((2, 2, 2, TILES, NV, ROWS), jnp.bfloat16),
            pltpu.VMEM((2, 2, TILES, NV, ROWS), jnp.bfloat16),
            pltpu.VMEM((2, TILES, NV, ROWS), jnp.bfloat16),
            pltpu.VMEM((TILES, NV, ROWS), jnp.bfloat16),
            pltpu.VMEM((2, 8, 8, 128), jnp.float32),
            pltpu.VMEM((7, 2, 8, 128), jnp.float32),
            pltpu.VMEM((PART_A * NV, ROWS), jnp.bfloat16),
            pltpu.VMEM((GROUPS, NV, NV), jnp.float32),
            pltpu.VMEM((SLOTS * NV, NV), jnp.float32),
            pltpu.VMEM((ROWS, NV), jnp.float32),
            pltpu.VMEM((8, 3 * CHUNK, 128), jnp.float32),
            pltpu.VMEM((7, 3 * CHUNK, 128), jnp.float32),
            pltpu.VMEM((owners, CHUNK, 128), jnp.float32),
            pltpu.VMEM((owners, CHUNK, 128), jnp.float32),
            pltpu.VMEM((GROUPS, NV, 1), jnp.float32),
            pltpu.VMEM((GROUPS, 1, ROWS), jnp.float32),
            pltpu.VMEM((GROUPS, GROUPS, ROWS), jnp.float32),
            pltpu.SemaphoreType.DMA((8,)),
            pltpu.SemaphoreType.DMA((len(STREAMS),)),
            pltpu.SemaphoreType.DMA((BINS, len(STREAMS))),
            pltpu.SemaphoreType.DMA((BINS, len(STREAMS))),
            pltpu.SemaphoreType.DMA((len(UNITS), 3)),
            pltpu.SemaphoreType.DMA((len(UNITS), 3)),
            pltpu.SemaphoreType.DMA((7, 2)),
            pltpu.SemaphoreType.DMA((7, 2)),
            pltpu.SemaphoreType.DMA((7,)),
            pltpu.SemaphoreType.DMA((7,)),
            pltpu.SemaphoreType.DMA((owners,)),
            pltpu.SemaphoreType.DMA((owners,)),
        ],
        compiler_params=pltpu.CompilerParams(
            collective_id=0, has_side_effects=True, vmem_limit_bytes=60 * 2**20
        ),
    )(
        origin.reshape(-1),
        meta,
        three_index.reshape(blocks * OB, NV, aux_local),
        meta,
        pair_screen,
        occupied_energy,
        virtual_energy,
    )
    return home.reshape(CHUNK, 2, 64)[: NV // SIDE, :, :NV].transpose(1, 0, 2)


def local(three_index, block_owner, pair_screen, orbital_counts, occupied_energy, virtual_energy):
    *spots, fits = plan(block_owner, orbital_counts)
    arguments = (
        three_index,
        block_owner,
        pair_screen,
        orbital_counts,
        occupied_energy,
        virtual_energy,
    )
    return lax.cond(
        fits,
        lambda: binned(*spots, *arguments),
        lambda: general(*arguments),
    )


def solution(mesh):
    in_specs = (P(None, None, ("grp", "aux")), P(), P(), P(), P(), P())
    out_specs = P("aux", "grp", None)
    return jax.shard_map(local, mesh=mesh, in_specs=in_specs, out_specs=out_specs, check_vma=False)
```

```python
import jax
import jax.numpy as jnp
from jax import lax
from jax.experimental import pallas as pl
from jax.experimental.pallas import tpu as pltpu
from jax.sharding import PartitionSpec as P

CAP = 3


def slot_tiles(source, slot_block, slot_valid, owners):
    picked = jnp.take(source, slot_block.reshape(-1), axis=0)
    picked = picked.reshape(owners, CAP, source.shape[1], source.shape[2])
    return jnp.where(slot_valid[:, :, None, None] > 0, picked, jnp.zeros_like(picked))


def pair_block(received, first, second):
    return lax.dot_general(
        received[:, first],
        received[:, second],
        (((0, 2), (0, 2)), ((), ())),
        preferred_element_type=jnp.float32,
    )


def general(three_index, block_owner, pair_screen, orbital_counts, occupied_energy, virtual_energy):
    block_count, row_count, aux_local = three_index.shape
    occupied_width = occupied_energy.shape[1]
    virtual_width = virtual_energy.shape[1]
    groups = lax.axis_size("grp")
    owners = lax.axis_size("aux")
    own_index = lax.axis_index("aux")
    group_index = lax.axis_index("grp")
    quarter = row_count // groups
    owner_ids = jnp.arange(owners, dtype=jnp.int32)
    owned = (block_owner[None, :] == owner_ids[:, None]).astype(jnp.int32)
    slot_rank = jnp.cumsum(owned, axis=1) - 1
    slot_ids = jnp.arange(CAP, dtype=jnp.int32)
    selection = owned[:, None, :] * (slot_rank[:, None, :] == slot_ids[None, :, None]).astype(
        jnp.int32
    )
    block_ids = jnp.arange(block_count, dtype=jnp.int32)
    slot_block = jnp.sum(selection * block_ids[None, None, :], axis=2)
    slot_valid = jnp.sum(selection, axis=2)
    mine = lax.dynamic_index_in_dim(selection, own_index, 0, keepdims=False)
    my_block = jnp.sum(mine * block_ids[None, :], axis=1)
    my_valid = jnp.sum(mine, axis=1)
    energy = (virtual_energy[:, None, :] - occupied_energy[:, :, None]).reshape(
        block_count, row_count
    )
    occupied_flags = (
        jnp.arange(occupied_width, dtype=jnp.int32)[None, :] < orbital_counts[:, None]
    ).astype(jnp.float32)
    occupancy = jnp.repeat(occupied_flags, virtual_width, axis=1)
    slot_energy = jnp.take(energy, my_block, axis=0)
    slot_occupancy = jnp.take(occupancy, my_block, axis=0)
    screened = jnp.take(jnp.take(pair_screen, my_block, axis=0), my_block, axis=1)
    is_live = screened * my_valid[:, None] * my_valid[None, :] > 0

    def slot_amplitude(integral, first, second):
        energy_rows = lax.dynamic_slice_in_dim(slot_energy[first], group_index * quarter, quarter)
        occupied_rows = lax.dynamic_slice_in_dim(
            slot_occupancy[first], group_index * quarter, quarter
        )
        divisor = energy_rows[:, None] + slot_energy[second][None, :]
        return (
            occupied_rows[:, None] * slot_occupancy[second][None, :] * integral / divisor
        ).astype(jnp.bfloat16)

    def own_density(amplitude):
        row_form = amplitude.reshape(quarter // virtual_width, virtual_width, row_count)
        return jnp.einsum("iax,ibx->ab", row_form, row_form, preferred_element_type=jnp.float32)

    outgoing = slot_tiles(three_index, slot_block, slot_valid, owners)
    received = lax.all_to_all(outgoing, "aux", split_axis=0, concat_axis=0, tiled=True)
    zero_block = jnp.zeros((row_count, row_count), jnp.float32)
    empty = jnp.zeros((virtual_width, virtual_width), jnp.float32)
    pair_keys = [(first, second) for first in range(CAP) for second in range(first, CAP)]
    uppers = []
    for first, second in pair_keys:
        uppers.append(
            lax.cond(
                is_live[first, second],
                lambda first=first, second=second: pair_block(received, first, second),
                lambda: zero_block,
            )
        )
    slot_parts = [empty for first in range(CAP)]
    blocks = [[zero_block for second in range(CAP)] for first in range(CAP)]
    for index, (first, second) in enumerate(pair_keys):
        blocks[first][second] = uppers[index]
        blocks[second][first] = uppers[index].T
    stacked = jnp.stack([jnp.stack(line) for line in blocks])
    sent = stacked.reshape(CAP, CAP, groups, quarter, row_count)
    summed = jnp.sum(lax.all_to_all(sent, "grp", 2, 2, tiled=True), axis=2)
    for first in range(CAP):
        for second in range(CAP):

            def one_part(first=first, second=second):
                return own_density(slot_amplitude(summed[first, second], first, second))

            slot_parts[first] = slot_parts[first] + lax.cond(
                is_live[first, second], one_part, lambda: empty
            )
    spread = jnp.stack(slot_parts).reshape(CAP, groups, virtual_width // groups, virtual_width)
    placed = jnp.einsum(
        "cb,cgxy->gbxy", mine.astype(jnp.float32), spread, precision=lax.Precision.HIGHEST
    )
    placed = placed.reshape(groups, owners, block_count // owners, virtual_width // groups, virtual_width)
    placed = jnp.sum(lax.all_to_all(placed, "grp", 0, 0, tiled=True), axis=0)
    return jnp.sum(lax.all_to_all(placed, "aux", 0, 0, tiled=True), axis=0)


NV = 48
OB = 16
BINS = 16
GROUP = 8
ROWS = GROUP * NV
SIDE = 4
PART_A = 6
PART_B = 2
GROUPS = PART_A + PART_B
SLOTS = GROUPS * GROUP
CHUNK = 16
ALL = (0, BINS)
LIMITS = (ALL, ALL, ALL, (0, 15), (0, 9), (0, 4), ALL, (2, BINS))
STREAMS = tuple((GROUP * k, GROUP, ALL) for k in range(5)) + (
    (40, 4, ALL),
    (44, 4, (0, 8)),
    (48, 4, (0, 4)),
)
SENT = 52
AHEAD = 2
COLUMNS = tuple(
    [(0, v, v * (v + 1) // 2) for v in range(PART_A)]
    + [(PART_A, v, PART_A * (PART_A + 1) // 2 + v * (v + 1) // 2) for v in range(PART_B)]
)
TILES = PART_A * (PART_A + 1) // 2 + PART_B * (PART_B + 1) // 2
UNITS = []
for column, (base, v, first) in enumerate(COLUMNS):
    for skip in range(0, v + 1, 2):
        turn = len(UNITS) % 3
        UNITS.append(
            (column, first + skip, min(2, v + 1 - skip), (turn, (turn + 1) % 3, (turn + 2) % 3))
        )
BITS = [(d % 2, (d // 2) % 2, d // 4) for d in range(8)]
MESH = pl.DeviceIdType.MESH
VMEM = pl.BlockSpec(memory_space=pltpu.VMEM)
SMEM = pl.BlockSpec(memory_space=pltpu.SMEM)
ANY = pl.BlockSpec(memory_space=pl.ANY)


def has(limits, index):
    first, end = limits
    return (index >= first) & (index < end)


def plan(block_owner, orbital_counts):
    ids = jnp.arange(block_owner.shape[0], dtype=jnp.int32)
    same = block_owner[:, None] == block_owner[None, :]
    earlier = same & (ids[None, :] < ids[:, None])
    load = jnp.sum(jnp.where(same, orbital_counts[None, :], 0), axis=1)
    base = jnp.sum(jnp.where(earlier, orbital_counts[None, :], 0), axis=1)
    place = jnp.sum(earlier.astype(jnp.int32), axis=1)
    ahead = (load[None, :] > load[:, None]) | (
        (load[None, :] == load[:, None]) & (block_owner[None, :] < block_owner[:, None])
    )
    rank = jnp.sum((ahead & (place == 0)[None, :]).astype(jnp.int32), axis=1)
    second = rank >= BINS
    bin_of = jnp.where(second, 2 * BINS - 1 - rank, rank)
    ahead_load = jnp.sum(
        jnp.where(
            (place == 0)[None, :] & (rank[None, :] == 2 * BINS - 1 - rank[:, None]), load[None, :], 0
        ),
        axis=1,
    )
    room = jnp.zeros_like(load)
    for group, limits in enumerate(LIMITS):
        room = room + jnp.where(second == (group >= PART_A), has(limits, bin_of) * GROUP, 0)
    sent = sum(has(limits, bin_of) * number for first, number, limits in STREAMS)
    fits = jnp.all((load <= room) & (load + ahead_load <= sent))
    return bin_of, base, jnp.where(second, ahead_load, 0), load, place, second, fits


def position():
    z = lax.axis_index("grp")
    aux = lax.axis_index("aux")
    core = lax.rem(aux, 2)
    x = lax.rem(aux // 2, SIDE)
    y = aux // (2 * SIDE)
    return x, y, z, core


def device(x, y, z, core):
    return (z, (y * SIDE + x) * 2 + core)


def bin_index(x, y, z, core):
    kind = lax.rem(x, 2) + 2 * lax.rem(y, 2) + 4 * lax.rem(z, 2)
    return kind + core * (BINS - 1 - 2 * kind)


def part_index(x, y, z):
    return x // 2 + 2 * (y // 2) + 4 * (z // 2)


def shifted(value, by):
    return lax.rem(value + by + SIDE, SIDE)


def kernel(
    origin_ref,
    meta_ref,
    source,
    meta,
    screen,
    occupied_energy,
    virtual_energy,
    out,
    whole,
    packed,
    held,
    tiles,
    parts_1,
    parts_2,
    parts_3,
    exact,
    exact_parts,
    stack,
    row_sums,
    slot_sums,
    fold,
    chunks,
    chunk_parts,
    dense,
    homes,
    row_energy,
    column_energy,
    mask,
    load_sem,
    local_sem,
    send_sem,
    recv_sem,
    tile_send,
    tile_recv,
    exact_send,
    exact_recv,
    chunk_send,
    chunk_recv,
    home_send,
    home_recv,
):
    x, y, z, core = position()
    aux = lax.axis_index("aux")
    owners = lax.axis_size("aux")
    sign = 1 - 2 * core
    own_bin = bin_index(x, y, z, core)
    own_part = part_index(x, y, z)
    quarter = lax.rem(own_part, SIDE)
    half = own_part // SIDE

    pieces = load_sem.shape[0]
    size = source.shape[0] // pieces

    def load(piece):
        part = pl.ds(piece * size, size)
        return pltpu.make_async_copy(source.at[part], whole.at[part], load_sem.at[piece])

    for piece in range(pieces):
        load(piece).start()

    barrier = pltpu.get_barrier_semaphore()

    def greet(target):
        pl.semaphore_signal(barrier, inc=1, device_id=target, device_id_type=MESH)

    greet(device(x, y, z, 1 - core))
    for d in range(1, 8):
        dx, dy, dz = BITS[d]
        greet(device(shifted(x, -dx), shifted(y, -dy), shifted(z, -dz), 0))
        greet(device(shifted(x, dx), shifted(y, dy), shifted(z, dz), 1))
        greet(device(shifted(x, 2 * dx), shifted(y, 2 * dy), shifted(z, 2 * dz), core))

    def feeder(index):
        number = index // 2
        feed_core = number // 8
        kind = number + feed_core * (BINS - 1 - 2 * number)
        return (
            lax.rem(kind, 2) + 2 * lax.rem(z, 2),
            lax.rem(kind // 2, 2) + 2 * (z // 2),
            kind // 4 + 2 * lax.rem(index, 2),
            feed_core,
        )

    own_feed = own_bin * 2 + half

    @pl.loop(0, owners)
    def _(index):
        @pl.when((quarter != z) | (index != own_feed))
        def _():
            greet(device(*feeder(index)))

    fold[...] = (
        lax.rem(lax.broadcasted_iota(jnp.int32, (ROWS, NV), 0), NV)
        == lax.broadcasted_iota(jnp.int32, (ROWS, NV), 1)
    ).astype(jnp.float32)
    slot_sums[...] = jnp.zeros_like(slot_sums)
    row_sums[...] = jnp.zeros_like(row_sums)
    chunks[...] = jnp.zeros_like(chunks)

    for piece in range(pieces):
        load(piece).wait()
    pl.semaphore_wait(barrier, 22 + owners - (quarter == z).astype(jnp.int32))

    def when(limits, index, act):
        if limits == ALL:
            act()
        else:
            pl.when(has(limits, index))(act)

    def slots(stream):
        first, number, limits = STREAMS[stream]
        return pl.ds(first, number)

    def gather(d, target_core, stream, act):
        dx, dy, dz = d % 2, (d // 2) % 2, d // 4
        tx, ty, tz = shifted(x, sign * dx), shifted(y, sign * dy), shifted(z, sign * dz)
        target_bin = bin_index(tx, ty, tz, target_core)
        copy = pltpu.make_async_remote_copy(
            src_ref=packed.at[target_bin, slots(stream)],
            dst_ref=held.at[2 * d + core, slots(stream)],
            send_sem=send_sem.at[2 * d + target_core, stream],
            recv_sem=recv_sem.at[2 * d + core, stream],
            device_id=device(tx, ty, tz, target_core),
            device_id_type=MESH,
        )
        when(STREAMS[stream][2], target_bin, lambda: act(copy))

    def keep(stream):
        return pltpu.make_async_copy(
            packed.at[own_bin, slots(stream)], held.at[core, slots(stream)], local_sem.at[stream]
        )

    def send_stream(stream):
        first_slot, number_of_slots, limits = STREAMS[stream]

        @pl.loop(0, BINS)
        def _(number):
            for slot in range(first_slot, first_slot + number_of_slots):
                origin = origin_ref[number * SENT + slot]
                packed[number, slot] = whole[origin]

        @pl.loop(0, 14)
        def _(index):
            gather(7 - index // 2, lax.rem(index, 2), stream, lambda copy: copy.start())

        gather(0, 1 - core, stream, lambda copy: copy.start())
        when(limits, own_bin, lambda: keep(stream).start())

    for stream in range(AHEAD):
        send_stream(stream)

    def arrived(stream):
        def wait_all():
            keep(stream).wait()

            @pl.loop(2, BINS)
            def _(sender):
                part = held.at[sender, slots(stream)]
                pltpu.make_async_copy(part, part, recv_sem.at[sender, stream]).wait()

            part = held.at[1 - core, slots(stream)]
            pltpu.make_async_copy(part, part, recv_sem.at[1 - core, stream]).wait()

        when(STREAMS[stream][2], own_bin, wait_all)

    row_number = lax.broadcasted_iota(jnp.int32, (ROWS, ROWS), 0)
    column_number = lax.broadcasted_iota(jnp.int32, (ROWS, ROWS), 1)
    own_diagonal = (
        lax.broadcasted_iota(jnp.int32, (NV, ROWS), 0) + own_part * NV
        == lax.broadcasted_iota(jnp.int32, (NV, ROWS), 1)
    )
    same_slot = (
        lax.broadcasted_iota(jnp.int32, (GROUP, ROWS), 1) // NV
        == lax.broadcasted_iota(jnp.int32, (GROUP, ROWS), 0)
    )

    def exact_dot(left, right, axis=0):
        return lax.dot_general(
            left,
            right,
            (((1,), (axis,)), ((), ())),
            precision=lax.Precision.HIGHEST,
            preferred_element_type=jnp.float32,
        )

    blocks = meta.shape[1]
    slot_number = lax.broadcasted_iota(jnp.int32, (SLOTS, blocks), 0)
    orbital = slot_number - meta[1:2, :]
    inside = (meta[0:1, :] == own_bin) & (orbital >= 0) & (orbital < meta[2:3, :])
    pick = jnp.where(inside, 1.0, 0.0)
    slot_orbital = jnp.sum(jnp.where(inside, orbital, 0), axis=1, keepdims=True)
    occupied = exact_dot(pick, occupied_energy[...], 1)
    occupied = jnp.where(
        lax.broadcasted_iota(jnp.int32, (SLOTS, OB), 1) == slot_orbital, occupied, 0.0
    )
    energy = exact_dot(pick, virtual_energy[...], 1) - jnp.sum(occupied, axis=1, keepdims=True)
    row_slot = lax.broadcasted_iota(jnp.int32, (GROUPS, SLOTS), 0) * GROUP + own_part
    column_slot = lax.broadcasted_iota(jnp.int32, (GROUPS, SLOTS), 1)
    row_pick = exact_dot(jnp.where(row_slot == column_slot, 1.0, 0.0), pick)
    live = exact_dot(exact_dot(row_pick, jnp.where(screen[...] == 1, 1.0, 0.0)), pick, 1)
    order = jnp.where(row_slot < column_slot, 2.0, jnp.where(row_slot == column_slot, 1.0, 0.0))
    kind = jnp.where(live > 0.5, order, 0.0)
    for group in range(GROUPS):
        lanes = exact_dot(energy[group * GROUP : (group + 1) * GROUP], fold[...], 1)
        lanes = jnp.sum(jnp.where(same_slot, lanes, 0.0), axis=0, keepdims=True)
        column_energy[group] = lanes
        row_energy[group] = jnp.sum(jnp.where(own_diagonal, lanes, 0.0), axis=1, keepdims=True)
        wide = lax.broadcasted_iota(jnp.int32, (SLOTS, ROWS), 0) == (
            group * GROUP + lax.broadcasted_iota(jnp.int32, (SLOTS, ROWS), 1) // NV
        )
        mask[group] = exact_dot(kind, jnp.where(wide, 1.0, 0.0))

    def find(block, found):
        result = []
        for index in range(6):
            hit = (
                (meta_ref[0, block] == own_bin)
                & (meta_ref[3, block] == index % 3)
                & (meta_ref[4, block] == index // 3)
            )
            old = found[3 * index : 3 * index + 3]
            new = (meta_ref[1, block], meta_ref[2, block], block)
            result += [jnp.where(hit, n, o) for n, o in zip(new, old)]
        return tuple(result)

    nothing = jnp.int32(0)
    found = lax.fori_loop(0, blocks, find, (nothing, nothing, jnp.int32(-1)) * 6)
    block_start, block_slots, block_id = found[0::3], found[1::3], found[2::3]

    def settle():
        offset = block_slots[0] + block_slots[1] + block_slots[2]

        @pl.loop(0, BINS)
        def _(sender):
            for slot in range(PART_B * GROUP):
                held[sender, SENT + slot] = held[sender, offset + slot]

    def rows_of(base, group):
        first = group * GROUP + (SENT if base else 0)
        return jnp.concatenate(
            [
                held[sender, pl.ds(first, GROUP)].reshape(ROWS, held.shape[-1])
                for sender in range(BINS)
            ],
            axis=1,
        )

    def peer(e):
        dx, dy, dz = BITS[e]
        px, py, pz = shifted(x, 2 * dx), shifted(y, 2 * dy), shifted(z, 2 * dz)
        return part_index(px, py, pz), device(px, py, pz, core)

    bit = (x // 2, y // 2, z // 2)

    def view(fixed):
        return tuple(fixed.get(axis, slice(None)) for axis in (2, 1, 0))

    def step(unit, phase):
        column, first, number, order = UNITS[unit]
        fixed = {axis: bit[axis] for axis in order[:phase]}
        axis = order[phase]
        fixed[axis] = 1 - bit[axis]
        run = pl.ds(first, number)
        far = [shifted(c, 2 * (axis == k)) for k, c in enumerate((x, y, z))]
        landing = (parts_1.at[:, :, run], parts_2.at[:, run], parts_3.at[run])[phase]
        return pltpu.make_async_remote_copy(
            src_ref=tiles.at[view(fixed) + (run,)],
            dst_ref=landing,
            send_sem=tile_send.at[unit, phase],
            recv_sem=tile_recv.at[unit, phase],
            device_id=device(*far, core),
            device_id_type=MESH,
        )

    def units_of(column):
        return [unit for unit in range(len(UNITS)) if UNITS[unit][0] == column]

    def merge(column, phase):
        for unit in units_of(column):
            _, first, number, order = UNITS[unit]
            step(unit, phase).wait_recv()
            fixed = {axis: bit[axis] for axis in order[: phase + 1]}
            rest = [axis for axis in (2, 1, 0) if axis not in fixed]
            landed = (parts_1, parts_2)[phase]

            @pl.loop(first, first + number)
            def _(index):
                for choice in range(2 ** len(rest)):
                    at = tuple((choice // 2**k) % 2 for k in range(len(rest)))
                    place = view({**fixed, **dict(zip(rest, at))}) + (index,)
                    tiles[place] = (
                        tiles[place].astype(jnp.float32) + landed[at + (index,)].astype(jnp.float32)
                    ).astype(jnp.bfloat16)

            step(unit, phase + 1).start()

    def scatter_exact(e, batch):
        part, target = peer(e)
        return pltpu.make_async_remote_copy(
            src_ref=exact.at[batch, part],
            dst_ref=exact_parts.at[e - 1, batch],
            send_sem=exact_send.at[e - 1, batch],
            recv_sem=exact_recv.at[e - 1, batch],
            device_id=target,
            device_id_type=MESH,
        )

    def make_column(column):
        base, v, first = COLUMNS[column]

        @pl.loop(0, v + 1)
        def _(u):
            tile = lax.dot_general(
                rows_of(base, u),
                rows_of(base, v),
                (((1,), (1,)), ((), ())),
                preferred_element_type=jnp.float32,
            )

            @pl.when(u == v)
            def _():
                diagonal = jnp.where(row_number == column_number, tile, 0.0)
                diagonal = jnp.where(same_slot, jnp.sum(diagonal, axis=0, keepdims=True), 0.0)
                diagonal = exact_dot(diagonal, fold[...])
                for part in range(8):
                    exact[column // 4, part, column % 4 : column % 4 + 1, :NV] = diagonal[
                        part : part + 1
                    ]

            rounded = tile.astype(jnp.bfloat16)
            for part in range(8):
                tiles[part // 4, (part // 2) % 2, part % 2, first + u] = rounded[
                    part * NV : (part + 1) * NV
                ]

        for unit in units_of(column):
            step(unit, 0).start()

    def add_column(column):
        base, v, first = COLUMNS[column]
        for unit in units_of(column):
            step(unit, 2).wait_recv()
        diagonal = exact[column // 4, own_part]
        for e in range(7):
            diagonal = diagonal + exact_parts[e, column // 4]
        diagonal = exact_dot(diagonal[:, :NV], fold[...], 1)[column % 4 : column % 4 + 1]

        @pl.loop(0, v + 1)
        def _(u):
            integral = tiles[bit[2], bit[1], bit[0], first + u].astype(jnp.float32) + parts_3[
                first + u
            ].astype(jnp.float32)
            integral = jnp.where(own_diagonal & (u == v), diagonal, integral)
            kind = mask[base + v, pl.ds(base + u, 1), :]
            quotient = integral / (row_energy[base + u] + column_energy[base + v])
            amplitude = jnp.where(kind > 0, quotient, 0.0).astype(jnp.bfloat16)
            row_sums[base + u] = row_sums[base + u] + lax.dot_general(
                amplitude, amplitude, (((1,), (1,)), ((), ())), preferred_element_type=jnp.float32
            )
            stack[pl.ds(pl.multiple_of(u * NV, NV), NV), :] = jnp.where(
                kind > 1, quotient, 0.0
            ).astype(jnp.bfloat16)

        stacked = stack[: (v + 1) * NV, :]
        product = lax.dot_general(
            stacked, stacked, (((0,), (0,)), ((), ())), preferred_element_type=jnp.float32
        )
        slot_sums[(base + v) * ROWS : (base + v + 1) * ROWS, :] = jnp.dot(
            jnp.where(row_number // NV == column_number // NV, product, 0.0),
            fold[...],
            precision=lax.Precision.HIGHEST,
            preferred_element_type=jnp.float32,
        )

    def advance(column, phase):
        if column < 0:
            return
        act = (
            lambda: make_column(column),
            lambda: merge(column, 0),
            lambda: merge(column, 1),
            lambda: add_column(column),
        )[phase]
        when(LIMITS[column], own_bin, act)

    def receive(stream):
        arrived(stream)
        if stream + AHEAD < len(STREAMS):
            send_stream(stream + AHEAD)

    def start_exact(batch):
        for e in range(7, 0, -1):
            scatter_exact(e, batch).start()

    def wait_exact(batch):
        for e in range(1, 8):
            scatter_exact(e, batch).wait_recv()

    for column in range(PART_A):
        receive(column)
        if column == PART_A - 1:
            receive(PART_A)
        advance(column, 0)
        if column == 3:
            start_exact(0)
        advance(column - 1, 1)
        advance(column - 2, 2)
        if column == 3:
            wait_exact(0)
        advance(column - 3, 3)
    receive(len(STREAMS) - 1)
    settle()
    late = range(PART_A, GROUPS)
    for column in late:
        advance(column, 0)
    start_exact(1)
    for column in (PART_A - 1, *late):
        advance(column, 1)
    advance(PART_A - 2, 2)
    advance(PART_A - 3, 3)
    for column in (PART_A - 1, *late):
        advance(column, 2)
    wait_exact(1)
    for column in (PART_A - 2, PART_A - 1, *late):
        advance(column, 3)
    for group in range(GROUPS):
        part = pl.ds(pl.multiple_of(group * ROWS + own_part * NV, NV), NV)
        slot_sums[part, :] = slot_sums[part, :] + row_sums[group]

    for side in range(2):
        first_slot = side * PART_A * GROUP

        def add_slot(step, sums):
            slot = first_slot + step
            value = slot_sums[pl.ds(pl.multiple_of(slot * NV, NV), NV), :]
            result = []
            for i in range(3 * side, 3 * side + 3):
                own = (slot >= block_start[i]) & (slot < block_start[i] + block_slots[i])
                result.append(sums[i % 3] + jnp.where(own, value, jnp.zeros_like(value)))
            return tuple(result)

        zero = jnp.zeros((NV, NV), jnp.float32)
        sums = lax.fori_loop(0, (PART_A, PART_B)[side] * GROUP, add_slot, (zero, zero, zero))
        width = NV // SIDE
        for i in range(3):
            for g in range(SIDE):
                chunks[side * SIDE + g, i * CHUNK : i * CHUNK + width, :NV] = sums[i][
                    g * width : (g + 1) * width
                ]

    def scatter_chunk(e):
        part, target = peer(e)
        return pltpu.make_async_remote_copy(
            src_ref=chunks.at[part],
            dst_ref=chunk_parts.at[e - 1],
            send_sem=chunk_send.at[e - 1],
            recv_sem=chunk_recv.at[e - 1],
            device_id=target,
            device_id_type=MESH,
        )

    for e in range(7, 0, -1):
        scatter_chunk(e).start()
    for e in range(1, 8):
        scatter_chunk(e).wait_recv()
    total = chunks[own_part]
    for e in range(7):
        total = total + chunk_parts[e]
    pieces = [total[i * CHUNK : (i + 1) * CHUNK] for i in range(3)]
    turned = [pltpu.roll(piece, 64, 1) for piece in pieces]

    def send_home(target):
        return pltpu.make_async_remote_copy(
            src_ref=dense.at[target],
            dst_ref=homes.at[own_feed],
            send_sem=home_send.at[target],
            recv_sem=home_recv.at[own_feed],
            device_id=(quarter, target),
            device_id_type=MESH,
        )

    def away(target):
        return (quarter != z) | (target != aux)

    @pl.loop(0, owners)
    def _(target):
        message = jnp.zeros((CHUNK, 128), jnp.float32)
        for i in range(3):
            block = jnp.where(half == 0, block_id[i], block_id[3 + i])
            message = message + jnp.where(block == 2 * target, pieces[i], 0.0)
            message = message + jnp.where(block == 2 * target + 1, turned[i], 0.0)
        dense[target] = message

        @pl.when(away(target))
        def _():
            send_home(target).start()

    @pl.when(quarter == z)
    def _():
        homes[own_feed] = dense[aux]

    @pl.loop(0, owners)
    def _(index):
        @pl.when((quarter != z) | (index != own_feed))
        def _():
            pltpu.make_async_copy(homes.at[index], homes.at[index], home_recv.at[index]).wait()

    out[...] = jnp.sum(homes[...], axis=0)

    @pl.loop(0, owners)
    def _(target):
        @pl.when(away(target))
        def _():
            send_home(target).wait_send()

    for e in range(1, 8):
        scatter_chunk(e).wait_send()

    def sent_column(column):
        for unit in units_of(column):
            for phase in range(3):
                step(unit, phase).wait_send()

    for column in range(GROUPS):
        when(LIMITS[column], own_bin, lambda: sent_column(column))
    for batch in range(2):
        for e in range(1, 8):
            scatter_exact(e, batch).wait_send()
    for stream in range(len(STREAMS)):
        gather(0, 1 - core, stream, lambda copy: copy.wait_send())

        @pl.loop(2, BINS)
        def _(index):
            gather(index // 2, lax.rem(index, 2), stream, lambda copy: copy.wait_send())


def binned(
    bin_of,
    base,
    offset,
    load,
    place,
    second,
    three_index,
    block_owner,
    pair_screen,
    orbital_counts,
    occupied_energy,
    virtual_energy,
):
    blocks, row_count, aux_local = three_index.shape
    block_ids = jnp.arange(blocks, dtype=jnp.int32)
    sent_ids = jnp.arange(SENT, dtype=jnp.int32)[:, None] - (base + offset)[None, :]
    bins = jnp.arange(BINS, dtype=jnp.int32)
    origin = jnp.sum(
        jnp.where(
            (bin_of[None, None, :] == bins[:, None, None])
            & ((sent_ids >= 0) & (sent_ids < orbital_counts[None, :]))[None],
            (block_ids[None, :] * OB + sent_ids)[None],
            0,
        ),
        axis=2,
    )
    start = base + jnp.where(second, PART_A * GROUP, 0)
    meta = jnp.stack([bin_of, start, orbital_counts, place, second.astype(jnp.int32)] + [base] * 3)
    owners = lax.axis_size("aux")
    home = pl.pallas_call(
        kernel,
        out_shape=jax.ShapeDtypeStruct((CHUNK, 128), jnp.float32),
        in_specs=[SMEM, SMEM, ANY, VMEM, VMEM, VMEM, VMEM],
        out_specs=VMEM,
        scratch_shapes=[
            pltpu.VMEM((blocks * OB, NV, aux_local), jnp.bfloat16),
            pltpu.VMEM((BINS, SENT, NV, aux_local), jnp.bfloat16),
            pltpu.VMEM((BINS, SENT + PART_B * GROUP, NV, aux_local), jnp.bfloat16),
            pltpu.VMEM((2, 2, 2, TILES, NV, ROWS), jnp.bfloat16),
            pltpu.VMEM((2, 2, TILES, NV, ROWS), jnp.bfloat16),
            pltpu.VMEM((2, TILES, NV, ROWS), jnp.bfloat16),
            pltpu.VMEM((TILES, NV, ROWS), jnp.bfloat16),
            pltpu.VMEM((2, 8, 8, 128), jnp.float32),
            pltpu.VMEM((7, 2, 8, 128), jnp.float32),
            pltpu.VMEM((PART_A * NV, ROWS), jnp.bfloat16),
            pltpu.VMEM((GROUPS, NV, NV), jnp.float32),
            pltpu.VMEM((SLOTS * NV, NV), jnp.float32),
            pltpu.VMEM((ROWS, NV), jnp.float32),
            pltpu.VMEM((8, 3 * CHUNK, 128), jnp.float32),
            pltpu.VMEM((7, 3 * CHUNK, 128), jnp.float32),
            pltpu.VMEM((owners, CHUNK, 128), jnp.float32),
            pltpu.VMEM((owners, CHUNK, 128), jnp.float32),
            pltpu.VMEM((GROUPS, NV, 1), jnp.float32),
            pltpu.VMEM((GROUPS, 1, ROWS), jnp.float32),
            pltpu.VMEM((GROUPS, GROUPS, ROWS), jnp.float32),
            pltpu.SemaphoreType.DMA((8,)),
            pltpu.SemaphoreType.DMA((len(STREAMS),)),
            pltpu.SemaphoreType.DMA((BINS, len(STREAMS))),
            pltpu.SemaphoreType.DMA((BINS, len(STREAMS))),
            pltpu.SemaphoreType.DMA((len(UNITS), 3)),
            pltpu.SemaphoreType.DMA((len(UNITS), 3)),
            pltpu.SemaphoreType.DMA((7, 2)),
            pltpu.SemaphoreType.DMA((7, 2)),
            pltpu.SemaphoreType.DMA((7,)),
            pltpu.SemaphoreType.DMA((7,)),
            pltpu.SemaphoreType.DMA((owners,)),
            pltpu.SemaphoreType.DMA((owners,)),
        ],
        compiler_params=pltpu.CompilerParams(
            collective_id=0, has_side_effects=True, vmem_limit_bytes=60 * 2**20
        ),
    )(
        origin.reshape(-1),
        meta,
        three_index.reshape(blocks * OB, NV, aux_local),
        meta,
        pair_screen,
        occupied_energy.T,
        virtual_energy.T,
    )
    return home.reshape(CHUNK, 2, 64)[: NV // SIDE, :, :NV].transpose(1, 0, 2)


def local(three_index, block_owner, pair_screen, orbital_counts, occupied_energy, virtual_energy):
    *spots, fits = plan(block_owner, orbital_counts)
    arguments = (
        three_index,
        block_owner,
        pair_screen,
        orbital_counts,
        occupied_energy,
        virtual_energy,
    )
    return lax.cond(
        fits,
        lambda: binned(*spots, *arguments),
        lambda: general(*arguments),
    )


def solution(mesh):
    in_specs = (P(None, None, ("grp", "aux")), P(), P(), P(), P(), P())
    out_specs = P("aux", "grp", None)
    return jax.shard_map(local, mesh=mesh, in_specs=in_specs, out_specs=out_specs, check_vma=False)
```

```python
import jax
import jax.numpy as jnp
from jax import lax
from jax.experimental import pallas as pl
from jax.experimental.pallas import tpu as pltpu
from jax.sharding import PartitionSpec as P

CAP = 3


def slot_tiles(source, slot_block, slot_valid, owners):
    picked = jnp.take(source, slot_block.reshape(-1), axis=0)
    picked = picked.reshape(owners, CAP, source.shape[1], source.shape[2])
    return jnp.where(slot_valid[:, :, None, None] > 0, picked, jnp.zeros_like(picked))


def pair_block(received, first, second):
    return lax.dot_general(
        lax.dynamic_index_in_dim(received, first, 1, False),
        lax.dynamic_index_in_dim(received, second, 1, False),
        (((0, 2), (0, 2)), ((), ())),
        preferred_element_type=jnp.float32,
    )


def general(three_index, block_owner, pair_screen, orbital_counts, occupied_energy, virtual_energy):
    block_count, row_count, aux_local = three_index.shape
    occupied_width = occupied_energy.shape[1]
    virtual_width = virtual_energy.shape[1]
    groups = lax.axis_size("grp")
    owners = lax.axis_size("aux")
    own_index = lax.axis_index("aux")
    group_index = lax.axis_index("grp")
    quarter = row_count // groups
    owner_ids = jnp.arange(owners, dtype=jnp.int32)
    owned = (block_owner[None, :] == owner_ids[:, None]).astype(jnp.int32)
    slot_rank = jnp.cumsum(owned, axis=1) - 1
    slot_ids = jnp.arange(CAP, dtype=jnp.int32)
    selection = owned[:, None, :] * (slot_rank[:, None, :] == slot_ids[None, :, None]).astype(
        jnp.int32
    )
    block_ids = jnp.arange(block_count, dtype=jnp.int32)
    slot_block = jnp.sum(selection * block_ids[None, None, :], axis=2)
    slot_valid = jnp.sum(selection, axis=2)
    mine = lax.dynamic_index_in_dim(selection, own_index, 0, keepdims=False)
    my_block = jnp.sum(mine * block_ids[None, :], axis=1)
    my_valid = jnp.sum(mine, axis=1)
    energy = (virtual_energy[:, None, :] - occupied_energy[:, :, None]).reshape(
        block_count, row_count
    )
    occupied_flags = (
        jnp.arange(occupied_width, dtype=jnp.int32)[None, :] < orbital_counts[:, None]
    ).astype(jnp.float32)
    occupancy = jnp.repeat(occupied_flags, virtual_width, axis=1)
    slot_energy = jnp.take(energy, my_block, axis=0)
    slot_occupancy = jnp.take(occupancy, my_block, axis=0)
    screened = jnp.take(jnp.take(pair_screen, my_block, axis=0), my_block, axis=1)
    is_live = screened * my_valid[:, None] * my_valid[None, :] > 0

    def slot_amplitude(integral, first, second):
        energy_rows = lax.dynamic_slice_in_dim(slot_energy[first], group_index * quarter, quarter)
        occupied_rows = lax.dynamic_slice_in_dim(
            slot_occupancy[first], group_index * quarter, quarter
        )
        divisor = energy_rows[:, None] + slot_energy[second][None, :]
        return (
            occupied_rows[:, None] * slot_occupancy[second][None, :] * integral / divisor
        ).astype(jnp.bfloat16)

    def own_density(amplitude):
        row_form = amplitude.reshape(quarter // virtual_width, virtual_width, row_count)
        return jnp.einsum("iax,ibx->ab", row_form, row_form, preferred_element_type=jnp.float32)

    outgoing = slot_tiles(three_index, slot_block, slot_valid, owners)
    received = lax.all_to_all(outgoing, "aux", split_axis=0, concat_axis=0, tiled=True)
    empty = jnp.zeros((virtual_width, virtual_width), jnp.float32)

    def one_pair(parts, pair):
        first = pair // CAP
        second = pair % CAP
        integral = pair_block(received, first, second)
        sent = integral.reshape(groups, quarter, row_count)
        summed = jnp.sum(lax.all_to_all(sent, "grp", 0, 0, tiled=True), axis=0)
        part = own_density(slot_amplitude(summed, first, second))
        part = jnp.where(is_live[first, second], part, empty)
        return parts.at[first].add(part), None

    slot_parts, _ = lax.scan(
        one_pair,
        jnp.zeros((CAP, virtual_width, virtual_width), jnp.float32),
        jnp.arange(CAP * CAP, dtype=jnp.int32),
    )
    spread = slot_parts.reshape(CAP, groups, virtual_width // groups, virtual_width)
    placed = jnp.einsum(
        "cb,cgxy->gbxy", mine.astype(jnp.float32), spread, precision=lax.Precision.HIGHEST
    )
    placed = placed.reshape(groups, owners, block_count // owners, virtual_width // groups, virtual_width)
    placed = jnp.sum(lax.all_to_all(placed, "grp", 0, 0, tiled=True), axis=0)
    return jnp.sum(lax.all_to_all(placed, "aux", 0, 0, tiled=True), axis=0)


NV = 48
OB = 16
BINS = 16
GROUP = 8
ROWS = GROUP * NV
SIDE = 4
PART_A = 6
PART_B = 2
GROUPS = PART_A + PART_B
SLOTS = GROUPS * GROUP
CHUNK = 16
ALL = (0, BINS)
LIMITS = (ALL, ALL, ALL, (0, 15), (0, 9), (0, 4), ALL, (2, BINS))
STREAMS = tuple((GROUP * k, GROUP, ALL) for k in range(5)) + (
    (40, 4, ALL),
    (44, 4, (0, 8)),
    (48, 4, (0, 4)),
)
SENT = 52
AHEAD = 2
COLUMNS = tuple(
    [(0, v, v * (v + 1) // 2) for v in range(PART_A)]
    + [(PART_A, v, PART_A * (PART_A + 1) // 2 + v * (v + 1) // 2) for v in range(PART_B)]
)
TILES = PART_A * (PART_A + 1) // 2 + PART_B * (PART_B + 1) // 2
UNITS = []
for column, (base, v, first) in enumerate(COLUMNS):
    for skip in range(0, v + 1, 2):
        turn = len(UNITS) % 3
        UNITS.append(
            (column, first + skip, min(2, v + 1 - skip), (turn, (turn + 1) % 3, (turn + 2) % 3))
        )
BITS = [(d % 2, (d // 2) % 2, d // 4) for d in range(8)]
MESH = pl.DeviceIdType.MESH
VMEM = pl.BlockSpec(memory_space=pltpu.VMEM)
SMEM = pl.BlockSpec(memory_space=pltpu.SMEM)
ANY = pl.BlockSpec(memory_space=pl.ANY)


def has(limits, index):
    first, end = limits
    return (index >= first) & (index < end)


def plan(block_owner, orbital_counts):
    ids = jnp.arange(block_owner.shape[0], dtype=jnp.int32)
    same = block_owner[:, None] == block_owner[None, :]
    earlier = same & (ids[None, :] < ids[:, None])
    load = jnp.sum(jnp.where(same, orbital_counts[None, :], 0), axis=1)
    base = jnp.sum(jnp.where(earlier, orbital_counts[None, :], 0), axis=1)
    place = jnp.sum(earlier.astype(jnp.int32), axis=1)
    ahead = (load[None, :] > load[:, None]) | (
        (load[None, :] == load[:, None]) & (block_owner[None, :] < block_owner[:, None])
    )
    rank = jnp.sum((ahead & (place == 0)[None, :]).astype(jnp.int32), axis=1)
    second = rank >= BINS
    bin_of = jnp.where(second, 2 * BINS - 1 - rank, rank)
    ahead_load = jnp.sum(
        jnp.where(
            (place == 0)[None, :] & (rank[None, :] == 2 * BINS - 1 - rank[:, None]), load[None, :], 0
        ),
        axis=1,
    )
    room = jnp.zeros_like(load)
    for group, limits in enumerate(LIMITS):
        room = room + jnp.where(second == (group >= PART_A), has(limits, bin_of) * GROUP, 0)
    sent = sum(has(limits, bin_of) * number for first, number, limits in STREAMS)
    fits = jnp.all((load <= room) & (load + ahead_load <= sent))
    return bin_of, base, jnp.where(second, ahead_load, 0), load, place, second, fits


def position():
    z = lax.axis_index("grp")
    aux = lax.axis_index("aux")
    core = lax.rem(aux, 2)
    x = lax.rem(aux // 2, SIDE)
    y = aux // (2 * SIDE)
    return x, y, z, core


def device(x, y, z, core):
    return (z, (y * SIDE + x) * 2 + core)


def bin_index(x, y, z, core):
    kind = lax.rem(x, 2) + 2 * lax.rem(y, 2) + 4 * lax.rem(z, 2)
    return kind + core * (BINS - 1 - 2 * kind)


def part_index(x, y, z):
    return x // 2 + 2 * (y // 2) + 4 * (z // 2)


def shifted(value, by):
    return lax.rem(value + by + SIDE, SIDE)


def kernel(
    origin_ref,
    meta_ref,
    source,
    meta,
    screen,
    occupied_energy,
    virtual_energy,
    out,
    whole,
    packed,
    held,
    tiles,
    parts_1,
    parts_2,
    parts_3,
    exact,
    exact_parts,
    stack,
    row_sums,
    slot_sums,
    fold,
    chunks,
    chunk_parts,
    dense,
    homes,
    row_energy,
    column_energy,
    mask,
    load_sem,
    local_sem,
    send_sem,
    recv_sem,
    tile_send,
    tile_recv,
    exact_send,
    exact_recv,
    chunk_send,
    chunk_recv,
    home_send,
    home_recv,
):
    x, y, z, core = position()
    aux = lax.axis_index("aux")
    owners = lax.axis_size("aux")
    sign = 1 - 2 * core
    own_bin = bin_index(x, y, z, core)
    own_part = part_index(x, y, z)
    quarter = lax.rem(own_part, SIDE)
    half = own_part // SIDE

    pieces = load_sem.shape[0]
    size = source.shape[0] // pieces

    def load(piece):
        part = pl.ds(piece * size, size)
        return pltpu.make_async_copy(source.at[part], whole.at[part], load_sem.at[piece])

    for piece in range(pieces):
        load(piece).start()

    barrier = pltpu.get_barrier_semaphore()

    def greet(target):
        pl.semaphore_signal(barrier, inc=1, device_id=target, device_id_type=MESH)

    greet(device(x, y, z, 1 - core))
    for d in range(1, 8):
        dx, dy, dz = BITS[d]
        greet(device(shifted(x, -dx), shifted(y, -dy), shifted(z, -dz), 0))
        greet(device(shifted(x, dx), shifted(y, dy), shifted(z, dz), 1))
        greet(device(shifted(x, 2 * dx), shifted(y, 2 * dy), shifted(z, 2 * dz), core))

    def feeder(index):
        number = index // 2
        feed_core = number // 8
        kind = number + feed_core * (BINS - 1 - 2 * number)
        return (
            lax.rem(kind, 2) + 2 * lax.rem(z, 2),
            lax.rem(kind // 2, 2) + 2 * (z // 2),
            kind // 4 + 2 * lax.rem(index, 2),
            feed_core,
        )

    own_feed = own_bin * 2 + half

    @pl.loop(0, owners)
    def _(index):
        @pl.when((quarter != z) | (index != own_feed))
        def _():
            greet(device(*feeder(index)))

    fold[...] = (
        lax.rem(lax.broadcasted_iota(jnp.int32, (ROWS, NV), 0), NV)
        == lax.broadcasted_iota(jnp.int32, (ROWS, NV), 1)
    ).astype(jnp.float32)
    slot_sums[...] = jnp.zeros_like(slot_sums)
    row_sums[...] = jnp.zeros_like(row_sums)
    chunks[...] = jnp.zeros_like(chunks)

    for piece in range(pieces):
        load(piece).wait()
    pl.semaphore_wait(barrier, 22 + owners - (quarter == z).astype(jnp.int32))

    def when(limits, index, act):
        if limits == ALL:
            act()
        else:
            pl.when(has(limits, index))(act)

    def slots(stream):
        first, number, limits = STREAMS[stream]
        return pl.ds(first, number)

    def gather(d, target_core, stream, act):
        dx, dy, dz = d % 2, (d // 2) % 2, d // 4
        tx, ty, tz = shifted(x, sign * dx), shifted(y, sign * dy), shifted(z, sign * dz)
        target_bin = bin_index(tx, ty, tz, target_core)
        copy = pltpu.make_async_remote_copy(
            src_ref=packed.at[target_bin, slots(stream)],
            dst_ref=held.at[2 * d + core, slots(stream)],
            send_sem=send_sem.at[2 * d + target_core, stream],
            recv_sem=recv_sem.at[2 * d + core, stream],
            device_id=device(tx, ty, tz, target_core),
            device_id_type=MESH,
        )
        when(STREAMS[stream][2], target_bin, lambda: act(copy))

    def keep(stream):
        return pltpu.make_async_copy(
            packed.at[own_bin, slots(stream)], held.at[core, slots(stream)], local_sem.at[stream]
        )

    def send_stream(stream):
        first_slot, number_of_slots, limits = STREAMS[stream]

        @pl.loop(0, BINS)
        def _(number):
            for slot in range(first_slot, first_slot + number_of_slots):
                origin = origin_ref[number * SENT + slot]
                packed[number, slot] = whole[origin]

        @pl.loop(0, 14)
        def _(index):
            gather(7 - index // 2, lax.rem(index, 2), stream, lambda copy: copy.start())

        gather(0, 1 - core, stream, lambda copy: copy.start())
        when(limits, own_bin, lambda: keep(stream).start())

    for stream in range(AHEAD):
        send_stream(stream)

    def arrived(stream):
        def wait_all():
            keep(stream).wait()

            @pl.loop(2, BINS)
            def _(sender):
                part = held.at[sender, slots(stream)]
                pltpu.make_async_copy(part, part, recv_sem.at[sender, stream]).wait()

            part = held.at[1 - core, slots(stream)]
            pltpu.make_async_copy(part, part, recv_sem.at[1 - core, stream]).wait()

        when(STREAMS[stream][2], own_bin, wait_all)

    row_number = lax.broadcasted_iota(jnp.int32, (ROWS, ROWS), 0)
    column_number = lax.broadcasted_iota(jnp.int32, (ROWS, ROWS), 1)
    own_diagonal = (
        lax.broadcasted_iota(jnp.int32, (NV, ROWS), 0) + own_part * NV
        == lax.broadcasted_iota(jnp.int32, (NV, ROWS), 1)
    )
    same_slot = (
        lax.broadcasted_iota(jnp.int32, (GROUP, ROWS), 1) // NV
        == lax.broadcasted_iota(jnp.int32, (GROUP, ROWS), 0)
    )

    def exact_dot(left, right, axis=0):
        return lax.dot_general(
            left,
            right,
            (((1,), (axis,)), ((), ())),
            precision=lax.Precision.HIGHEST,
            preferred_element_type=jnp.float32,
        )

    blocks = meta.shape[1]
    slot_number = lax.broadcasted_iota(jnp.int32, (SLOTS, blocks), 0)
    orbital = slot_number - meta[1:2, :]
    inside = (meta[0:1, :] == own_bin) & (orbital >= 0) & (orbital < meta[2:3, :])
    pick = jnp.where(inside, 1.0, 0.0)
    slot_orbital = jnp.sum(jnp.where(inside, orbital, 0), axis=1, keepdims=True)
    occupied = exact_dot(pick, occupied_energy[...], 1)
    occupied = jnp.where(
        lax.broadcasted_iota(jnp.int32, (SLOTS, OB), 1) == slot_orbital, occupied, 0.0
    )
    energy = exact_dot(pick, virtual_energy[...], 1) - jnp.sum(occupied, axis=1, keepdims=True)
    row_slot = lax.broadcasted_iota(jnp.int32, (GROUPS, SLOTS), 0) * GROUP + own_part
    column_slot = lax.broadcasted_iota(jnp.int32, (GROUPS, SLOTS), 1)
    row_pick = exact_dot(jnp.where(row_slot == column_slot, 1.0, 0.0), pick)
    live = exact_dot(exact_dot(row_pick, jnp.where(screen[...] == 1, 1.0, 0.0)), pick, 1)
    order = jnp.where(row_slot < column_slot, 2.0, jnp.where(row_slot == column_slot, 1.0, 0.0))
    kind = jnp.where(live > 0.5, order, 0.0)
    for group in range(GROUPS):
        lanes = exact_dot(energy[group * GROUP : (group + 1) * GROUP], fold[...], 1)
        lanes = jnp.sum(jnp.where(same_slot, lanes, 0.0), axis=0, keepdims=True)
        column_energy[group] = lanes
        row_energy[group] = jnp.sum(jnp.where(own_diagonal, lanes, 0.0), axis=1, keepdims=True)
        wide = lax.broadcasted_iota(jnp.int32, (SLOTS, ROWS), 0) == (
            group * GROUP + lax.broadcasted_iota(jnp.int32, (SLOTS, ROWS), 1) // NV
        )
        mask[group] = exact_dot(kind, jnp.where(wide, 1.0, 0.0))

    def find(block, found):
        result = []
        for index in range(6):
            hit = (
                (meta_ref[0, block] == own_bin)
                & (meta_ref[3, block] == index % 3)
                & (meta_ref[4, block] == index // 3)
            )
            old = found[3 * index : 3 * index + 3]
            new = (meta_ref[1, block], meta_ref[2, block], block)
            result += [jnp.where(hit, n, o) for n, o in zip(new, old)]
        return tuple(result)

    nothing = jnp.int32(0)
    found = lax.fori_loop(0, blocks, find, (nothing, nothing, jnp.int32(-1)) * 6)
    block_start, block_slots, block_id = found[0::3], found[1::3], found[2::3]

    def settle():
        offset = block_slots[0] + block_slots[1] + block_slots[2]

        @pl.loop(0, BINS)
        def _(sender):
            for slot in range(PART_B * GROUP):
                held[sender, SENT + slot] = held[sender, offset + slot]

    def rows_of(base, group):
        first = group * GROUP + (SENT if base else 0)
        return jnp.concatenate(
            [
                held[sender, pl.ds(first, GROUP)].reshape(ROWS, held.shape[-1])
                for sender in range(BINS)
            ],
            axis=1,
        )

    def peer(e):
        dx, dy, dz = BITS[e]
        px, py, pz = shifted(x, 2 * dx), shifted(y, 2 * dy), shifted(z, 2 * dz)
        return part_index(px, py, pz), device(px, py, pz, core)

    bit = (x // 2, y // 2, z // 2)

    def view(fixed):
        return tuple(fixed.get(axis, slice(None)) for axis in (2, 1, 0))

    def step(unit, phase):
        column, first, number, order = UNITS[unit]
        fixed = {axis: bit[axis] for axis in order[:phase]}
        axis = order[phase]
        fixed[axis] = 1 - bit[axis]
        run = pl.ds(first, number)
        far = [shifted(c, 2 * (axis == k)) for k, c in enumerate((x, y, z))]
        landing = (parts_1.at[:, :, run], parts_2.at[:, run], parts_3.at[run])[phase]
        return pltpu.make_async_remote_copy(
            src_ref=tiles.at[view(fixed) + (run,)],
            dst_ref=landing,
            send_sem=tile_send.at[unit, phase],
            recv_sem=tile_recv.at[unit, phase],
            device_id=device(*far, core),
            device_id_type=MESH,
        )

    def units_of(column):
        return [unit for unit in range(len(UNITS)) if UNITS[unit][0] == column]

    def merge(column, phase):
        for unit in units_of(column):
            _, first, number, order = UNITS[unit]
            step(unit, phase).wait_recv()
            fixed = {axis: bit[axis] for axis in order[: phase + 1]}
            rest = [axis for axis in (2, 1, 0) if axis not in fixed]
            landed = (parts_1, parts_2)[phase]

            @pl.loop(first, first + number)
            def _(index):
                for choice in range(2 ** len(rest)):
                    at = tuple((choice // 2**k) % 2 for k in range(len(rest)))
                    place = view({**fixed, **dict(zip(rest, at))}) + (index,)
                    tiles[place] = (
                        tiles[place].astype(jnp.float32) + landed[at + (index,)].astype(jnp.float32)
                    ).astype(jnp.bfloat16)

            step(unit, phase + 1).start()

    def scatter_exact(e, batch):
        part, target = peer(e)
        return pltpu.make_async_remote_copy(
            src_ref=exact.at[batch, part],
            dst_ref=exact_parts.at[e - 1, batch],
            send_sem=exact_send.at[e - 1, batch],
            recv_sem=exact_recv.at[e - 1, batch],
            device_id=target,
            device_id_type=MESH,
        )

    def make_column(column):
        base, v, first = COLUMNS[column]

        @pl.loop(0, v + 1)
        def _(u):
            tile = lax.dot_general(
                rows_of(base, u),
                rows_of(base, v),
                (((1,), (1,)), ((), ())),
                preferred_element_type=jnp.float32,
            )

            @pl.when(u == v)
            def _():
                diagonal = jnp.where(row_number == column_number, tile, 0.0)
                diagonal = jnp.where(same_slot, jnp.sum(diagonal, axis=0, keepdims=True), 0.0)
                diagonal = exact_dot(diagonal, fold[...])
                for part in range(8):
                    exact[column // 4, part, column % 4 : column % 4 + 1, :NV] = diagonal[
                        part : part + 1
                    ]

            rounded = tile.astype(jnp.bfloat16)
            for part in range(8):
                tiles[part // 4, (part // 2) % 2, part % 2, first + u] = rounded[
                    part * NV : (part + 1) * NV
                ]

        for unit in units_of(column):
            step(unit, 0).start()

    def add_column(column):
        base, v, first = COLUMNS[column]
        for unit in units_of(column):
            step(unit, 2).wait_recv()
        diagonal = exact[column // 4, own_part]
        for e in range(7):
            diagonal = diagonal + exact_parts[e, column // 4]
        diagonal = exact_dot(diagonal[:, :NV], fold[...], 1)[column % 4 : column % 4 + 1]

        @pl.loop(0, v + 1)
        def _(u):
            integral = tiles[bit[2], bit[1], bit[0], first + u].astype(jnp.float32) + parts_3[
                first + u
            ].astype(jnp.float32)
            integral = jnp.where(own_diagonal & (u == v), diagonal, integral)
            kind = mask[base + v, pl.ds(base + u, 1), :]
            quotient = integral / (row_energy[base + u] + column_energy[base + v])
            amplitude = jnp.where(kind > 0, quotient, 0.0).astype(jnp.bfloat16)
            row_sums[base + u] = row_sums[base + u] + lax.dot_general(
                amplitude, amplitude, (((1,), (1,)), ((), ())), preferred_element_type=jnp.float32
            )
            stack[pl.ds(pl.multiple_of(u * NV, NV), NV), :] = jnp.where(
                kind > 1, quotient, 0.0
            ).astype(jnp.bfloat16)

        stacked = stack[: (v + 1) * NV, :]
        product = lax.dot_general(
            stacked, stacked, (((0,), (0,)), ((), ())), preferred_element_type=jnp.float32
        )
        slot_sums[(base + v) * ROWS : (base + v + 1) * ROWS, :] = jnp.dot(
            jnp.where(row_number // NV == column_number // NV, product, 0.0),
            fold[...],
            precision=lax.Precision.HIGHEST,
            preferred_element_type=jnp.float32,
        )

    def advance(column, phase):
        if column < 0:
            return
        act = (
            lambda: make_column(column),
            lambda: merge(column, 0),
            lambda: merge(column, 1),
            lambda: add_column(column),
        )[phase]
        when(LIMITS[column], own_bin, act)

    def receive(stream):
        arrived(stream)
        if stream + AHEAD < len(STREAMS):
            send_stream(stream + AHEAD)

    def start_exact(batch):
        for e in range(7, 0, -1):
            scatter_exact(e, batch).start()

    def wait_exact(batch):
        for e in range(1, 8):
            scatter_exact(e, batch).wait_recv()

    for column in range(PART_A):
        receive(column)
        if column == PART_A - 1:
            receive(PART_A)
        advance(column, 0)
        if column == 3:
            start_exact(0)
        advance(column - 1, 1)
        advance(column - 2, 2)
        if column == 3:
            wait_exact(0)
        advance(column - 3, 3)
    receive(len(STREAMS) - 1)
    settle()
    late = range(PART_A, GROUPS)
    for column in late:
        advance(column, 0)
    start_exact(1)
    for column in (PART_A - 1, *late):
        advance(column, 1)
    advance(PART_A - 2, 2)
    advance(PART_A - 3, 3)
    for column in (PART_A - 1, *late):
        advance(column, 2)
    wait_exact(1)
    for column in (PART_A - 2, PART_A - 1, *late):
        advance(column, 3)
    for group in range(GROUPS):
        part = pl.ds(pl.multiple_of(group * ROWS + own_part * NV, NV), NV)
        slot_sums[part, :] = slot_sums[part, :] + row_sums[group]

    for side in range(2):
        first_slot = side * PART_A * GROUP

        def add_slot(step, sums):
            slot = first_slot + step
            value = slot_sums[pl.ds(pl.multiple_of(slot * NV, NV), NV), :]
            result = []
            for i in range(3 * side, 3 * side + 3):
                own = (slot >= block_start[i]) & (slot < block_start[i] + block_slots[i])
                result.append(sums[i % 3] + jnp.where(own, value, jnp.zeros_like(value)))
            return tuple(result)

        zero = jnp.zeros((NV, NV), jnp.float32)
        sums = lax.fori_loop(0, (PART_A, PART_B)[side] * GROUP, add_slot, (zero, zero, zero))
        width = NV // SIDE
        for i in range(3):
            for g in range(SIDE):
                chunks[side * SIDE + g, i * CHUNK : i * CHUNK + width, :NV] = sums[i][
                    g * width : (g + 1) * width
                ]

    def scatter_chunk(e):
        part, target = peer(e)
        return pltpu.make_async_remote_copy(
            src_ref=chunks.at[part],
            dst_ref=chunk_parts.at[e - 1],
            send_sem=chunk_send.at[e - 1],
            recv_sem=chunk_recv.at[e - 1],
            device_id=target,
            device_id_type=MESH,
        )

    for e in range(7, 0, -1):
        scatter_chunk(e).start()
    for e in range(1, 8):
        scatter_chunk(e).wait_recv()
    total = chunks[own_part]
    for e in range(7):
        total = total + chunk_parts[e]
    pieces = [total[i * CHUNK : (i + 1) * CHUNK] for i in range(3)]
    turned = [pltpu.roll(piece, 64, 1) for piece in pieces]

    def send_home(target):
        return pltpu.make_async_remote_copy(
            src_ref=dense.at[target],
            dst_ref=homes.at[own_feed],
            send_sem=home_send.at[target],
            recv_sem=home_recv.at[own_feed],
            device_id=(quarter, target),
            device_id_type=MESH,
        )

    def away(target):
        return (quarter != z) | (target != aux)

    @pl.loop(0, owners)
    def _(target):
        message = jnp.zeros((CHUNK, 128), jnp.float32)
        for i in range(3):
            block = jnp.where(half == 0, block_id[i], block_id[3 + i])
            message = message + jnp.where(block == 2 * target, pieces[i], 0.0)
            message = message + jnp.where(block == 2 * target + 1, turned[i], 0.0)
        dense[target] = message

        @pl.when(away(target))
        def _():
            send_home(target).start()

    @pl.when(quarter == z)
    def _():
        homes[own_feed] = dense[aux]

    @pl.loop(0, owners)
    def _(index):
        @pl.when((quarter != z) | (index != own_feed))
        def _():
            pltpu.make_async_copy(homes.at[index], homes.at[index], home_recv.at[index]).wait()

    out[...] = jnp.sum(homes[...], axis=0)

    @pl.loop(0, owners)
    def _(target):
        @pl.when(away(target))
        def _():
            send_home(target).wait_send()

    for e in range(1, 8):
        scatter_chunk(e).wait_send()

    def sent_column(column):
        for unit in units_of(column):
            for phase in range(3):
                step(unit, phase).wait_send()

    for column in range(GROUPS):
        when(LIMITS[column], own_bin, lambda: sent_column(column))
    for batch in range(2):
        for e in range(1, 8):
            scatter_exact(e, batch).wait_send()
    for stream in range(len(STREAMS)):
        gather(0, 1 - core, stream, lambda copy: copy.wait_send())

        @pl.loop(2, BINS)
        def _(index):
            gather(index // 2, lax.rem(index, 2), stream, lambda copy: copy.wait_send())


def binned(
    bin_of,
    base,
    offset,
    load,
    place,
    second,
    three_index,
    block_owner,
    pair_screen,
    orbital_counts,
    occupied_energy,
    virtual_energy,
):
    blocks, row_count, aux_local = three_index.shape
    block_ids = jnp.arange(blocks, dtype=jnp.int32)
    sent_ids = jnp.arange(SENT, dtype=jnp.int32)[:, None] - (base + offset)[None, :]
    bins = jnp.arange(BINS, dtype=jnp.int32)
    origin = jnp.sum(
        jnp.where(
            (bin_of[None, None, :] == bins[:, None, None])
            & ((sent_ids >= 0) & (sent_ids < orbital_counts[None, :]))[None],
            (block_ids[None, :] * OB + sent_ids)[None],
            0,
        ),
        axis=2,
    )
    start = base + jnp.where(second, PART_A * GROUP, 0)
    meta = jnp.stack([bin_of, start, orbital_counts, place, second.astype(jnp.int32)] + [base] * 3)
    owners = lax.axis_size("aux")
    home = pl.pallas_call(
        kernel,
        out_shape=jax.ShapeDtypeStruct((CHUNK, 128), jnp.float32),
        in_specs=[SMEM, SMEM, ANY, VMEM, VMEM, VMEM, VMEM],
        out_specs=VMEM,
        scratch_shapes=[
            pltpu.VMEM((blocks * OB, NV, aux_local), jnp.bfloat16),
            pltpu.VMEM((BINS, SENT, NV, aux_local), jnp.bfloat16),
            pltpu.VMEM((BINS, SENT + PART_B * GROUP, NV, aux_local), jnp.bfloat16),
            pltpu.VMEM((2, 2, 2, TILES, NV, ROWS), jnp.bfloat16),
            pltpu.VMEM((2, 2, TILES, NV, ROWS), jnp.bfloat16),
            pltpu.VMEM((2, TILES, NV, ROWS), jnp.bfloat16),
            pltpu.VMEM((TILES, NV, ROWS), jnp.bfloat16),
            pltpu.VMEM((2, 8, 8, 128), jnp.float32),
            pltpu.VMEM((7, 2, 8, 128), jnp.float32),
            pltpu.VMEM((PART_A * NV, ROWS), jnp.bfloat16),
            pltpu.VMEM((GROUPS, NV, NV), jnp.float32),
            pltpu.VMEM((SLOTS * NV, NV), jnp.float32),
            pltpu.VMEM((ROWS, NV), jnp.float32),
            pltpu.VMEM((8, 3 * CHUNK, 128), jnp.float32),
            pltpu.VMEM((7, 3 * CHUNK, 128), jnp.float32),
            pltpu.VMEM((owners, CHUNK, 128), jnp.float32),
            pltpu.VMEM((owners, CHUNK, 128), jnp.float32),
            pltpu.VMEM((GROUPS, NV, 1), jnp.float32),
            pltpu.VMEM((GROUPS, 1, ROWS), jnp.float32),
            pltpu.VMEM((GROUPS, GROUPS, ROWS), jnp.float32),
            pltpu.SemaphoreType.DMA((8,)),
            pltpu.SemaphoreType.DMA((len(STREAMS),)),
            pltpu.SemaphoreType.DMA((BINS, len(STREAMS))),
            pltpu.SemaphoreType.DMA((BINS, len(STREAMS))),
            pltpu.SemaphoreType.DMA((len(UNITS), 3)),
            pltpu.SemaphoreType.DMA((len(UNITS), 3)),
            pltpu.SemaphoreType.DMA((7, 2)),
            pltpu.SemaphoreType.DMA((7, 2)),
            pltpu.SemaphoreType.DMA((7,)),
            pltpu.SemaphoreType.DMA((7,)),
            pltpu.SemaphoreType.DMA((owners,)),
            pltpu.SemaphoreType.DMA((owners,)),
        ],
        compiler_params=pltpu.CompilerParams(
            collective_id=0, has_side_effects=True, vmem_limit_bytes=60 * 2**20
        ),
    )(
        origin.reshape(-1),
        meta,
        three_index.reshape(blocks * OB, NV, aux_local),
        meta,
        pair_screen,
        occupied_energy.T,
        virtual_energy.T,
    )
    return home.reshape(CHUNK, 2, 64)[: NV // SIDE, :, :NV].transpose(1, 0, 2)


def local(three_index, block_owner, pair_screen, orbital_counts, occupied_energy, virtual_energy):
    *spots, fits = plan(block_owner, orbital_counts)
    arguments = (
        three_index,
        block_owner,
        pair_screen,
        orbital_counts,
        occupied_energy,
        virtual_energy,
    )
    return lax.cond(
        fits,
        lambda: binned(*spots, *arguments),
        lambda: general(*arguments),
    )


def solution(mesh):
    in_specs = (P(None, None, ("grp", "aux")), P(), P(), P(), P(), P())
    out_specs = P("aux", "grp", None)
    return jax.shard_map(local, mesh=mesh, in_specs=in_specs, out_specs=out_specs, check_vma=False)
```

```python
import jax
import jax.numpy as jnp
from jax import lax
from jax.experimental import pallas as pl
from jax.experimental.pallas import tpu as pltpu
from jax.sharding import PartitionSpec as P

CAP = 3


def slot_tiles(source, slot_block, slot_valid, owners):
    picked = jnp.take(source, slot_block.reshape(-1), axis=0)
    picked = picked.reshape(owners, CAP, source.shape[1], source.shape[2])
    return jnp.where(slot_valid[:, :, None, None] > 0, picked, jnp.zeros_like(picked))


def pair_block(received, first, second):
    return lax.dot_general(
        lax.dynamic_index_in_dim(received, first, 1, False),
        lax.dynamic_index_in_dim(received, second, 1, False),
        (((0, 2), (0, 2)), ((), ())),
        preferred_element_type=jnp.float32,
    )


def general(three_index, block_owner, pair_screen, orbital_counts, occupied_energy, virtual_energy):
    block_count, row_count, aux_local = three_index.shape
    occupied_width = occupied_energy.shape[1]
    virtual_width = virtual_energy.shape[1]
    groups = lax.axis_size("grp")
    owners = lax.axis_size("aux")
    own_index = lax.axis_index("aux")
    group_index = lax.axis_index("grp")
    quarter = row_count // groups
    owner_ids = jnp.arange(owners, dtype=jnp.int32)
    owned = (block_owner[None, :] == owner_ids[:, None]).astype(jnp.int32)
    slot_rank = jnp.cumsum(owned, axis=1) - 1
    slot_ids = jnp.arange(CAP, dtype=jnp.int32)
    selection = owned[:, None, :] * (slot_rank[:, None, :] == slot_ids[None, :, None]).astype(
        jnp.int32
    )
    block_ids = jnp.arange(block_count, dtype=jnp.int32)
    slot_block = jnp.sum(selection * block_ids[None, None, :], axis=2)
    slot_valid = jnp.sum(selection, axis=2)
    mine = lax.dynamic_index_in_dim(selection, own_index, 0, keepdims=False)
    my_block = jnp.sum(mine * block_ids[None, :], axis=1)
    my_valid = jnp.sum(mine, axis=1)
    energy = (virtual_energy[:, None, :] - occupied_energy[:, :, None]).reshape(
        block_count, row_count
    )
    occupied_flags = (
        jnp.arange(occupied_width, dtype=jnp.int32)[None, :] < orbital_counts[:, None]
    ).astype(jnp.float32)
    occupancy = jnp.repeat(occupied_flags, virtual_width, axis=1)
    slot_energy = jnp.take(energy, my_block, axis=0)
    slot_occupancy = jnp.take(occupancy, my_block, axis=0)
    screened = jnp.take(jnp.take(pair_screen, my_block, axis=0), my_block, axis=1)
    is_live = screened * my_valid[:, None] * my_valid[None, :] > 0

    def slot_amplitude(integral, first, second):
        energy_rows = lax.dynamic_slice_in_dim(slot_energy[first], group_index * quarter, quarter)
        occupied_rows = lax.dynamic_slice_in_dim(
            slot_occupancy[first], group_index * quarter, quarter
        )
        divisor = energy_rows[:, None] + slot_energy[second][None, :]
        return (
            occupied_rows[:, None] * slot_occupancy[second][None, :] * integral / divisor
        ).astype(jnp.bfloat16)

    def own_density(amplitude):
        row_form = amplitude.reshape(quarter // virtual_width, virtual_width, row_count)
        return jnp.einsum("iax,ibx->ab", row_form, row_form, preferred_element_type=jnp.float32)

    outgoing = slot_tiles(three_index, slot_block, slot_valid, owners)
    received = lax.all_to_all(outgoing, "aux", split_axis=0, concat_axis=0, tiled=True)
    empty = jnp.zeros((virtual_width, virtual_width), jnp.float32)

    def one_pair(parts, pair):
        first = pair // CAP
        second = pair % CAP
        integral = pair_block(received, first, second)
        sent = integral.reshape(groups, quarter, row_count)
        summed = jnp.sum(lax.all_to_all(sent, "grp", 0, 0, tiled=True), axis=0)
        part = own_density(slot_amplitude(summed, first, second))
        part = jnp.where(is_live[first, second], part, empty)
        return parts.at[first].add(part), None

    slot_parts, _ = lax.scan(
        one_pair,
        jnp.zeros((CAP, virtual_width, virtual_width), jnp.float32),
        jnp.arange(CAP * CAP, dtype=jnp.int32),
    )
    spread = slot_parts.reshape(CAP, groups, virtual_width // groups, virtual_width)
    placed = jnp.einsum(
        "cb,cgxy->gbxy", mine.astype(jnp.float32), spread, precision=lax.Precision.HIGHEST
    )
    placed = placed.reshape(groups, owners, block_count // owners, virtual_width // groups, virtual_width)
    placed = jnp.sum(lax.all_to_all(placed, "grp", 0, 0, tiled=True), axis=0)
    return jnp.sum(lax.all_to_all(placed, "aux", 0, 0, tiled=True), axis=0)


NV = 48
OB = 16
BINS = 16
GROUP = 8
ROWS = GROUP * NV
SIDE = 4
PART_A = 6
PART_B = 2
GROUPS = PART_A + PART_B
SLOTS = GROUPS * GROUP
CHUNK = 16
ALL = (0, BINS)
LIMITS = (ALL, ALL, ALL, (0, 15), (0, 9), (0, 4), ALL, (2, BINS))
STREAMS = tuple((GROUP * k, GROUP, ALL) for k in range(5)) + (
    (40, 4, ALL),
    (44, 4, (0, 8)),
    (48, 4, (0, 4)),
)
SENT = 52
AHEAD = 2
COLUMNS = tuple(
    [(0, v, v * (v + 1) // 2) for v in range(PART_A)]
    + [(PART_A, v, PART_A * (PART_A + 1) // 2 + v * (v + 1) // 2) for v in range(PART_B)]
)
TILES = PART_A * (PART_A + 1) // 2 + PART_B * (PART_B + 1) // 2
UNITS = []
for column, (base, v, first) in enumerate(COLUMNS):
    for skip in range(0, v + 1, 2):
        turn = len(UNITS) % 3
        UNITS.append(
            (column, first + skip, min(2, v + 1 - skip), (turn, (turn + 1) % 3, (turn + 2) % 3))
        )
BITS = [(d % 2, (d // 2) % 2, d // 4) for d in range(8)]
MESH = pl.DeviceIdType.MESH
VMEM = pl.BlockSpec(memory_space=pltpu.VMEM)
SMEM = pl.BlockSpec(memory_space=pltpu.SMEM)
ANY = pl.BlockSpec(memory_space=pl.ANY)


def has(limits, index):
    first, end = limits
    return (index >= first) & (index < end)


def plan(block_owner, orbital_counts):
    ids = jnp.arange(block_owner.shape[0], dtype=jnp.int32)
    same = block_owner[:, None] == block_owner[None, :]
    earlier = same & (ids[None, :] < ids[:, None])
    load = jnp.sum(jnp.where(same, orbital_counts[None, :], 0), axis=1)
    base = jnp.sum(jnp.where(earlier, orbital_counts[None, :], 0), axis=1)
    place = jnp.sum(earlier.astype(jnp.int32), axis=1)
    ahead = (load[None, :] > load[:, None]) | (
        (load[None, :] == load[:, None]) & (block_owner[None, :] < block_owner[:, None])
    )
    rank = jnp.sum((ahead & (place == 0)[None, :]).astype(jnp.int32), axis=1)
    second = rank >= BINS
    bin_of = jnp.where(second, 2 * BINS - 1 - rank, rank)
    ahead_load = jnp.sum(
        jnp.where(
            (place == 0)[None, :] & (rank[None, :] == 2 * BINS - 1 - rank[:, None]), load[None, :], 0
        ),
        axis=1,
    )
    room = jnp.zeros_like(load)
    for group, limits in enumerate(LIMITS):
        room = room + jnp.where(second == (group >= PART_A), has(limits, bin_of) * GROUP, 0)
    sent = sum(has(limits, bin_of) * number for first, number, limits in STREAMS)
    fits = jnp.all((load <= room) & (load + ahead_load <= sent))
    return bin_of, base, jnp.where(second, ahead_load, 0), load, place, second, fits


def position():
    z = lax.axis_index("grp")
    aux = lax.axis_index("aux")
    core = lax.rem(aux, 2)
    x = lax.rem(aux // 2, SIDE)
    y = aux // (2 * SIDE)
    return x, y, z, core


def device(x, y, z, core):
    return (z, (y * SIDE + x) * 2 + core)


def bin_index(x, y, z, core):
    kind = lax.rem(x, 2) + 2 * lax.rem(y, 2) + 4 * lax.rem(z, 2)
    return kind + core * (BINS - 1 - 2 * kind)


def part_index(x, y, z):
    return x // 2 + 2 * (y // 2) + 4 * (z // 2)


def shifted(value, by):
    return lax.rem(value + by + SIDE, SIDE)


def kernel(
    origin_ref,
    meta_ref,
    source,
    meta,
    screen,
    occupied_energy,
    virtual_energy,
    out,
    whole,
    packed,
    held,
    tiles,
    parts_1,
    parts_2,
    parts_3,
    exact,
    exact_parts,
    stack,
    row_sums,
    slot_sums,
    fold,
    chunks,
    chunk_parts,
    dense,
    homes,
    row_energy,
    column_energy,
    mask,
    load_sem,
    local_sem,
    send_sem,
    recv_sem,
    tile_send,
    tile_recv,
    exact_send,
    exact_recv,
    chunk_send,
    chunk_recv,
    home_send,
    home_recv,
):
    x, y, z, core = position()
    aux = lax.axis_index("aux")
    owners = lax.axis_size("aux")
    sign = 1 - 2 * core
    own_bin = bin_index(x, y, z, core)
    own_part = part_index(x, y, z)
    quarter = lax.rem(own_part, SIDE)
    half = own_part // SIDE

    pieces = load_sem.shape[0]
    size = source.shape[0] // pieces

    def load(piece):
        part = pl.ds(piece * size, size)
        return pltpu.make_async_copy(source.at[part], whole.at[part], load_sem.at[piece])

    for piece in range(pieces):
        load(piece).start()

    barrier = pltpu.get_barrier_semaphore()

    def greet(target):
        pl.semaphore_signal(barrier, inc=1, device_id=target, device_id_type=MESH)

    greet(device(x, y, z, 1 - core))
    for d in range(1, 8):
        dx, dy, dz = BITS[d]
        greet(device(shifted(x, -dx), shifted(y, -dy), shifted(z, -dz), 0))
        greet(device(shifted(x, dx), shifted(y, dy), shifted(z, dz), 1))
        greet(device(shifted(x, 2 * dx), shifted(y, 2 * dy), shifted(z, 2 * dz), core))

    def feeder(index):
        number = index // 2
        feed_core = number // 8
        kind = number + feed_core * (BINS - 1 - 2 * number)
        return (
            lax.rem(kind, 2) + 2 * lax.rem(z, 2),
            lax.rem(kind // 2, 2) + 2 * (z // 2),
            kind // 4 + 2 * lax.rem(index, 2),
            feed_core,
        )

    own_feed = own_bin * 2 + half

    @pl.loop(0, owners)
    def _(index):
        @pl.when((quarter != z) | (index != own_feed))
        def _():
            greet(device(*feeder(index)))

    fold[...] = (
        lax.rem(lax.broadcasted_iota(jnp.int32, (ROWS, NV), 0), NV)
        == lax.broadcasted_iota(jnp.int32, (ROWS, NV), 1)
    ).astype(jnp.bfloat16)
    slot_sums[...] = jnp.zeros_like(slot_sums)
    row_sums[...] = jnp.zeros_like(row_sums)
    chunks[...] = jnp.zeros_like(chunks)

    for piece in range(pieces):
        load(piece).wait()
    pl.semaphore_wait(barrier, 22 + owners - (quarter == z).astype(jnp.int32))

    def when(limits, index, act):
        if limits == ALL:
            act()
        else:
            pl.when(has(limits, index))(act)

    def slots(stream):
        first, number, limits = STREAMS[stream]
        return pl.ds(first, number)

    def gather(d, target_core, stream, act):
        dx, dy, dz = d % 2, (d // 2) % 2, d // 4
        tx, ty, tz = shifted(x, sign * dx), shifted(y, sign * dy), shifted(z, sign * dz)
        target_bin = bin_index(tx, ty, tz, target_core)
        copy = pltpu.make_async_remote_copy(
            src_ref=packed.at[target_bin, slots(stream)],
            dst_ref=held.at[2 * d + core, slots(stream)],
            send_sem=send_sem.at[2 * d + target_core, stream],
            recv_sem=recv_sem.at[2 * d + core, stream],
            device_id=device(tx, ty, tz, target_core),
            device_id_type=MESH,
        )
        when(STREAMS[stream][2], target_bin, lambda: act(copy))

    def keep(stream):
        return pltpu.make_async_copy(
            packed.at[own_bin, slots(stream)], held.at[core, slots(stream)], local_sem.at[stream]
        )

    def send_stream(stream):
        first_slot, number_of_slots, limits = STREAMS[stream]

        @pl.loop(0, BINS)
        def _(number):
            for slot in range(first_slot, first_slot + number_of_slots):
                origin = origin_ref[number * SENT + slot]
                packed[number, slot] = whole[origin]

        @pl.loop(0, 14)
        def _(index):
            gather(7 - index // 2, lax.rem(index, 2), stream, lambda copy: copy.start())

        gather(0, 1 - core, stream, lambda copy: copy.start())
        when(limits, own_bin, lambda: keep(stream).start())

    for stream in range(AHEAD):
        send_stream(stream)

    def arrived(stream):
        def wait_all():
            keep(stream).wait()

            @pl.loop(2, BINS)
            def _(sender):
                part = held.at[sender, slots(stream)]
                pltpu.make_async_copy(part, part, recv_sem.at[sender, stream]).wait()

            part = held.at[1 - core, slots(stream)]
            pltpu.make_async_copy(part, part, recv_sem.at[1 - core, stream]).wait()

        when(STREAMS[stream][2], own_bin, wait_all)

    row_number = lax.broadcasted_iota(jnp.int32, (ROWS, ROWS), 0)
    column_number = lax.broadcasted_iota(jnp.int32, (ROWS, ROWS), 1)
    own_diagonal = (
        lax.broadcasted_iota(jnp.int32, (NV, ROWS), 0) + own_part * NV
        == lax.broadcasted_iota(jnp.int32, (NV, ROWS), 1)
    )
    same_slot = (
        lax.broadcasted_iota(jnp.int32, (GROUP, ROWS), 1) // NV
        == lax.broadcasted_iota(jnp.int32, (GROUP, ROWS), 0)
    )

    def exact_dot(left, right, axis=0):
        return lax.dot_general(
            left,
            right,
            (((1,), (axis,)), ((), ())),
            precision=lax.Precision.HIGHEST,
            preferred_element_type=jnp.float32,
        )

    def fold_dot(left, axis=0):
        total = 0.0
        for _ in range(3):
            piece = left.astype(jnp.bfloat16)
            left = left - piece.astype(jnp.float32)
            total = total + lax.dot_general(
                piece, fold[...], (((1,), (axis,)), ((), ())), preferred_element_type=jnp.float32
            )
        return total

    blocks = meta.shape[1]
    slot_number = lax.broadcasted_iota(jnp.int32, (SLOTS, blocks), 0)
    orbital = slot_number - meta[1:2, :]
    inside = (meta[0:1, :] == own_bin) & (orbital >= 0) & (orbital < meta[2:3, :])
    pick = jnp.where(inside, 1.0, 0.0)
    slot_orbital = jnp.sum(jnp.where(inside, orbital, 0), axis=1, keepdims=True)
    occupied = exact_dot(pick, occupied_energy[...], 1)
    occupied = jnp.where(
        lax.broadcasted_iota(jnp.int32, (SLOTS, OB), 1) == slot_orbital, occupied, 0.0
    )
    energy = exact_dot(pick, virtual_energy[...], 1) - jnp.sum(occupied, axis=1, keepdims=True)
    row_slot = lax.broadcasted_iota(jnp.int32, (GROUPS, SLOTS), 0) * GROUP + own_part
    column_slot = lax.broadcasted_iota(jnp.int32, (GROUPS, SLOTS), 1)
    row_pick = exact_dot(jnp.where(row_slot == column_slot, 1.0, 0.0), pick)
    live = exact_dot(exact_dot(row_pick, jnp.where(screen[...] == 1, 1.0, 0.0)), pick, 1)
    order = jnp.where(row_slot < column_slot, 2.0, jnp.where(row_slot == column_slot, 1.0, 0.0))
    kind = jnp.where(live > 0.5, order, 0.0)
    for group in range(GROUPS):
        lanes = fold_dot(energy[group * GROUP : (group + 1) * GROUP], 1)
        lanes = jnp.sum(jnp.where(same_slot, lanes, 0.0), axis=0, keepdims=True)
        column_energy[group] = lanes
        row_energy[group] = jnp.sum(jnp.where(own_diagonal, lanes, 0.0), axis=1, keepdims=True)
        wide = lax.broadcasted_iota(jnp.int32, (SLOTS, ROWS), 0) == (
            group * GROUP + lax.broadcasted_iota(jnp.int32, (SLOTS, ROWS), 1) // NV
        )
        mask[group] = jnp.dot(
            kind.astype(jnp.bfloat16),
            jnp.where(wide, 1.0, 0.0).astype(jnp.bfloat16),
            preferred_element_type=jnp.float32,
        )

    def find(block, found):
        result = []
        for index in range(6):
            hit = (
                (meta_ref[0, block] == own_bin)
                & (meta_ref[3, block] == index % 3)
                & (meta_ref[4, block] == index // 3)
            )
            old = found[3 * index : 3 * index + 3]
            new = (meta_ref[1, block], meta_ref[2, block], block)
            result += [jnp.where(hit, n, o) for n, o in zip(new, old)]
        return tuple(result)

    nothing = jnp.int32(0)
    found = lax.fori_loop(0, blocks, find, (nothing, nothing, jnp.int32(-1)) * 6)
    block_start, block_slots, block_id = found[0::3], found[1::3], found[2::3]

    def settle():
        offset = block_slots[0] + block_slots[1] + block_slots[2]

        @pl.loop(0, BINS)
        def _(sender):
            for slot in range(PART_B * GROUP):
                held[sender, SENT + slot] = held[sender, offset + slot]

    def rows_of(base, group):
        first = group * GROUP + (SENT if base else 0)
        return jnp.concatenate(
            [
                held[sender, pl.ds(first, GROUP)].reshape(ROWS, held.shape[-1])
                for sender in range(BINS)
            ],
            axis=1,
        )

    def peer(e):
        dx, dy, dz = BITS[e]
        px, py, pz = shifted(x, 2 * dx), shifted(y, 2 * dy), shifted(z, 2 * dz)
        return part_index(px, py, pz), device(px, py, pz, core)

    bit = (x // 2, y // 2, z // 2)

    def view(fixed):
        return tuple(fixed.get(axis, slice(None)) for axis in (2, 1, 0))

    def step(unit, phase):
        column, first, number, order = UNITS[unit]
        fixed = {axis: bit[axis] for axis in order[:phase]}
        axis = order[phase]
        fixed[axis] = 1 - bit[axis]
        run = pl.ds(first, number)
        far = [shifted(c, 2 * (axis == k)) for k, c in enumerate((x, y, z))]
        landing = (parts_1.at[:, :, run], parts_2.at[:, run], parts_3.at[run])[phase]
        return pltpu.make_async_remote_copy(
            src_ref=tiles.at[view(fixed) + (run,)],
            dst_ref=landing,
            send_sem=tile_send.at[unit, phase],
            recv_sem=tile_recv.at[unit, phase],
            device_id=device(*far, core),
            device_id_type=MESH,
        )

    def units_of(column):
        return [unit for unit in range(len(UNITS)) if UNITS[unit][0] == column]

    def merge(column, phase):
        for unit in units_of(column):
            _, first, number, order = UNITS[unit]
            step(unit, phase).wait_recv()
            fixed = {axis: bit[axis] for axis in order[: phase + 1]}
            rest = [axis for axis in (2, 1, 0) if axis not in fixed]
            landed = (parts_1, parts_2)[phase]

            @pl.loop(first, first + number)
            def _(index):
                for choice in range(2 ** len(rest)):
                    at = tuple((choice // 2**k) % 2 for k in range(len(rest)))
                    place = view({**fixed, **dict(zip(rest, at))}) + (index,)
                    tiles[place] = (
                        tiles[place].astype(jnp.float32) + landed[at + (index,)].astype(jnp.float32)
                    ).astype(jnp.bfloat16)

            step(unit, phase + 1).start()

    def scatter_exact(e, batch):
        part, target = peer(e)
        return pltpu.make_async_remote_copy(
            src_ref=exact.at[batch, part],
            dst_ref=exact_parts.at[e - 1, batch],
            send_sem=exact_send.at[e - 1, batch],
            recv_sem=exact_recv.at[e - 1, batch],
            device_id=target,
            device_id_type=MESH,
        )

    def make_column(column):
        base, v, first = COLUMNS[column]

        @pl.loop(0, v + 1)
        def _(u):
            tile = lax.dot_general(
                rows_of(base, u),
                rows_of(base, v),
                (((1,), (1,)), ((), ())),
                preferred_element_type=jnp.float32,
            )

            @pl.when(u == v)
            def _():
                diagonal = jnp.where(row_number == column_number, tile, 0.0)
                diagonal = jnp.where(same_slot, jnp.sum(diagonal, axis=0, keepdims=True), 0.0)
                diagonal = fold_dot(diagonal)
                for part in range(8):
                    exact[column // 4, part, column % 4 : column % 4 + 1, :NV] = diagonal[
                        part : part + 1
                    ]

            rounded = tile.astype(jnp.bfloat16)
            for part in range(8):
                tiles[part // 4, (part // 2) % 2, part % 2, first + u] = rounded[
                    part * NV : (part + 1) * NV
                ]

        for unit in units_of(column):
            step(unit, 0).start()

    def add_column(column):
        base, v, first = COLUMNS[column]
        for unit in units_of(column):
            step(unit, 2).wait_recv()
        diagonal = exact[column // 4, own_part]
        for e in range(7):
            diagonal = diagonal + exact_parts[e, column // 4]
        diagonal = fold_dot(diagonal[:, :NV], 1)[column % 4 : column % 4 + 1]

        @pl.loop(0, v + 1)
        def _(u):
            integral = tiles[bit[2], bit[1], bit[0], first + u].astype(jnp.float32) + parts_3[
                first + u
            ].astype(jnp.float32)
            integral = jnp.where(own_diagonal & (u == v), diagonal, integral)
            kind = mask[base + v, pl.ds(base + u, 1), :]
            quotient = integral / (row_energy[base + u] + column_energy[base + v])
            amplitude = jnp.where(kind > 0, quotient, 0.0).astype(jnp.bfloat16)
            row_sums[base + u] = row_sums[base + u] + lax.dot_general(
                amplitude, amplitude, (((1,), (1,)), ((), ())), preferred_element_type=jnp.float32
            )
            stack[pl.ds(pl.multiple_of(u * NV, NV), NV), :] = jnp.where(
                kind > 1, quotient, 0.0
            ).astype(jnp.bfloat16)

        stacked = stack[: (v + 1) * NV, :]
        product = lax.dot_general(
            stacked, stacked, (((0,), (0,)), ((), ())), preferred_element_type=jnp.float32
        )
        slot_sums[(base + v) * ROWS : (base + v + 1) * ROWS, :] = fold_dot(
            jnp.where(row_number // NV == column_number // NV, product, 0.0)
        )

    def advance(column, phase):
        if column < 0:
            return
        act = (
            lambda: make_column(column),
            lambda: merge(column, 0),
            lambda: merge(column, 1),
            lambda: add_column(column),
        )[phase]
        when(LIMITS[column], own_bin, act)

    def receive(stream):
        arrived(stream)
        if stream + AHEAD < len(STREAMS):
            send_stream(stream + AHEAD)

    def start_exact(batch):
        for e in range(7, 0, -1):
            scatter_exact(e, batch).start()

    def wait_exact(batch):
        for e in range(1, 8):
            scatter_exact(e, batch).wait_recv()

    for column in range(PART_A):
        receive(column)
        if column == PART_A - 1:
            receive(PART_A)
        advance(column, 0)
        if column == 3:
            start_exact(0)
        advance(column - 1, 1)
        advance(column - 2, 2)
        if column == 3:
            wait_exact(0)
        advance(column - 3, 3)
    receive(len(STREAMS) - 1)
    settle()
    late = range(PART_A, GROUPS)
    for column in late:
        advance(column, 0)
    start_exact(1)
    for column in (PART_A - 1, *late):
        advance(column, 1)
    advance(PART_A - 2, 2)
    advance(PART_A - 3, 3)
    for column in (PART_A - 1, *late):
        advance(column, 2)
    wait_exact(1)
    for column in (PART_A - 2, PART_A - 1, *late):
        advance(column, 3)
    for group in range(GROUPS):
        part = pl.ds(pl.multiple_of(group * ROWS + own_part * NV, NV), NV)
        slot_sums[part, :] = slot_sums[part, :] + row_sums[group]

    for side in range(2):
        first_slot = side * PART_A * GROUP

        def add_slot(step, sums):
            slot = first_slot + step
            value = slot_sums[pl.ds(pl.multiple_of(slot * NV, NV), NV), :]
            result = []
            for i in range(3 * side, 3 * side + 3):
                own = (slot >= block_start[i]) & (slot < block_start[i] + block_slots[i])
                result.append(sums[i % 3] + jnp.where(own, value, jnp.zeros_like(value)))
            return tuple(result)

        zero = jnp.zeros((NV, NV), jnp.float32)
        sums = lax.fori_loop(0, (PART_A, PART_B)[side] * GROUP, add_slot, (zero, zero, zero))
        width = NV // SIDE
        for i in range(3):
            for g in range(SIDE):
                chunks[side * SIDE + g, i * CHUNK : i * CHUNK + width, :NV] = sums[i][
                    g * width : (g + 1) * width
                ]

    def scatter_chunk(e):
        part, target = peer(e)
        return pltpu.make_async_remote_copy(
            src_ref=chunks.at[part],
            dst_ref=chunk_parts.at[e - 1],
            send_sem=chunk_send.at[e - 1],
            recv_sem=chunk_recv.at[e - 1],
            device_id=target,
            device_id_type=MESH,
        )

    for e in range(7, 0, -1):
        scatter_chunk(e).start()
    for e in range(1, 8):
        scatter_chunk(e).wait_recv()
    total = chunks[own_part]
    for e in range(7):
        total = total + chunk_parts[e]
    pieces = [total[i * CHUNK : (i + 1) * CHUNK] for i in range(3)]
    turned = [pltpu.roll(piece, 64, 1) for piece in pieces]

    def send_home(target):
        return pltpu.make_async_remote_copy(
            src_ref=dense.at[target],
            dst_ref=homes.at[own_feed],
            send_sem=home_send.at[target],
            recv_sem=home_recv.at[own_feed],
            device_id=(quarter, target),
            device_id_type=MESH,
        )

    def away(target):
        return (quarter != z) | (target != aux)

    @pl.loop(0, owners)
    def _(target):
        message = jnp.zeros((CHUNK, 128), jnp.float32)
        for i in range(3):
            block = jnp.where(half == 0, block_id[i], block_id[3 + i])
            message = message + jnp.where(block == 2 * target, pieces[i], 0.0)
            message = message + jnp.where(block == 2 * target + 1, turned[i], 0.0)
        dense[target] = message

        @pl.when(away(target))
        def _():
            send_home(target).start()

    @pl.when(quarter == z)
    def _():
        homes[own_feed] = dense[aux]

    @pl.loop(0, owners)
    def _(index):
        @pl.when((quarter != z) | (index != own_feed))
        def _():
            pltpu.make_async_copy(homes.at[index], homes.at[index], home_recv.at[index]).wait()

    out[...] = jnp.sum(homes[...], axis=0)

    @pl.loop(0, owners)
    def _(target):
        @pl.when(away(target))
        def _():
            send_home(target).wait_send()

    for e in range(1, 8):
        scatter_chunk(e).wait_send()

    def sent_column(column):
        for unit in units_of(column):
            for phase in range(3):
                step(unit, phase).wait_send()

    for column in range(GROUPS):
        when(LIMITS[column], own_bin, lambda: sent_column(column))
    for batch in range(2):
        for e in range(1, 8):
            scatter_exact(e, batch).wait_send()
    for stream in range(len(STREAMS)):
        gather(0, 1 - core, stream, lambda copy: copy.wait_send())

        @pl.loop(2, BINS)
        def _(index):
            gather(index // 2, lax.rem(index, 2), stream, lambda copy: copy.wait_send())


def binned(
    bin_of,
    base,
    offset,
    load,
    place,
    second,
    three_index,
    block_owner,
    pair_screen,
    orbital_counts,
    occupied_energy,
    virtual_energy,
):
    blocks, row_count, aux_local = three_index.shape
    block_ids = jnp.arange(blocks, dtype=jnp.int32)
    sent_ids = jnp.arange(SENT, dtype=jnp.int32)[:, None] - (base + offset)[None, :]
    bins = jnp.arange(BINS, dtype=jnp.int32)
    origin = jnp.sum(
        jnp.where(
            (bin_of[None, None, :] == bins[:, None, None])
            & ((sent_ids >= 0) & (sent_ids < orbital_counts[None, :]))[None],
            (block_ids[None, :] * OB + sent_ids)[None],
            0,
        ),
        axis=2,
    )
    start = base + jnp.where(second, PART_A * GROUP, 0)
    meta = jnp.stack([bin_of, start, orbital_counts, place, second.astype(jnp.int32)] + [base] * 3)
    owners = lax.axis_size("aux")
    home = pl.pallas_call(
        kernel,
        out_shape=jax.ShapeDtypeStruct((CHUNK, 128), jnp.float32),
        in_specs=[SMEM, SMEM, ANY, VMEM, VMEM, VMEM, VMEM],
        out_specs=VMEM,
        scratch_shapes=[
            pltpu.VMEM((blocks * OB, NV, aux_local), jnp.bfloat16),
            pltpu.VMEM((BINS, SENT, NV, aux_local), jnp.bfloat16),
            pltpu.VMEM((BINS, SENT + PART_B * GROUP, NV, aux_local), jnp.bfloat16),
            pltpu.VMEM((2, 2, 2, TILES, NV, ROWS), jnp.bfloat16),
            pltpu.VMEM((2, 2, TILES, NV, ROWS), jnp.bfloat16),
            pltpu.VMEM((2, TILES, NV, ROWS), jnp.bfloat16),
            pltpu.VMEM((TILES, NV, ROWS), jnp.bfloat16),
            pltpu.VMEM((2, 8, 8, 128), jnp.float32),
            pltpu.VMEM((7, 2, 8, 128), jnp.float32),
            pltpu.VMEM((PART_A * NV, ROWS), jnp.bfloat16),
            pltpu.VMEM((GROUPS, NV, NV), jnp.float32),
            pltpu.VMEM((SLOTS * NV, NV), jnp.float32),
            pltpu.VMEM((ROWS, NV), jnp.bfloat16),
            pltpu.VMEM((8, 3 * CHUNK, 128), jnp.float32),
            pltpu.VMEM((7, 3 * CHUNK, 128), jnp.float32),
            pltpu.VMEM((owners, CHUNK, 128), jnp.float32),
            pltpu.VMEM((owners, CHUNK, 128), jnp.float32),
            pltpu.VMEM((GROUPS, NV, 1), jnp.float32),
            pltpu.VMEM((GROUPS, 1, ROWS), jnp.float32),
            pltpu.VMEM((GROUPS, GROUPS, ROWS), jnp.float32),
            pltpu.SemaphoreType.DMA((8,)),
            pltpu.SemaphoreType.DMA((len(STREAMS),)),
            pltpu.SemaphoreType.DMA((BINS, len(STREAMS))),
            pltpu.SemaphoreType.DMA((BINS, len(STREAMS))),
            pltpu.SemaphoreType.DMA((len(UNITS), 3)),
            pltpu.SemaphoreType.DMA((len(UNITS), 3)),
            pltpu.SemaphoreType.DMA((7, 2)),
            pltpu.SemaphoreType.DMA((7, 2)),
            pltpu.SemaphoreType.DMA((7,)),
            pltpu.SemaphoreType.DMA((7,)),
            pltpu.SemaphoreType.DMA((owners,)),
            pltpu.SemaphoreType.DMA((owners,)),
        ],
        compiler_params=pltpu.CompilerParams(
            collective_id=0, has_side_effects=True, vmem_limit_bytes=60 * 2**20
        ),
    )(
        origin.reshape(-1),
        meta,
        three_index.reshape(blocks * OB, NV, aux_local),
        meta,
        pair_screen,
        occupied_energy.T,
        virtual_energy.T,
    )
    return home.reshape(CHUNK, 2, 64)[: NV // SIDE, :, :NV].transpose(1, 0, 2)


def local(three_index, block_owner, pair_screen, orbital_counts, occupied_energy, virtual_energy):
    *spots, fits = plan(block_owner, orbital_counts)
    arguments = (
        three_index,
        block_owner,
        pair_screen,
        orbital_counts,
        occupied_energy,
        virtual_energy,
    )
    return lax.cond(
        fits,
        lambda: binned(*spots, *arguments),
        lambda: general(*arguments),
    )


def solution(mesh):
    in_specs = (P(None, None, ("grp", "aux")), P(), P(), P(), P(), P())
    out_specs = P("aux", "grp", None)
    return jax.shard_map(local, mesh=mesh, in_specs=in_specs, out_specs=out_specs, check_vma=False)
```

```python
import jax
import jax.numpy as jnp
from jax import lax
from jax.experimental import pallas as pl
from jax.experimental.pallas import tpu as pltpu
from jax.sharding import PartitionSpec as P

CAP = 3


def slot_tiles(source, slot_block, slot_valid, owners):
    picked = jnp.take(source, slot_block.reshape(-1), axis=0)
    picked = picked.reshape(owners, CAP, source.shape[1], source.shape[2])
    return jnp.where(slot_valid[:, :, None, None] > 0, picked, jnp.zeros_like(picked))


def pair_block(received, first, second):
    return lax.dot_general(
        lax.dynamic_index_in_dim(received, first, 1, False),
        lax.dynamic_index_in_dim(received, second, 1, False),
        (((0, 2), (0, 2)), ((), ())),
        preferred_element_type=jnp.float32,
    )


def general(three_index, block_owner, pair_screen, orbital_counts, occupied_energy, virtual_energy):
    block_count, row_count, aux_local = three_index.shape
    occupied_width = occupied_energy.shape[1]
    virtual_width = virtual_energy.shape[1]
    groups = lax.axis_size("grp")
    owners = lax.axis_size("aux")
    own_index = lax.axis_index("aux")
    group_index = lax.axis_index("grp")
    quarter = row_count // groups
    owner_ids = jnp.arange(owners, dtype=jnp.int32)
    owned = (block_owner[None, :] == owner_ids[:, None]).astype(jnp.int32)
    slot_rank = jnp.cumsum(owned, axis=1) - 1
    slot_ids = jnp.arange(CAP, dtype=jnp.int32)
    selection = owned[:, None, :] * (slot_rank[:, None, :] == slot_ids[None, :, None]).astype(
        jnp.int32
    )
    block_ids = jnp.arange(block_count, dtype=jnp.int32)
    slot_block = jnp.sum(selection * block_ids[None, None, :], axis=2)
    slot_valid = jnp.sum(selection, axis=2)
    mine = lax.dynamic_index_in_dim(selection, own_index, 0, keepdims=False)
    my_block = jnp.sum(mine * block_ids[None, :], axis=1)
    my_valid = jnp.sum(mine, axis=1)
    energy = (virtual_energy[:, None, :] - occupied_energy[:, :, None]).reshape(
        block_count, row_count
    )
    occupied_flags = (
        jnp.arange(occupied_width, dtype=jnp.int32)[None, :] < orbital_counts[:, None]
    ).astype(jnp.float32)
    occupancy = jnp.repeat(occupied_flags, virtual_width, axis=1)
    slot_energy = jnp.take(energy, my_block, axis=0)
    slot_occupancy = jnp.take(occupancy, my_block, axis=0)
    screened = jnp.take(jnp.take(pair_screen, my_block, axis=0), my_block, axis=1)
    is_live = screened * my_valid[:, None] * my_valid[None, :] > 0

    def slot_amplitude(integral, first, second):
        energy_rows = lax.dynamic_slice_in_dim(slot_energy[first], group_index * quarter, quarter)
        occupied_rows = lax.dynamic_slice_in_dim(
            slot_occupancy[first], group_index * quarter, quarter
        )
        divisor = energy_rows[:, None] + slot_energy[second][None, :]
        return (
            occupied_rows[:, None] * slot_occupancy[second][None, :] * integral / divisor
        ).astype(jnp.bfloat16)

    def own_density(amplitude):
        row_form = amplitude.reshape(quarter // virtual_width, virtual_width, row_count)
        return jnp.einsum("iax,ibx->ab", row_form, row_form, preferred_element_type=jnp.float32)

    outgoing = slot_tiles(three_index, slot_block, slot_valid, owners)
    received = lax.all_to_all(outgoing, "aux", split_axis=0, concat_axis=0, tiled=True)
    empty = jnp.zeros((virtual_width, virtual_width), jnp.float32)

    def one_pair(parts, pair):
        first = pair // CAP
        second = pair % CAP
        integral = pair_block(received, first, second)
        sent = integral.reshape(groups, quarter, row_count)
        summed = jnp.sum(lax.all_to_all(sent, "grp", 0, 0, tiled=True), axis=0)
        part = own_density(slot_amplitude(summed, first, second))
        part = jnp.where(is_live[first, second], part, empty)
        return parts.at[first].add(part), None

    slot_parts, _ = lax.scan(
        one_pair,
        jnp.zeros((CAP, virtual_width, virtual_width), jnp.float32),
        jnp.arange(CAP * CAP, dtype=jnp.int32),
    )
    spread = slot_parts.reshape(CAP, groups, virtual_width // groups, virtual_width)
    placed = jnp.einsum(
        "cb,cgxy->gbxy", mine.astype(jnp.float32), spread, precision=lax.Precision.HIGHEST
    )
    placed = placed.reshape(groups, owners, block_count // owners, virtual_width // groups, virtual_width)
    placed = jnp.sum(lax.all_to_all(placed, "grp", 0, 0, tiled=True), axis=0)
    return jnp.sum(lax.all_to_all(placed, "aux", 0, 0, tiled=True), axis=0)


NV = 48
OB = 16
BINS = 16
GROUP = 8
ROWS = GROUP * NV
SIDE = 4
PART_A = 6
PART_B = 2
GROUPS = PART_A + PART_B
SLOTS = GROUPS * GROUP
CHUNK = 16
ALL = (0, BINS)
LIMITS = (ALL, ALL, ALL, (0, 15), (0, 9), (0, 4), ALL, (2, BINS))
STREAMS = tuple((GROUP * k, GROUP, ALL) for k in range(5)) + (
    (40, 4, ALL),
    (44, 4, (0, 8)),
    (48, 4, (0, 4)),
)
SENT = 52
AHEAD = 1
COLUMNS = tuple(
    [(0, v, v * (v + 1) // 2) for v in range(PART_A)]
    + [(PART_A, v, PART_A * (PART_A + 1) // 2 + v * (v + 1) // 2) for v in range(PART_B)]
)
TILES = PART_A * (PART_A + 1) // 2 + PART_B * (PART_B + 1) // 2
UNITS = []
for column, (base, v, first) in enumerate(COLUMNS):
    for skip in range(0, v + 1, 2):
        turn = len(UNITS) % 3
        UNITS.append(
            (column, first + skip, min(2, v + 1 - skip), (turn, (turn + 1) % 3, (turn + 2) % 3))
        )
BITS = [(d % 2, (d // 2) % 2, d // 4) for d in range(8)]
MESH = pl.DeviceIdType.MESH
VMEM = pl.BlockSpec(memory_space=pltpu.VMEM)
SMEM = pl.BlockSpec(memory_space=pltpu.SMEM)
ANY = pl.BlockSpec(memory_space=pl.ANY)


def has(limits, index):
    first, end = limits
    return (index >= first) & (index < end)


def plan(block_owner, orbital_counts):
    ids = jnp.arange(block_owner.shape[0], dtype=jnp.int32)
    same = block_owner[:, None] == block_owner[None, :]
    earlier = same & (ids[None, :] < ids[:, None])
    load = jnp.sum(jnp.where(same, orbital_counts[None, :], 0), axis=1)
    base = jnp.sum(jnp.where(earlier, orbital_counts[None, :], 0), axis=1)
    place = jnp.sum(earlier.astype(jnp.int32), axis=1)
    ahead = (load[None, :] > load[:, None]) | (
        (load[None, :] == load[:, None]) & (block_owner[None, :] < block_owner[:, None])
    )
    rank = jnp.sum((ahead & (place == 0)[None, :]).astype(jnp.int32), axis=1)
    second = rank >= BINS
    bin_of = jnp.where(second, 2 * BINS - 1 - rank, rank)
    ahead_load = jnp.sum(
        jnp.where(
            (place == 0)[None, :] & (rank[None, :] == 2 * BINS - 1 - rank[:, None]), load[None, :], 0
        ),
        axis=1,
    )
    room = jnp.zeros_like(load)
    for group, limits in enumerate(LIMITS):
        room = room + jnp.where(second == (group >= PART_A), has(limits, bin_of) * GROUP, 0)
    sent = sum(has(limits, bin_of) * number for first, number, limits in STREAMS)
    fits = jnp.all((load <= room) & (load + ahead_load <= sent))
    return bin_of, base, jnp.where(second, ahead_load, 0), load, place, second, fits


def position():
    z = lax.axis_index("grp")
    aux = lax.axis_index("aux")
    core = lax.rem(aux, 2)
    x = lax.rem(aux // 2, SIDE)
    y = aux // (2 * SIDE)
    return x, y, z, core


def device(x, y, z, core):
    return (z, (y * SIDE + x) * 2 + core)


def bin_index(x, y, z, core):
    kind = lax.rem(x, 2) + 2 * lax.rem(y, 2) + 4 * lax.rem(z, 2)
    return kind + core * (BINS - 1 - 2 * kind)


def part_index(x, y, z):
    return x // 2 + 2 * (y // 2) + 4 * (z // 2)


def shifted(value, by):
    return lax.rem(value + by + SIDE, SIDE)


def kernel(
    origin_ref,
    meta_ref,
    source,
    meta,
    screen,
    occupied_energy,
    virtual_energy,
    out,
    whole,
    packed,
    held,
    tiles,
    parts_1,
    parts_2,
    parts_3,
    exact,
    exact_parts,
    stack,
    row_sums,
    slot_sums,
    fold,
    chunks,
    chunk_parts,
    dense,
    homes,
    row_energy,
    column_energy,
    mask,
    load_sem,
    local_sem,
    send_sem,
    recv_sem,
    tile_send,
    tile_recv,
    exact_send,
    exact_recv,
    chunk_send,
    chunk_recv,
    home_send,
    home_recv,
):
    x, y, z, core = position()
    aux = lax.axis_index("aux")
    owners = lax.axis_size("aux")
    sign = 1 - 2 * core
    own_bin = bin_index(x, y, z, core)
    own_part = part_index(x, y, z)
    quarter = lax.rem(own_part, SIDE)
    half = own_part // SIDE

    pieces = load_sem.shape[0]
    size = source.shape[0] // pieces

    def load(piece):
        part = pl.ds(piece * size, size)
        return pltpu.make_async_copy(source.at[part], whole.at[part], load_sem.at[piece])

    for piece in range(pieces):
        load(piece).start()

    barrier = pltpu.get_barrier_semaphore()

    def greet(target):
        pl.semaphore_signal(barrier, inc=1, device_id=target, device_id_type=MESH)

    greet(device(x, y, z, 1 - core))
    for d in range(1, 8):
        dx, dy, dz = BITS[d]
        greet(device(shifted(x, -dx), shifted(y, -dy), shifted(z, -dz), 0))
        greet(device(shifted(x, dx), shifted(y, dy), shifted(z, dz), 1))
        greet(device(shifted(x, 2 * dx), shifted(y, 2 * dy), shifted(z, 2 * dz), core))

    def feeder(index):
        number = index // 2
        feed_core = number // 8
        kind = number + feed_core * (BINS - 1 - 2 * number)
        return (
            lax.rem(kind, 2) + 2 * lax.rem(z, 2),
            lax.rem(kind // 2, 2) + 2 * (z // 2),
            kind // 4 + 2 * lax.rem(index, 2),
            feed_core,
        )

    own_feed = own_bin * 2 + half

    @pl.loop(0, owners)
    def _(index):
        @pl.when((quarter != z) | (index != own_feed))
        def _():
            greet(device(*feeder(index)))

    fold[...] = (
        lax.rem(lax.broadcasted_iota(jnp.int32, (ROWS, NV), 0), NV)
        == lax.broadcasted_iota(jnp.int32, (ROWS, NV), 1)
    ).astype(jnp.bfloat16)
    slot_sums[...] = jnp.zeros_like(slot_sums)
    row_sums[...] = jnp.zeros_like(row_sums)
    chunks[...] = jnp.zeros_like(chunks)

    for piece in range(pieces):
        load(piece).wait()
    pl.semaphore_wait(barrier, 22 + owners - (quarter == z).astype(jnp.int32))

    def when(limits, index, act):
        if limits == ALL:
            act()
        else:
            pl.when(has(limits, index))(act)

    def slots(stream):
        first, number, limits = STREAMS[stream]
        return pl.ds(first, number)

    def gather(d, target_core, stream, act):
        dx, dy, dz = d % 2, (d // 2) % 2, d // 4
        tx, ty, tz = shifted(x, sign * dx), shifted(y, sign * dy), shifted(z, sign * dz)
        target_bin = bin_index(tx, ty, tz, target_core)
        copy = pltpu.make_async_remote_copy(
            src_ref=packed.at[target_bin, slots(stream)],
            dst_ref=held.at[2 * d + core, slots(stream)],
            send_sem=send_sem.at[2 * d + target_core, stream],
            recv_sem=recv_sem.at[2 * d + core, stream],
            device_id=device(tx, ty, tz, target_core),
            device_id_type=MESH,
        )
        when(STREAMS[stream][2], target_bin, lambda: act(copy))

    def keep(stream):
        return pltpu.make_async_copy(
            packed.at[own_bin, slots(stream)], held.at[core, slots(stream)], local_sem.at[stream]
        )

    def send_stream(stream):
        first_slot, number_of_slots, limits = STREAMS[stream]

        @pl.loop(0, BINS)
        def _(number):
            for slot in range(first_slot, first_slot + number_of_slots):
                origin = origin_ref[number * SENT + slot]
                packed[number, slot] = whole[origin]

        @pl.loop(0, 14)
        def _(index):
            gather(7 - index // 2, lax.rem(index, 2), stream, lambda copy: copy.start())

        gather(0, 1 - core, stream, lambda copy: copy.start())
        when(limits, own_bin, lambda: keep(stream).start())

    for stream in range(AHEAD):
        send_stream(stream)

    def arrived(stream):
        def wait_all():
            keep(stream).wait()

            @pl.loop(2, BINS)
            def _(sender):
                part = held.at[sender, slots(stream)]
                pltpu.make_async_copy(part, part, recv_sem.at[sender, stream]).wait()

            part = held.at[1 - core, slots(stream)]
            pltpu.make_async_copy(part, part, recv_sem.at[1 - core, stream]).wait()

        when(STREAMS[stream][2], own_bin, wait_all)

    row_number = lax.broadcasted_iota(jnp.int32, (ROWS, ROWS), 0)
    column_number = lax.broadcasted_iota(jnp.int32, (ROWS, ROWS), 1)
    own_diagonal = (
        lax.broadcasted_iota(jnp.int32, (NV, ROWS), 0) + own_part * NV
        == lax.broadcasted_iota(jnp.int32, (NV, ROWS), 1)
    )
    same_slot = (
        lax.broadcasted_iota(jnp.int32, (GROUP, ROWS), 1) // NV
        == lax.broadcasted_iota(jnp.int32, (GROUP, ROWS), 0)
    )

    def exact_dot(left, right, axis=0):
        return lax.dot_general(
            left,
            right,
            (((1,), (axis,)), ((), ())),
            precision=lax.Precision.HIGHEST,
            preferred_element_type=jnp.float32,
        )

    def fold_dot(left, axis=0):
        total = 0.0
        for _ in range(3):
            piece = left.astype(jnp.bfloat16)
            left = left - piece.astype(jnp.float32)
            total = total + lax.dot_general(
                piece, fold[...], (((1,), (axis,)), ((), ())), preferred_element_type=jnp.float32
            )
        return total

    blocks = meta.shape[1]
    slot_number = lax.broadcasted_iota(jnp.int32, (SLOTS, blocks), 0)
    orbital = slot_number - meta[1:2, :]
    inside = (meta[0:1, :] == own_bin) & (orbital >= 0) & (orbital < meta[2:3, :])
    pick = jnp.where(inside, 1.0, 0.0)
    slot_orbital = jnp.sum(jnp.where(inside, orbital, 0), axis=1, keepdims=True)
    occupied = exact_dot(pick, occupied_energy[...], 1)
    occupied = jnp.where(
        lax.broadcasted_iota(jnp.int32, (SLOTS, OB), 1) == slot_orbital, occupied, 0.0
    )
    energy = exact_dot(pick, virtual_energy[...], 1) - jnp.sum(occupied, axis=1, keepdims=True)
    row_slot = lax.broadcasted_iota(jnp.int32, (GROUPS, SLOTS), 0) * GROUP + own_part
    column_slot = lax.broadcasted_iota(jnp.int32, (GROUPS, SLOTS), 1)
    row_pick = exact_dot(jnp.where(row_slot == column_slot, 1.0, 0.0), pick)
    live = exact_dot(exact_dot(row_pick, jnp.where(screen[...] == 1, 1.0, 0.0)), pick, 1)
    order = jnp.where(row_slot < column_slot, 2.0, jnp.where(row_slot == column_slot, 1.0, 0.0))
    kind = jnp.where(live > 0.5, order, 0.0)
    for group in range(GROUPS):
        lanes = fold_dot(energy[group * GROUP : (group + 1) * GROUP], 1)
        lanes = jnp.sum(jnp.where(same_slot, lanes, 0.0), axis=0, keepdims=True)
        column_energy[group] = lanes
        row_energy[group] = jnp.sum(jnp.where(own_diagonal, lanes, 0.0), axis=1, keepdims=True)
        wide = lax.broadcasted_iota(jnp.int32, (SLOTS, ROWS), 0) == (
            group * GROUP + lax.broadcasted_iota(jnp.int32, (SLOTS, ROWS), 1) // NV
        )
        mask[group] = jnp.dot(
            kind.astype(jnp.bfloat16),
            jnp.where(wide, 1.0, 0.0).astype(jnp.bfloat16),
            preferred_element_type=jnp.float32,
        )

    def find(block, found):
        result = []
        for index in range(6):
            hit = (
                (meta_ref[0, block] == own_bin)
                & (meta_ref[3, block] == index % 3)
                & (meta_ref[4, block] == index // 3)
            )
            old = found[3 * index : 3 * index + 3]
            new = (meta_ref[1, block], meta_ref[2, block], block)
            result += [jnp.where(hit, n, o) for n, o in zip(new, old)]
        return tuple(result)

    nothing = jnp.int32(0)
    found = lax.fori_loop(0, blocks, find, (nothing, nothing, jnp.int32(-1)) * 6)
    block_start, block_slots, block_id = found[0::3], found[1::3], found[2::3]

    def settle():
        offset = block_slots[0] + block_slots[1] + block_slots[2]

        @pl.loop(0, BINS)
        def _(sender):
            for slot in range(PART_B * GROUP):
                held[sender, SENT + slot] = held[sender, offset + slot]

    def rows_of(base, group):
        first = group * GROUP + (SENT if base else 0)
        return jnp.concatenate(
            [
                held[sender, pl.ds(first, GROUP)].reshape(ROWS, held.shape[-1])
                for sender in range(BINS)
            ],
            axis=1,
        )

    def peer(e):
        dx, dy, dz = BITS[e]
        px, py, pz = shifted(x, 2 * dx), shifted(y, 2 * dy), shifted(z, 2 * dz)
        return part_index(px, py, pz), device(px, py, pz, core)

    bit = (x // 2, y // 2, z // 2)

    def view(fixed):
        return tuple(fixed.get(axis, slice(None)) for axis in (2, 1, 0))

    def step(unit, phase):
        column, first, number, order = UNITS[unit]
        fixed = {axis: bit[axis] for axis in order[:phase]}
        axis = order[phase]
        fixed[axis] = 1 - bit[axis]
        run = pl.ds(first, number)
        far = [shifted(c, 2 * (axis == k)) for k, c in enumerate((x, y, z))]
        landing = (parts_1.at[:, :, run], parts_2.at[:, run], parts_3.at[run])[phase]
        return pltpu.make_async_remote_copy(
            src_ref=tiles.at[view(fixed) + (run,)],
            dst_ref=landing,
            send_sem=tile_send.at[unit, phase],
            recv_sem=tile_recv.at[unit, phase],
            device_id=device(*far, core),
            device_id_type=MESH,
        )

    def units_of(column):
        return [unit for unit in range(len(UNITS)) if UNITS[unit][0] == column]

    def merge(column, phase):
        for unit in units_of(column):
            _, first, number, order = UNITS[unit]
            step(unit, phase).wait_recv()
            fixed = {axis: bit[axis] for axis in order[: phase + 1]}
            rest = [axis for axis in (2, 1, 0) if axis not in fixed]
            landed = (parts_1, parts_2)[phase]

            @pl.loop(first, first + number)
            def _(index):
                for choice in range(2 ** len(rest)):
                    at = tuple((choice // 2**k) % 2 for k in range(len(rest)))
                    place = view({**fixed, **dict(zip(rest, at))}) + (index,)
                    tiles[place] = (
                        tiles[place].astype(jnp.float32) + landed[at + (index,)].astype(jnp.float32)
                    ).astype(jnp.bfloat16)

            step(unit, phase + 1).start()

    def scatter_exact(e, batch):
        part, target = peer(e)
        return pltpu.make_async_remote_copy(
            src_ref=exact.at[batch, part],
            dst_ref=exact_parts.at[e - 1, batch],
            send_sem=exact_send.at[e - 1, batch],
            recv_sem=exact_recv.at[e - 1, batch],
            device_id=target,
            device_id_type=MESH,
        )

    def make_column(column):
        base, v, first = COLUMNS[column]

        @pl.loop(0, v + 1)
        def _(u):
            tile = lax.dot_general(
                rows_of(base, u),
                rows_of(base, v),
                (((1,), (1,)), ((), ())),
                preferred_element_type=jnp.float32,
            )

            @pl.when(u == v)
            def _():
                diagonal = jnp.where(row_number == column_number, tile, 0.0)
                diagonal = jnp.where(same_slot, jnp.sum(diagonal, axis=0, keepdims=True), 0.0)
                diagonal = fold_dot(diagonal)
                for part in range(8):
                    exact[column // 4, part, column % 4 : column % 4 + 1, :NV] = diagonal[
                        part : part + 1
                    ]

            rounded = tile.astype(jnp.bfloat16)
            for part in range(8):
                tiles[part // 4, (part // 2) % 2, part % 2, first + u] = rounded[
                    part * NV : (part + 1) * NV
                ]

        for unit in units_of(column):
            step(unit, 0).start()

    def add_column(column):
        base, v, first = COLUMNS[column]
        for unit in units_of(column):
            step(unit, 2).wait_recv()
        diagonal = exact[column // 4, own_part]
        for e in range(7):
            diagonal = diagonal + exact_parts[e, column // 4]
        diagonal = fold_dot(diagonal[:, :NV], 1)[column % 4 : column % 4 + 1]

        @pl.loop(0, v + 1)
        def _(u):
            integral = tiles[bit[2], bit[1], bit[0], first + u].astype(jnp.float32) + parts_3[
                first + u
            ].astype(jnp.float32)
            integral = jnp.where(own_diagonal & (u == v), diagonal, integral)
            kind = mask[base + v, pl.ds(base + u, 1), :]
            quotient = integral / (row_energy[base + u] + column_energy[base + v])
            amplitude = jnp.where(kind > 0, quotient, 0.0).astype(jnp.bfloat16)
            row_sums[base + u] = row_sums[base + u] + lax.dot_general(
                amplitude, amplitude, (((1,), (1,)), ((), ())), preferred_element_type=jnp.float32
            )
            stack[pl.ds(pl.multiple_of(u * NV, NV), NV), :] = jnp.where(
                kind > 1, quotient, 0.0
            ).astype(jnp.bfloat16)

        stacked = stack[: (v + 1) * NV, :]
        product = lax.dot_general(
            stacked, stacked, (((0,), (0,)), ((), ())), preferred_element_type=jnp.float32
        )
        slot_sums[(base + v) * ROWS : (base + v + 1) * ROWS, :] = fold_dot(
            jnp.where(row_number // NV == column_number // NV, product, 0.0)
        )

    def advance(column, phase):
        if column < 0:
            return
        act = (
            lambda: make_column(column),
            lambda: merge(column, 0),
            lambda: merge(column, 1),
            lambda: add_column(column),
        )[phase]
        when(LIMITS[column], own_bin, act)

    def receive(stream):
        arrived(stream)
        if stream + AHEAD < len(STREAMS):
            send_stream(stream + AHEAD)

    def start_exact(batch):
        for e in range(7, 0, -1):
            scatter_exact(e, batch).start()

    def wait_exact(batch):
        for e in range(1, 8):
            scatter_exact(e, batch).wait_recv()

    for column in range(PART_A):
        receive(column)
        if column == PART_A - 1:
            receive(PART_A)
        advance(column, 0)
        if column == 3:
            start_exact(0)
        advance(column - 1, 1)
        advance(column - 2, 2)
        if column == 3:
            wait_exact(0)
        advance(column - 3, 3)
    receive(len(STREAMS) - 1)
    settle()
    late = range(PART_A, GROUPS)
    for column in late:
        advance(column, 0)
    start_exact(1)
    for column in (PART_A - 1, *late):
        advance(column, 1)
    advance(PART_A - 2, 2)
    advance(PART_A - 3, 3)
    for column in (PART_A - 1, *late):
        advance(column, 2)
    wait_exact(1)
    for column in (PART_A - 2, PART_A - 1, *late):
        advance(column, 3)
    for group in range(GROUPS):
        part = pl.ds(pl.multiple_of(group * ROWS + own_part * NV, NV), NV)
        slot_sums[part, :] = slot_sums[part, :] + row_sums[group]

    for side in range(2):
        first_slot = side * PART_A * GROUP

        def add_slot(step, sums):
            slot = first_slot + step
            value = slot_sums[pl.ds(pl.multiple_of(slot * NV, NV), NV), :]
            result = []
            for i in range(3 * side, 3 * side + 3):
                own = (slot >= block_start[i]) & (slot < block_start[i] + block_slots[i])
                result.append(sums[i % 3] + jnp.where(own, value, jnp.zeros_like(value)))
            return tuple(result)

        zero = jnp.zeros((NV, NV), jnp.float32)
        sums = lax.fori_loop(0, (PART_A, PART_B)[side] * GROUP, add_slot, (zero, zero, zero))
        width = NV // SIDE
        for i in range(3):
            for g in range(SIDE):
                chunks[side * SIDE + g, i * CHUNK : i * CHUNK + width, :NV] = sums[i][
                    g * width : (g + 1) * width
                ]

    def scatter_chunk(e):
        part, target = peer(e)
        return pltpu.make_async_remote_copy(
            src_ref=chunks.at[part],
            dst_ref=chunk_parts.at[e - 1],
            send_sem=chunk_send.at[e - 1],
            recv_sem=chunk_recv.at[e - 1],
            device_id=target,
            device_id_type=MESH,
        )

    for e in range(7, 0, -1):
        scatter_chunk(e).start()
    for e in range(1, 8):
        scatter_chunk(e).wait_recv()
    total = chunks[own_part]
    for e in range(7):
        total = total + chunk_parts[e]
    pieces = [total[i * CHUNK : (i + 1) * CHUNK] for i in range(3)]
    turned = [pltpu.roll(piece, 64, 1) for piece in pieces]

    def send_home(target):
        return pltpu.make_async_remote_copy(
            src_ref=dense.at[target],
            dst_ref=homes.at[own_feed],
            send_sem=home_send.at[target],
            recv_sem=home_recv.at[own_feed],
            device_id=(quarter, target),
            device_id_type=MESH,
        )

    def away(target):
        return (quarter != z) | (target != aux)

    @pl.loop(0, owners)
    def _(target):
        message = jnp.zeros((CHUNK, 128), jnp.float32)
        for i in range(3):
            block = jnp.where(half == 0, block_id[i], block_id[3 + i])
            message = message + jnp.where(block == 2 * target, pieces[i], 0.0)
            message = message + jnp.where(block == 2 * target + 1, turned[i], 0.0)
        dense[target] = message

        @pl.when(away(target))
        def _():
            send_home(target).start()

    @pl.when(quarter == z)
    def _():
        homes[own_feed] = dense[aux]

    @pl.loop(0, owners)
    def _(index):
        @pl.when((quarter != z) | (index != own_feed))
        def _():
            pltpu.make_async_copy(homes.at[index], homes.at[index], home_recv.at[index]).wait()

    out[...] = jnp.sum(homes[...], axis=0)

    @pl.loop(0, owners)
    def _(target):
        @pl.when(away(target))
        def _():
            send_home(target).wait_send()

    for e in range(1, 8):
        scatter_chunk(e).wait_send()

    def sent_column(column):
        for unit in units_of(column):
            for phase in range(3):
                step(unit, phase).wait_send()

    for column in range(GROUPS):
        when(LIMITS[column], own_bin, lambda: sent_column(column))
    for batch in range(2):
        for e in range(1, 8):
            scatter_exact(e, batch).wait_send()
    for stream in range(len(STREAMS)):
        gather(0, 1 - core, stream, lambda copy: copy.wait_send())

        @pl.loop(2, BINS)
        def _(index):
            gather(index // 2, lax.rem(index, 2), stream, lambda copy: copy.wait_send())


def binned(
    bin_of,
    base,
    offset,
    load,
    place,
    second,
    three_index,
    block_owner,
    pair_screen,
    orbital_counts,
    occupied_energy,
    virtual_energy,
):
    blocks, row_count, aux_local = three_index.shape
    block_ids = jnp.arange(blocks, dtype=jnp.int32)
    sent_ids = jnp.arange(SENT, dtype=jnp.int32)[:, None] - (base + offset)[None, :]
    bins = jnp.arange(BINS, dtype=jnp.int32)
    origin = jnp.sum(
        jnp.where(
            (bin_of[None, None, :] == bins[:, None, None])
            & ((sent_ids >= 0) & (sent_ids < orbital_counts[None, :]))[None],
            (block_ids[None, :] * OB + sent_ids)[None],
            0,
        ),
        axis=2,
    )
    start = base + jnp.where(second, PART_A * GROUP, 0)
    meta = jnp.stack([bin_of, start, orbital_counts, place, second.astype(jnp.int32)] + [base] * 3)
    owners = lax.axis_size("aux")
    home = pl.pallas_call(
        kernel,
        out_shape=jax.ShapeDtypeStruct((CHUNK, 128), jnp.float32),
        in_specs=[SMEM, SMEM, ANY, VMEM, VMEM, VMEM, VMEM],
        out_specs=VMEM,
        scratch_shapes=[
            pltpu.VMEM((blocks * OB, NV, aux_local), jnp.bfloat16),
            pltpu.VMEM((BINS, SENT, NV, aux_local), jnp.bfloat16),
            pltpu.VMEM((BINS, SENT + PART_B * GROUP, NV, aux_local), jnp.bfloat16),
            pltpu.VMEM((2, 2, 2, TILES, NV, ROWS), jnp.bfloat16),
            pltpu.VMEM((2, 2, TILES, NV, ROWS), jnp.bfloat16),
            pltpu.VMEM((2, TILES, NV, ROWS), jnp.bfloat16),
            pltpu.VMEM((TILES, NV, ROWS), jnp.bfloat16),
            pltpu.VMEM((2, 8, 8, 128), jnp.float32),
            pltpu.VMEM((7, 2, 8, 128), jnp.float32),
            pltpu.VMEM((PART_A * NV, ROWS), jnp.bfloat16),
            pltpu.VMEM((GROUPS, NV, NV), jnp.float32),
            pltpu.VMEM((SLOTS * NV, NV), jnp.float32),
            pltpu.VMEM((ROWS, NV), jnp.bfloat16),
            pltpu.VMEM((8, 3 * CHUNK, 128), jnp.float32),
            pltpu.VMEM((7, 3 * CHUNK, 128), jnp.float32),
            pltpu.VMEM((owners, CHUNK, 128), jnp.float32),
            pltpu.VMEM((owners, CHUNK, 128), jnp.float32),
            pltpu.VMEM((GROUPS, NV, 1), jnp.float32),
            pltpu.VMEM((GROUPS, 1, ROWS), jnp.float32),
            pltpu.VMEM((GROUPS, GROUPS, ROWS), jnp.float32),
            pltpu.SemaphoreType.DMA((8,)),
            pltpu.SemaphoreType.DMA((len(STREAMS),)),
            pltpu.SemaphoreType.DMA((BINS, len(STREAMS))),
            pltpu.SemaphoreType.DMA((BINS, len(STREAMS))),
            pltpu.SemaphoreType.DMA((len(UNITS), 3)),
            pltpu.SemaphoreType.DMA((len(UNITS), 3)),
            pltpu.SemaphoreType.DMA((7, 2)),
            pltpu.SemaphoreType.DMA((7, 2)),
            pltpu.SemaphoreType.DMA((7,)),
            pltpu.SemaphoreType.DMA((7,)),
            pltpu.SemaphoreType.DMA((owners,)),
            pltpu.SemaphoreType.DMA((owners,)),
        ],
        compiler_params=pltpu.CompilerParams(
            collective_id=0, has_side_effects=True, vmem_limit_bytes=60 * 2**20
        ),
    )(
        origin.reshape(-1),
        meta,
        three_index.reshape(blocks * OB, NV, aux_local),
        meta,
        pair_screen,
        occupied_energy.T,
        virtual_energy.T,
    )
    return home.reshape(CHUNK, 2, 64)[: NV // SIDE, :, :NV].transpose(1, 0, 2)


def local(three_index, block_owner, pair_screen, orbital_counts, occupied_energy, virtual_energy):
    *spots, fits = plan(block_owner, orbital_counts)
    arguments = (
        three_index,
        block_owner,
        pair_screen,
        orbital_counts,
        occupied_energy,
        virtual_energy,
    )
    return lax.cond(
        fits,
        lambda: binned(*spots, *arguments),
        lambda: general(*arguments),
    )


def solution(mesh):
    in_specs = (P(None, None, ("grp", "aux")), P(), P(), P(), P(), P())
    out_specs = P("aux", "grp", None)
    return jax.shard_map(local, mesh=mesh, in_specs=in_specs, out_specs=out_specs, check_vma=False)
```
